128 devices in a mesh: lat: 8 (over y, z_hi), lon: 16 (over x, z_lo, core).
Axes of the slice: x: 4, y: 4, z: 4 (z_hi: 2, z_lo: 2; z = z_hi * 2 + z_lo), core: 2. Of those that a mesh axis runs over, the one named last changes fastest.
Arguments:
- tokens: bfloat16 [2, 96, 384, 512], P(None, 'lat', 'lon'), may hold values from -36 to 36
- cotangent: bfloat16 [2, 48, 192, 1024], P(None, 'lat', 'lon'), may hold values from -6 to 6
- gain_fine: float32 [512], replicated, may hold values from 0.25 to 1.75
- qkv_fine: bfloat16 [512, 1536], replicated, may hold values from -1.06066017 to 1.06066017
- proj_fine: bfloat16 [512, 512], replicated, may hold values from -0.25 to 0.25
- gain_merge: float32 [2048], replicated, may hold values from 0.25 to 1.75
- merge_weight: bfloat16 [2048, 1024], replicated, may hold values from -0.125 to 0.125
- gain_coarse: float32 [1024], replicated, may hold values from 0.25 to 1.75
- qkv_coarse: bfloat16 [1024, 3072], replicated, may hold values from -0.75 to 0.75
- proj_coarse: bfloat16 [1024, 1024], replicated, may hold values from -0.1875 to 0.1875
Outputs:
- coarse_tokens: bfloat16 [2, 48, 192, 1024], P(None, 'lat', 'lon')
- tokens_grad: bfloat16 [2, 96, 384, 512], P(None, 'lat', 'lon')
- gain_fine_grad: float32 [512], P(('lat', 'lon'))
- qkv_fine_grad: float32 [512, 1536], P(('lat', 'lon'))
- proj_fine_grad: float32 [512, 512], P(('lat', 'lon'))
- gain_merge_grad: float32 [2048], P(('lat', 'lon'))
- merge_grad: float32 [2048, 1024], P(('lat', 'lon'))
- gain_coarse_grad: float32 [1024], P(('lat', 'lon'))
- qkv_coarse_grad: float32 [1024, 3072], P(('lat', 'lon'))
- proj_coarse_grad: float32 [1024, 1024], P(('lat', 'lon'))
The draws below stay inside these ranges and needn't reach their ends.
All inputs are finite; a program needn't handle non-finite values.
Results may differ from the reference program's by a relative error of at most 0.039.
Values may be sent and summed in bfloat16 or wider, within the bound.
A program may use at most 192 MiB of HBM per device.

```python
import math
import jax
import jax.numpy as jnp
from jax import lax

D1 = 512
D2 = 1024
HD = 64
LV = 2
WH = 6
WW = 12
NH = 96
NW = 384


def drawn_qkv(key, width_size, strongest):
    first_key, second_key, third_key, head_key = jax.random.split(key, 4)
    shape_pair = (width_size, width_size)
    base_part = jnp.clip(jax.random.normal(first_key, shape_pair, jnp.float32), -4.0, 4.0)
    other_part = jnp.clip(jax.random.normal(second_key, shape_pair, jnp.float32), -4.0, 4.0)
    third_part = jnp.clip(jax.random.normal(third_key, shape_pair, jnp.float32), -4.0, 4.0)
    strength = jnp.exp(jax.random.uniform(head_key, (width_size // HD,), jnp.float32, 0.0, math.log(strongest)))
    columns = jnp.repeat(strength, HD) / math.sqrt(width_size)
    queries = base_part * columns
    keys_part = other_part * columns
    values_part = third_part / math.sqrt(width_size)
    return jnp.concatenate([queries, keys_part, values_part], axis=1).astype(jnp.bfloat16)


def draw_tokens(key, part):
    key = jax.random.fold_in(key, 11)
    row_key, col_key, noise_key = jax.random.split(key, 3)
    row_scale = jnp.exp(jax.random.uniform(row_key, (LV, NH, NW, 1), jnp.float32, math.log(0.3), math.log(3.0)))
    col_scale = jnp.exp(jax.random.uniform(col_key, (D1,), jnp.float32, math.log(0.3), math.log(3.0)))
    noise_values = jnp.clip(jax.random.normal(noise_key, (LV, NH, NW, D1), jnp.float32), -4.0, 4.0)
    return (row_scale * col_scale * noise_values).astype(jnp.bfloat16)


def draw_qkv_fine(key, part):
    key = jax.random.fold_in(key, 21)
    return drawn_qkv(key, D1, 1.0)


def draw_qkv_coarse(key, part):
    key = jax.random.fold_in(key, 31)
    return drawn_qkv(key, D2, 1.0)


def level_of(key, extent, cuts, smallest, largest):
    factor_of, own = 1.0, jax.random.fold_in(key, 6)
    for dim, shards_of in cuts:
        steps = jnp.exp(jax.random.uniform(jax.random.fold_in(own, dim), (shards_of,), jnp.float32, smallest / len(cuts), largest / len(cuts)))
        factor_of = factor_of * jnp.repeat(steps, extent[dim] // shards_of).reshape([-1 if axis == dim else 1 for axis in range(len(extent))])
    return factor_of


def centred(key, dims, deviation, bound, cuts=(), dtype=jnp.bfloat16):
    gain = level_of(key, dims, cuts, -0.22, 0.18) if cuts else 1.0
    entries = jax.random.normal(key, dims, jnp.float32) * deviation * gain
    return jnp.minimum(jnp.maximum(entries, -bound), bound).astype(dtype)


def setup_inputs(seed: int = 0) -> dict:
    splits = jax.random.split(jax.random.key(seed), 11)
    return {
        "tokens": draw_tokens(jax.random.fold_in(splits[10], 71), 0),
        "cotangent": centred(splits[1], (LV, NH // 2, NW // 2, D2), 1.0, 6.0, ((1, 8), (2, 16))),
        "gain_fine": jnp.clip(1.0 + 0.15 * jax.random.normal(splits[2], (D1,), jnp.float32), 0.25, 1.75),
        "qkv_fine": draw_qkv_fine(jax.random.fold_in(splits[10], 71), 0),
        "proj_fine": centred(splits[4], (D1, D1), D1 ** -0.5, 0.25),
        "gain_merge": jnp.clip(1.0 + 0.15 * jax.random.normal(splits[5], (4 * D1,), jnp.float32), 0.25, 1.75),
        "merge_weight": centred(splits[6], (4 * D1, D2), (4 * D1) ** -0.5, 0.125),
        "gain_coarse": jnp.clip(1.0 + 0.15 * jax.random.normal(splits[7], (D2,), jnp.float32), 0.25, 1.75),
        "qkv_coarse": draw_qkv_coarse(jax.random.fold_in(splits[10], 71), 0),
        "proj_coarse": centred(splits[9], (D2, D2), D2 ** -0.5, 0.1875),
    }


EPSILON = 1e-05
MASKED = -1e+30

def normalize(values, gain_vector):
    centre = lax.optimization_barrier(jnp.mean(values, axis=-1, keepdims=True))
    offset = values - centre
    spread = lax.optimization_barrier(jnp.mean(offset * offset, axis=-1, keepdims=True))
    return (offset * lax.rsqrt(spread + EPSILON) * gain_vector).astype(jnp.bfloat16)

def to_windows(block_grid, win_height, win_width):
    levels, row_count, col_count, features = block_grid.shape
    pieces = block_grid.reshape(levels, row_count // win_height, win_height, col_count // win_width, win_width, features)
    pieces = pieces.transpose(1, 3, 0, 2, 4, 5)
    return pieces.reshape(row_count // win_height * (col_count // win_width), levels * win_height * win_width, features)

def from_windows(pieces, levels, row_count, col_count, win_height, win_width):
    features = pieces.shape[-1]
    grid_view = pieces.reshape(row_count // win_height, col_count // win_width, levels, win_height, win_width, features)
    grid_view = grid_view.transpose(2, 0, 3, 1, 4, 5)
    return grid_view.reshape(levels, row_count, col_count, features)

def visible(edge_flags, cell_count):
    places = jnp.arange(cell_count) // WW % WH
    upper_rows = places < WH - WH // 2
    same_group = upper_rows[:, None] == upper_rows[None, :]
    return jnp.logical_or(same_group[None, None], jnp.logical_not(edge_flags)[:, None, None, None])

def split_heads(windows, head_count):
    win_count, cell_count, triple_width = windows.shape
    features = triple_width // 3
    split_parts = windows.reshape(win_count, cell_count, 3, head_count, features // head_count)
    return (split_parts[:, :, 0], split_parts[:, :, 1], split_parts[:, :, 2])

def softmax_weights(queries, keys_part, edge_flags):
    score_scale = queries.shape[-1] ** (-0.5)
    scores = jnp.einsum('wqhd,wkhd->whqk', queries.astype(jnp.float32), keys_part.astype(jnp.float32)) * score_scale
    scores = jnp.where(visible(edge_flags, queries.shape[1]), scores, MASKED)
    highest = lax.optimization_barrier(jnp.max(scores, axis=-1, keepdims=True))
    powers = jnp.exp(scores - highest)
    return powers / lax.optimization_barrier(jnp.sum(powers, axis=-1, keepdims=True))

def attend(windows, edge_flags, head_count):
    queries, keys_part, values_part = split_heads(windows, head_count)
    weights = softmax_weights(queries, keys_part, edge_flags).astype(jnp.bfloat16)
    mixed_values = jnp.einsum('whqk,wkhd->wqhd', weights.astype(jnp.float32), values_part.astype(jnp.float32))
    return mixed_values.astype(jnp.bfloat16).reshape(windows.shape[0], windows.shape[1], -1)

def attend_back(windows, edge_flags, head_count, upstream):
    queries, keys_part, values_part = split_heads(windows, head_count)
    weights = softmax_weights(queries, keys_part, edge_flags)
    rounded = weights.astype(jnp.bfloat16)
    win_count, cell_count, features = upstream.shape
    incoming = upstream.reshape(win_count, cell_count, head_count, features // head_count)
    prob_grad = jnp.einsum('wqhd,wkhd->whqk', incoming.astype(jnp.float32), values_part.astype(jnp.float32))
    score_grad = weights * (prob_grad - lax.optimization_barrier(jnp.sum(weights * prob_grad, axis=-1, keepdims=True)))
    score_grad = (score_grad * queries.shape[-1] ** (-0.5)).astype(jnp.bfloat16).astype(jnp.float32)
    query_grad = jnp.einsum('whqk,wkhd->wqhd', score_grad, keys_part.astype(jnp.float32)).astype(jnp.bfloat16)
    key_grad = jnp.einsum('whqk,wqhd->wkhd', score_grad, queries.astype(jnp.float32)).astype(jnp.bfloat16)
    value_grad = jnp.einsum('whqk,wqhd->wkhd', rounded.astype(jnp.float32), incoming.astype(jnp.float32)).astype(jnp.bfloat16)
    return jnp.stack([query_grad, key_grad, value_grad], axis=2).reshape(win_count, cell_count, 3 * features)

def attention_grid(qkv_grid, head_count):
    levels, row_count, col_count, triple_width = qkv_grid.shape
    band_count = row_count // WH
    bands = qkv_grid.reshape(levels, band_count, WH, col_count, triple_width).transpose(1, 0, 2, 3, 4)

    def one_band(band_item):
        band_cells, position = band_item
        windows = to_windows(band_cells, WH, WW)
        edge_flags = jnp.full((windows.shape[0],), position == band_count - 1)
        return from_windows(attend(windows, edge_flags, head_count), levels, WH, col_count, WH, WW)
    result = lax.map(one_band, (bands, jnp.arange(band_count)))
    return result.transpose(1, 0, 2, 3, 4).reshape(levels, row_count, col_count, triple_width // 3)

def attention_grid_back(qkv_grid, grad_grid, head_count):
    levels, row_count, col_count, triple_width = qkv_grid.shape
    band_count = row_count // WH
    bands = qkv_grid.reshape(levels, band_count, WH, col_count, triple_width).transpose(1, 0, 2, 3, 4)
    grad_bands = grad_grid.reshape(levels, band_count, WH, col_count, triple_width // 3).transpose(1, 0, 2, 3, 4)

    def one_band(band_item):
        band_cells, band_grads, position = band_item
        windows = to_windows(band_cells, WH, WW)
        upstream = to_windows(band_grads, WH, WW)
        edge_flags = jnp.full((windows.shape[0],), position == band_count - 1)
        return from_windows(attend_back(windows, edge_flags, head_count, upstream), levels, WH, col_count, WH, WW)
    result = lax.map(one_band, (bands, grad_bands, jnp.arange(band_count)))
    return result.transpose(1, 0, 2, 3, 4).reshape(levels, row_count, col_count, triple_width)

def roll_ahead(grid_values):
    return jnp.roll(grid_values, (-(WH // 2), -(WW // 2)), axis=(1, 2))

def roll_behind(grid_values):
    return jnp.roll(grid_values, (WH // 2, WW // 2), axis=(1, 2))

def as_rows(grid_values):
    return grid_values.reshape(-1, grid_values.shape[-1])

def weight_gradient(left_grid, right_grid):
    return jnp.dot(as_rows(left_grid).T, as_rows(right_grid), preferred_element_type=jnp.float32)

def merge_patches(grid_values):
    levels, row_count, col_count, features = grid_values.shape
    pieces = grid_values.reshape(levels, row_count // 2, 2, col_count // 2, 2, features)
    return pieces.transpose(0, 1, 3, 4, 2, 5).reshape(levels, row_count // 2, col_count // 2, 4 * features)

def split_patches(grid_values):
    levels, row_count, col_count, features = grid_values.shape
    pieces = grid_values.reshape(levels, row_count, col_count, 2, 2, features // 4)
    return pieces.transpose(0, 1, 4, 2, 3, 5).reshape(levels, 2 * row_count, 2 * col_count, features // 4)

def level_forward(tokens_f, gain_vector, qkv_weight, proj_weight):
    head_count = qkv_weight.shape[0] // HD
    normed = normalize(tokens_f, gain_vector)
    rolled = roll_ahead(normed)
    qkv_grid = jnp.dot(rolled, qkv_weight, preferred_element_type=jnp.float32).astype(jnp.bfloat16)
    attended = roll_behind(attention_grid(qkv_grid, head_count))
    output = (tokens_f + jnp.dot(attended, proj_weight, preferred_element_type=jnp.float32)).astype(jnp.bfloat16)
    return (output, (rolled, qkv_grid, attended))

def level_backward(tokens_f, gain_vector, qkv_weight, proj_weight, saved, result_grad):
    rolled, qkv_grid, attended = saved
    head_count = qkv_weight.shape[0] // HD
    proj_grad = weight_gradient(attended, result_grad)
    attended_grad = jnp.dot(result_grad, proj_weight.T, preferred_element_type=jnp.float32).astype(jnp.bfloat16)
    qkv_grad = attention_grid_back(qkv_grid, roll_ahead(attended_grad), head_count)
    qkv_weight_grad = weight_gradient(rolled, qkv_grad)
    rolled_grad = jnp.dot(qkv_grad, qkv_weight.T, preferred_element_type=jnp.float32).astype(jnp.bfloat16)
    normed_grad = roll_behind(rolled_grad)
    normed_value, pullback = jax.vjp(normalize, tokens_f, gain_vector)
    tokens_ln_grad, gain_grad = pullback(normed_grad)
    return (result_grad.astype(jnp.float32) + tokens_ln_grad, gain_grad, qkv_weight_grad, proj_grad)

def reference(tokens, cotangent, gain_fine, qkv_fine, proj_fine, gain_merge, merge_weight, gain_coarse, qkv_coarse, proj_coarse):
    tokens_f = tokens.astype(jnp.float32)
    fine_out, fine_saved = level_forward(tokens_f, gain_fine, qkv_fine, proj_fine)
    patches = merge_patches(fine_out).astype(jnp.float32)
    merged_norm = normalize(patches, gain_merge)
    coarse_in = jnp.dot(merged_norm, merge_weight, preferred_element_type=jnp.float32).astype(jnp.bfloat16)
    coarse_f = coarse_in.astype(jnp.float32)
    coarse_tokens, coarse_saved = level_forward(coarse_f, gain_coarse, qkv_coarse, proj_coarse)
    coarse_grad_f, gain_coarse_grad, qkv_coarse_grad, proj_coarse_grad = level_backward(coarse_f, gain_coarse, qkv_coarse, proj_coarse, coarse_saved, cotangent)
    coarse_grad = coarse_grad_f.astype(jnp.bfloat16)
    merge_grad = weight_gradient(merged_norm, coarse_grad)
    merged_norm_grad = jnp.dot(coarse_grad, merge_weight.T, preferred_element_type=jnp.float32).astype(jnp.bfloat16)
    normed_value, pullback = jax.vjp(normalize, patches, gain_merge)
    patches_grad, gain_merge_grad = pullback(merged_norm_grad)
    fine_grad = split_patches(patches_grad).astype(jnp.bfloat16)
    tokens_grad_f, gain_fine_grad, qkv_fine_grad, proj_fine_grad = level_backward(tokens_f, gain_fine, qkv_fine, proj_fine, fine_saved, fine_grad)
    return (coarse_tokens, tokens_grad_f.astype(jnp.bfloat16), gain_fine_grad, qkv_fine_grad, proj_fine_grad, gain_merge_grad, merge_grad, gain_coarse_grad, qkv_coarse_grad, proj_coarse_grad)
```

```python
import functools

import jax
import jax.numpy as jnp
import numpy as np
from jax import lax
from jax.experimental import pallas as pl
from jax.experimental.pallas import tpu as pltpu
from jax.sharding import PartitionSpec as P

MESH = pl.DeviceIdType.MESH
HALF = jnp.bfloat16
FULL = jnp.float32
HD = 64
WH = 6
WW = 12
CELLS = 144
EPSILON = 1e-05
MASKED = -1e30
LIMIT = 58 * 1024 * 1024
VMEM = pl.BlockSpec(memory_space=pltpu.VMEM)
SMEM = pl.BlockSpec(memory_space=pltpu.SMEM)
ANYWHERE = pl.BlockSpec(memory_space=pl.ANY)


def dot(left, right):
    return jnp.dot(left, right, preferred_element_type=FULL)


def dot_nt(left, right):
    return lax.dot_general(left, right, (((1,), (1,)), ((), ())), preferred_element_type=FULL)


def dot_tn(left, right):
    return lax.dot_general(left, right, (((0,), (0,)), ((), ())), preferred_element_type=FULL)


def natural_order(rows, cols):
    return lambda level, i, j: (level * rows + i) * cols + j


def window_order(rows, cols):
    def place(level, i, j):
        window = i // WH * (cols // WW) + j // WW
        return window * CELLS + ((i % WH // 3 * 2 + level) * 3 + i % 3) * WW + j % WW

    return place


def patch_order(rows, cols):
    coarse = window_order(rows // 2, cols // 2)

    def place(level, i, j):
        return (j % 2 * 2 + i % 2) * CELLS + coarse(level, i // 2, j // 2)

    return place


@functools.lru_cache(maxsize=None)
def roll_matrices(rows, cols, source, target, sign):
    orders = {"natural": natural_order, "window": window_order, "patch": patch_order}
    from_place, to_place = orders[source](rows, cols), orders[target](rows, cols)
    count = 2 * rows * cols
    pieces = ([], [], [])
    own = np.zeros((count, count), np.float32)
    for level in range(2):
        for i in range(rows):
            for j in range(cols):
                far_i, far_j = i + 3 * sign, j + 6 * sign
                across = (far_i // rows != 0, far_j // cols != 0)
                here = from_place(level, far_i % rows, far_j % cols)
                there = to_place(level, i, j)
                if across == (False, False):
                    own[there, here] = 1
                else:
                    slot = {(False, True): 0, (True, False): 1, (True, True): 2}[across]
                    pieces[slot].append((there, here))
    sizes = tuple((len(piece) + 15) // 16 * 16 for piece in pieces)
    pack = np.zeros((sum(sizes), count), np.float32)
    halo = np.zeros((count, sum(sizes)), np.float32)
    start = 0
    for piece, size in zip(pieces, sizes):
        for k, (there, here) in enumerate(piece):
            pack[start + k, here] = 1
            halo[there, start + k] = 1
        start += size
    return pack, own, halo, sizes


def roll_kernel(count, sizes, sign, *refs):
    given = [refs[4 * n : 4 * n + 4] for n in range(count)]
    result = refs[4 * count : 5 * count]
    packed = refs[5 * count : 6 * count]
    landed = refs[6 * count : 7 * count]
    send_sem, recv_sem = refs[7 * count :]
    lat, lon = lax.axis_index("lat"), lax.axis_index("lon")
    lats, lons = lax.axis_size("lat"), lax.axis_size("lon")
    steps = ((0, 1), (1, 0), (1, 1))

    def neighbour(step, way):
        return (
            lax.rem(lat + lats + way * step[0], lats),
            lax.rem(lon + lons + way * step[1], lons),
        )

    barrier = pltpu.get_barrier_semaphore()
    for step in steps:
        pl.semaphore_signal(
            barrier, inc=1, device_id=neighbour(step, sign), device_id_type=MESH
        )
    for n in range(count):
        value, pack, own, halo = given[n]
        packed[n][...] = dot(pack[...], value[...]).astype(HALF)
    pl.semaphore_wait(barrier, 3)
    copies = []
    for n in range(count):
        start = 0
        for slot, step in enumerate(steps):
            rows = pl.ds(start, sizes[n][slot])
            copy = pltpu.make_async_remote_copy(
                src_ref=packed[n].at[rows],
                dst_ref=landed[n].at[rows],
                send_sem=send_sem.at[n, slot],
                recv_sem=recv_sem.at[n, slot],
                device_id=neighbour(step, -sign),
                device_id_type=MESH,
            )
            copy.start()
            copies.append(copy)
            start += sizes[n][slot]
    for n in range(count):
        value, pack, own, halo = given[n]
        result[n][...] = dot(own[...], value[...]).astype(HALF)
    for n in range(count):
        value, pack, own, halo = given[n]
        for copy in copies[3 * n : 3 * n + 3]:
            copy.wait()
        result[n][...] = result[n][...] + dot(halo[...], landed[n][...]).astype(HALF)


def roll_grids(items, sign, identity):
    count = len(items)
    operands, shapes, packed, landed, sizes = [], [], [], [], []
    for value, rows, cols, source, target in items:
        pack, own, halo, size = roll_matrices(rows, cols, source, target, sign)
        operands += [value] + [jnp.asarray(matrix, HALF) for matrix in (pack, own, halo)]
        shapes.append(jax.ShapeDtypeStruct(value.shape, HALF))
        packed.append(pltpu.VMEM((sum(size), value.shape[1]), HALF))
        landed.append(pltpu.VMEM((sum(size), value.shape[1]), HALF))
        sizes.append(size)
    return pl.pallas_call(
        functools.partial(roll_kernel, count, tuple(sizes), sign),
        out_shape=shapes,
        in_specs=[VMEM] * len(operands),
        out_specs=[VMEM] * count,
        scratch_shapes=packed
        + landed
        + [pltpu.SemaphoreType.DMA((count, 3)), pltpu.SemaphoreType.DMA((count, 3))],
        compiler_params=pltpu.CompilerParams(
            collective_id=identity, has_side_effects=True, vmem_limit_bytes=LIMIT
        ),
    )(*operands)


def norm_parts(values):
    centre = jnp.mean(values, axis=-1, keepdims=True)
    offset = values - centre
    spread = jnp.mean(offset * offset, axis=-1, keepdims=True)
    scale = lax.rsqrt(spread + EPSILON)
    return offset * scale, scale


def norm_back(grad, normal, scale, gain):
    inner = grad * gain
    mean = jnp.mean(inner, axis=-1, keepdims=True)
    along = jnp.mean(inner * normal, axis=-1, keepdims=True)
    return (inner - mean - normal * along) * scale


def two_heads(pair):
    first = lax.broadcasted_iota(jnp.int32, pair.shape, 1) < HD
    zero = jnp.zeros_like(pair)
    return jnp.concatenate([jnp.where(first, pair, zero), jnp.where(first, zero, pair)], axis=0)


def one_pair(stack):
    half = stack.shape[0] // 2
    first = lax.broadcasted_iota(jnp.int32, (half, 2 * HD), 1) < HD
    return jnp.where(first, stack[:half], stack[half:])


def pair_mask(edge):
    shape = (CELLS, 2 * CELLS)
    key = lax.broadcasted_iota(jnp.int32, shape, 0)
    query = lax.broadcasted_iota(jnp.int32, shape, 1)
    query = jnp.where(query >= CELLS, query - CELLS, query)
    apart = (key < CELLS // 2) != (query < CELLS // 2)
    return jnp.where(apart, edge, 0) > 0


def pair_weights(queries, keys, mask):
    scores = dot_nt(keys, queries * 0.125)
    scores = jnp.where(mask, MASKED, scores)
    powers = jnp.exp(scores - jnp.max(scores, axis=0, keepdims=True))
    return powers * (1.0 / jnp.sum(powers, axis=0, keepdims=True))


def pair_forward(weights, values):
    return one_pair(dot_tn(weights.astype(HALF), values)).astype(HALF)


def pair_back(weights, queries, keys, values, upstream):
    weight_grad = dot_nt(values, upstream)
    inner = jnp.sum(weights * weight_grad, axis=0, keepdims=True)
    score_grad = (weights * (weight_grad - inner) * 0.125).astype(HALF)
    query_grad = one_pair(dot_tn(score_grad, keys)).astype(HALF)
    key_grad = dot(score_grad, queries).astype(HALF)
    value_grad = dot(weights.astype(HALF), upstream).astype(HALF)
    return query_grad, key_grad, value_grad


def fine_forward_kernel(edge, tokens, gain, qkv_w, proj_w, normal, qkv, attended, result):
    def window(w, carry):
        rows = pl.ds(pl.multiple_of(w * CELLS, 16), CELLS)
        values = tokens[rows, :].astype(FULL)
        unit, _ = norm_parts(values)
        normed = (unit * gain[...]).astype(HALF)
        normal[rows, :] = normed
        qkv[rows, :] = dot(normed, qkv_w[...]).astype(HALF)
        mask = pair_mask(jnp.where(w >= 2, edge[0], 0))
        for p in range(4):
            at = 128 * p
            queries = two_heads(qkv[rows, at : at + 128])
            weights = pair_weights(queries, qkv[rows, 512 + at : 640 + at], mask)
            attended[rows, at : at + 128] = pair_forward(weights, qkv[rows, 1024 + at : 1152 + at])
        result[rows, :] = (values + dot(attended[rows, :], proj_w[...])).astype(HALF)
        return carry

    lax.fori_loop(0, 4, window, 0)


def fine_forward(edge, tokens, gain, qkv_w, proj_w):
    return pl.pallas_call(
        fine_forward_kernel,
        out_shape=[jax.ShapeDtypeStruct((576, width), HALF) for width in (512, 1536, 512, 512)],
        in_specs=[SMEM] + [VMEM] * 4,
        out_specs=[VMEM] * 4,
        compiler_params=pltpu.CompilerParams(vmem_limit_bytes=LIMIT),
    )(edge, tokens, gain, qkv_w, proj_w)


def coarse_kernel(
    edge,
    patches,
    cotangent,
    gain_merge,
    gain_coarse,
    merge_any,
    qkv_any,
    proj_any,
    tokens_out,
    patches_grad,
    share_a,
    share_b,
    share_c,
    merge_w,
    qkv_w,
    proj_w,
    unit_merge,
    merged,
    unit_coarse,
    normed,
    qkv,
    attended,
    attended_grad,
    qkv_grad,
    inner_grad,
    weights_all,
    sems,
):
    loads = [
        pltpu.make_async_copy(source, target, sems.at[n])
        for n, (source, target) in enumerate(
            ((merge_any, merge_w), (proj_any, proj_w), (qkv_any, qkv_w))
        )
    ]
    for load in loads:
        load.start()
    values = jnp.concatenate(
        [patches[CELLS * g : CELLS * (g + 1), :] for g in range(4)], axis=1
    ).astype(FULL)
    unit, scale_merge = norm_parts(values)
    unit_merge[...] = unit
    merged[...] = (unit * gain_merge[...]).astype(HALF)
    loads[0].wait()
    coarse_in = dot(merged[...], merge_w[...]).astype(HALF).astype(FULL)
    unit, scale_coarse = norm_parts(coarse_in)
    unit_coarse[...] = unit
    normed[...] = (unit * gain_coarse[...]).astype(HALF)
    loads[1].wait()
    attended_grad[...] = dot_nt(cotangent[...], proj_w[...]).astype(HALF)
    loads[2].wait()
    for n in range(3):
        cols = slice(1024 * n, 1024 * (n + 1))
        qkv[:, cols] = dot(normed[...], qkv_w[:, cols]).astype(HALF)
    mask = pair_mask(edge[0])
    for p in range(8):
        at = 128 * p
        queries = two_heads(qkv[:, at : at + 128])
        weights = pair_weights(queries, qkv[:, 1024 + at : 1152 + at], mask)
        attended[:, at : at + 128] = pair_forward(weights, qkv[:, 2048 + at : 2176 + at])
        upstream = two_heads(attended_grad[:, at : at + 128])
        grads = pair_back(
            weights, queries, qkv[:, 1024 + at : 1152 + at], qkv[:, 2048 + at : 2176 + at], upstream
        )
        for n in range(3):
            qkv_grad[:, 1024 * n + at : 1024 * n + at + 128] = grads[n]
    tokens_out[...] = (coarse_in + dot(attended[...], proj_w[...])).astype(HALF)
    normed_grad = dot_nt(qkv_grad[...], qkv_w[...]).astype(HALF).astype(FULL)
    gain_coarse_terms = (normed_grad * unit_coarse[...]).astype(HALF)
    coarse_grad = cotangent[...].astype(FULL) + norm_back(
        normed_grad, unit_coarse[...], scale_coarse, gain_coarse[...]
    )
    inner_grad[...] = coarse_grad.astype(HALF)
    merged_grad = dot_nt(inner_grad[...], merge_w[...]).astype(HALF).astype(FULL)
    gain_merge_terms = (merged_grad * unit_merge[...]).astype(HALF)
    back = norm_back(merged_grad, unit_merge[...], scale_merge, gain_merge[...]).astype(HALF)
    for g in range(4):
        patches_grad[CELLS * g : CELLS * (g + 1), :] = back[:, 512 * g : 512 * (g + 1)]
    ones = jnp.ones((CELLS, 128), HALF)
    left_lane = lax.broadcasted_iota(jnp.int32, (128, 16, 128), 2) < HD
    by_merge = dot_tn(gain_merge_terms, ones).reshape(128, 16, 128)
    by_coarse = dot_tn(gain_coarse_terms, ones).reshape(128, 8, 128)
    by_coarse = jnp.concatenate([by_coarse, by_coarse], axis=1)
    share_a[:, :, 1024:] = jnp.where(left_lane, by_merge, by_coarse).astype(HALF)

    def merge_rows(n, carry):
        left = merged[:, pl.ds(pl.multiple_of(n * 256, 256), 256)]
        grad = dot_tn(left, inner_grad[...])
        share_a[pl.ds(n * 16, 16), :, :1024] = grad.reshape(16, 16, 1024).astype(HALF)
        return carry

    lax.fori_loop(0, 8, merge_rows, 0)

    def paired(grad, low, high):
        width = low.stop - low.start
        pieces = [grad[:, part].reshape(32, 8, width) for part in (low, high)]
        return jnp.concatenate(pieces, axis=1).astype(HALF)

    def other_rows(n, carry):
        cols = pl.ds(pl.multiple_of(n * 256, 256), 256)
        owners = pl.ds(n * 32, 32)
        left = normed[:, cols]
        for low, high, share, at in (
            (0, 1536, share_b, 0),
            (512, 2048, share_b, 512),
            (1024, 2560, share_c, 0),
        ):
            right = jnp.concatenate(
                [qkv_grad[:, low : low + 512], qkv_grad[:, high : high + 512]], axis=1
            )
            grad = dot_tn(left, right)
            share[owners, :, at : at + 512] = paired(grad, slice(0, 512), slice(512, 1024))
        grad = dot_tn(attended[:, cols], cotangent[...])
        share_c[owners, :, 512:] = paired(grad, slice(0, 512), slice(512, 1024))
        return carry

    lax.fori_loop(0, 4, other_rows, 0)


def coarse_level(edge, patches, cotangent, gain_merge, gain_coarse, merge_w, qkv_w, proj_w):
    half = lambda *shape: pltpu.VMEM(shape, HALF)
    full = lambda *shape: pltpu.VMEM(shape, FULL)
    return pl.pallas_call(
        coarse_kernel,
        out_shape=[
            jax.ShapeDtypeStruct((CELLS, 1024), HALF),
            jax.ShapeDtypeStruct((576, 512), HALF),
            jax.ShapeDtypeStruct((128, 16, 1152), HALF),
            jax.ShapeDtypeStruct((128, 16, 1024), HALF),
            jax.ShapeDtypeStruct((128, 16, 1024), HALF),
        ],
        in_specs=[SMEM] + [VMEM] * 4 + [ANYWHERE] * 3,
        out_specs=[VMEM] * 5,
        scratch_shapes=[
            half(2048, 1024),
            half(1024, 3072),
            half(1024, 1024),
            full(CELLS, 2048),
            half(CELLS, 2048),
            full(CELLS, 1024),
            half(CELLS, 1024),
            half(CELLS, 3072),
            half(CELLS, 1024),
            half(CELLS, 1024),
            half(CELLS, 3072),
            half(CELLS, 1024),
            full(8, 128),
            pltpu.SemaphoreType.DMA((3,)),
        ],
        compiler_params=pltpu.CompilerParams(vmem_limit_bytes=LIMIT),
    )(edge, patches, cotangent, gain_merge, gain_coarse, merge_w, qkv_w, proj_w)


def four_stacked(pieces):
    rows, width = pieces[0].shape
    shaped = [piece.reshape(rows // 8, 8, width) for piece in pieces]
    upper = lax.broadcasted_iota(jnp.int32, shaped[0].shape, 1) < 4
    turned = [pltpu.roll(piece, 4, 1) for piece in shaped]
    even = [jnp.where(upper, shaped[n], turned[n + 1]) for n in (0, 2)]
    odd = [jnp.where(upper, turned[n], shaped[n + 1]) for n in (0, 2)]
    return [jnp.concatenate(pair, axis=1).astype(HALF) for pair in (even, odd)]


def fine_backward_kernel(
    edge,
    tokens,
    normal,
    qkv,
    attended,
    result_grad,
    gain,
    qkv_w,
    proj_w,
    tokens_grad,
    share_a,
    share_b,
    share_c,
    qkv_grad,
    terms,
):
    def window(w, carry):
        rows = pl.ds(pl.multiple_of(w * CELLS, 16), CELLS)
        attended_grad = dot_nt(result_grad[rows, :], proj_w[...]).astype(HALF)
        mask = pair_mask(jnp.where(w >= 2, edge[0], 0))
        for p in range(4):
            at = 128 * p
            queries = two_heads(qkv[rows, at : at + 128])
            keys = qkv[rows, 512 + at : 640 + at]
            weights = pair_weights(queries, keys, mask)
            grads = pair_back(
                weights,
                queries,
                keys,
                qkv[rows, 1024 + at : 1152 + at],
                two_heads(attended_grad[:, at : at + 128]),
            )
            for n in range(3):
                qkv_grad[rows, 512 * n + at : 512 * n + at + 128] = grads[n]
        normed_grad = dot_nt(qkv_grad[rows, :], qkv_w[...]).astype(HALF).astype(FULL)
        unit, scale = norm_parts(tokens[rows, :].astype(FULL))
        terms[rows, :] = (normed_grad * unit).astype(HALF)
        back = norm_back(normed_grad, unit, scale, gain[...])
        tokens_grad[rows, :] = (result_grad[rows, :].astype(FULL) + back).astype(HALF)
        return carry

    lax.fori_loop(0, 4, window, 0)
    ones = jnp.ones((576, 128), HALF)

    def weight_rows(n, carry):
        cols = pl.ds(pl.multiple_of(n * 128, 128), 128)
        owners = pl.ds(n * 16, 16)

        def store(share, at, pieces):
            width = pieces[0].shape[1]
            for side, value in enumerate(four_stacked(pieces)):
                share[owners, side, :, at : at + width] = value

        grad = dot_tn(normal[:, cols], qkv_grad[...])
        store(share_a, 0, [grad[:, 384 * m : 384 * m + 256] for m in range(4)])
        store(share_b, 0, [grad[:, 384 * m + 256 : 384 * m + 384] for m in range(4)])
        grad = dot_tn(attended[:, cols], result_grad[...])
        store(share_b, 128, [grad[:, 128 * m : 128 * m + 128] for m in range(4)])
        store(share_c, 0, [dot_tn(terms[:, cols], ones)] * 4)
        return carry

    lax.fori_loop(0, 4, weight_rows, 0)


def fine_backward(edge, tokens, normal, qkv, attended, result_grad, gain, qkv_w, proj_w):
    return pl.pallas_call(
        fine_backward_kernel,
        out_shape=[jax.ShapeDtypeStruct((576, 512), HALF)]
        + [jax.ShapeDtypeStruct((64, 2, 16, width), HALF) for width in (256, 256, 128)],
        in_specs=[SMEM] + [VMEM] * 8,
        out_specs=[VMEM] * 4,
        scratch_shapes=[pltpu.VMEM((576, 1536), HALF), pltpu.VMEM((576, 512), HALF)],
        compiler_params=pltpu.CompilerParams(vmem_limit_bytes=LIMIT),
    )(edge, tokens, normal, qkv, attended, result_grad, gain, qkv_w, proj_w)


def device_parts(
    tokens,
    cotangent,
    gain_fine,
    qkv_fine,
    proj_fine,
    gain_merge,
    merge_weight,
    gain_coarse,
    qkv_coarse,
    proj_coarse,
):
    last = lax.axis_index("lat") == lax.axis_size("lat") - 1
    edge = last.astype(jnp.int32).reshape(1)
    gain_f = gain_fine.reshape(1, 512)
    gain_m = gain_merge.reshape(1, 2048)
    gain_c = gain_coarse.reshape(1, 1024)
    rolled, cotangent_rolled = roll_grids(
        [
            (tokens.reshape(576, 512), 12, 24, "natural", "window"),
            (cotangent.reshape(CELLS, 1024), 6, 12, "natural", "window"),
        ],
        1,
        1,
    )
    normal, qkv, attended, fine_out = fine_forward(edge, rolled, gain_f, qkv_fine, proj_fine)
    (patches,) = roll_grids([(fine_out, 12, 24, "window", "patch")], 1, 2)
    coarse_out, patches_grad, *coarse_shares = coarse_level(
        edge, patches, cotangent_rolled, gain_m, gain_c, merge_weight, qkv_coarse, proj_coarse
    )
    coarse_tokens, fine_grad = roll_grids(
        [
            (coarse_out, 6, 12, "window", "natural"),
            (patches_grad, 12, 24, "patch", "window"),
        ],
        -1,
        3,
    )
    tokens_grad, *fine_shares = fine_backward(
        edge, rolled, normal, qkv, attended, fine_grad, gain_f, qkv_fine, proj_fine
    )
    (tokens_grad,) = roll_grids([(tokens_grad, 12, 24, "window", "natural")], -1, 4)
    return (
        coarse_tokens.reshape(2, 6, 12, 1024),
        tokens_grad.reshape(2, 12, 24, 512),
        coarse_shares,
        fine_shares,
    )


ORDERS = (("x", "y", "z"), ("y", "z", "x"), ("z", "x", "y"))
LEADS = (((4, 2, 2), (2, 2)), ((2, 4, 2), (4,)), ((4, 4), (4,)))


def position():
    lat = lax.axis_index("lat")
    lon = lax.axis_index("lon")
    return {"y": lat // 2, "x": lon // 4, "z": lat % 2 * 2 + lon // 2 % 2}, lon % 2


def device_at(place, core):
    lat = place["y"] * 2 + place["z"] // 2
    lon = place["x"] * 4 + place["z"] % 2 * 2 + core
    return (lat, lon)


def along(place, axis, steps):
    moved = dict(place)
    moved[axis] = lax.rem(place[axis] + steps, 4)
    return moved


def first_cut(kind, ref, index, core):
    if kind == 0:
        return ref.at[:, :, index, :, core]
    if kind == 1:
        return ref.at[index, :, :, :, core]
    return ref.at[:, index // 2, :, index % 2, core]


def second_cut(kind, ref, index):
    if kind == 0:
        return ref.at[index]
    if kind == 1:
        return ref.at[index // 2, :, index % 2]
    return ref.at[:, index]


def third_cut(kind, ref, index):
    if kind == 0:
        return ref.at[index // 2, index % 2]
    return ref.at[index]


def spots(lead, i):
    found = []
    for size in reversed(lead):
        found.insert(0, i % size)
        i = i // size
    return tuple(found)


def greet(place, core):
    barrier = pltpu.get_barrier_semaphore()
    partners = [device_at(place, 1 - core)] + [
        device_at(along(place, axis, k), core) for axis in ("x", "y", "z") for k in (1, 2, 3)
    ]
    for partner in partners:
        pl.semaphore_signal(barrier, inc=1, device_id=partner, device_id_type=MESH)
    pl.semaphore_wait(barrier, len(partners))


def scatter_steps(place, core, given, own, first, landed, summed, sems):
    local_sem, send_sem, recv_sem = sems
    parts = range(len(given))
    sibling = device_at(place, 1 - core)

    def remote(source, target, p, slot, device):
        return pltpu.make_async_remote_copy(
            src_ref=source,
            dst_ref=target,
            send_sem=send_sem.at[p, slot],
            recv_sem=recv_sem.at[p, slot],
            device_id=device,
            device_id_type=MESH,
        )

    pairs, keeps = {}, {}
    for k in (1, 2, 3, 0):
        for p in parts:
            index = lax.rem(place[ORDERS[p % 3][0]] + k, 4)
            pairs[p, k] = remote(
                first_cut(p % 3, given[p], index, 1 - core), first[p].at[k], p, k, sibling
            )
            pairs[p, k].start()
            keeps[p, k] = pltpu.make_async_copy(
                first_cut(p % 3, given[p], index, core), own[p].at[k], local_sem.at[p, k]
            )
            keeps[p, k].start()

    sends = {}
    for k in (1, 2, 3, 0):
        for p in parts:
            pairs[p, k].wait()
            keeps[p, k].wait()

            def add_one(i, carry, p=p, k=k):
                at = (k,) + spots(LEADS[p % 3][0], i)
                first[p][at] = first[p][at] + own[p][at]
                return carry

            lax.fori_loop(0, 16, add_one, 0)
            if k > 0:
                target = device_at(along(place, ORDERS[p % 3][0], k), core)
                sends[p, k] = remote(first[p].at[k], landed[p][0].at[k - 1], p, 3 + k, target)
                sends[p, k].start()

    def added(base, arrivals):
        total = base.astype(FULL)
        for arrival in arrivals:
            total = total + arrival.astype(FULL)
        return total

    second = {}
    for p in parts:
        for k in (1, 2, 3):
            sends[p, k].wait()

        def add_three(i, carry, p=p):
            at = spots(LEADS[p % 3][0], i)
            total = added(first[p][(0,) + at], [landed[p][0][(k,) + at] for k in range(3)])
            summed[p][0][at] = total.astype(HALF)
            return carry

        lax.fori_loop(0, 16, add_three, 0)
        axis = ORDERS[p % 3][1]
        for k in (1, 2, 3):
            moved = along(place, axis, k)
            second[p, k] = remote(
                second_cut(p % 3, summed[p][0], moved[axis]),
                landed[p][1].at[k - 1],
                p,
                6 + k,
                device_at(moved, core),
            )
            second[p, k].start()
    third = {}
    for p in parts:
        for k in (1, 2, 3):
            second[p, k].wait()
        mine = second_cut(p % 3, summed[p][0], place[ORDERS[p % 3][1]])
        total = added(mine[...], [landed[p][1][k] for k in range(3)])
        summed[p][1][...] = total.astype(HALF)
        axis = ORDERS[p % 3][2]
        for k in (1, 2, 3):
            moved = along(place, axis, k)
            third[p, k] = remote(
                third_cut(p % 3, summed[p][1], moved[axis]),
                landed[p][2].at[k - 1],
                p,
                9 + k,
                device_at(moved, core),
            )
            third[p, k].start()
    results = []
    for p in parts:
        for k in (1, 2, 3):
            third[p, k].wait()
        mine = third_cut(p % 3, summed[p][1], place[ORDERS[p % 3][2]])
        results.append(added(mine[...], [landed[p][2][k] for k in range(3)]))
    return results


def scatter_scratch(widths):
    scratch = []
    for n, width in enumerate(widths):
        lead = LEADS[n % 3]
        scratch += [
            pltpu.VMEM((4,) + lead[0] + (16, width), HALF),
            pltpu.VMEM((4,) + lead[0] + (16, width), HALF),
            pltpu.VMEM((3,) + lead[0] + (16, width), HALF),
            pltpu.VMEM((3,) + lead[1] + (16, width), HALF),
            pltpu.VMEM((3, 16, width), HALF),
            pltpu.VMEM(lead[0] + (16, width), HALF),
            pltpu.VMEM(lead[1] + (16, width), HALF),
        ]
    count = len(widths)
    return scratch + [
        pltpu.SemaphoreType.DMA((count, 4)),
        pltpu.SemaphoreType.DMA((count, 13)),
        pltpu.SemaphoreType.DMA((count, 13)),
    ]


def scatter_groups(scratch, count):
    groups = [scratch[7 * p : 7 * p + 7] for p in range(count)]
    return (
        [group[0] for group in groups],
        [group[1] for group in groups],
        [group[2:5] for group in groups],
        [group[5:7] for group in groups],
        scratch[7 * count :],
    )


def write_coarse(shares, merge_out, qkv_out, proj_out, gains_out):
    a, b, c = shares
    merge_out[...] = a[:, :1024]
    gains_out[...] = a[:, 1024:]
    for n in range(2):
        rows = slice(8 * n, 8 * n + 8)
        qkv_out[:, 1536 * n : 1536 * n + 1024] = b[rows]
        qkv_out[:, 1536 * n + 1024 : 1536 * n + 1536] = c[rows, :512]
        proj_out[:, 512 * n : 512 * n + 512] = c[rows, 512:]


def write_fine(shares, qkv_out, proj_out, gains_out):
    a, b, c = shares
    gains_out[...] = c
    for n in range(4):
        rows = slice(4 * n, 4 * n + 4)
        qkv_out[:, 384 * n : 384 * n + 256] = a[rows]
        qkv_out[:, 384 * n + 256 : 384 * n + 384] = b[rows, :128]
        proj_out[:, 128 * n : 128 * n + 128] = b[rows, 128:]


COARSE_OUT = ((16, 1024), (8, 3072), (8, 1024), (16, 128))
FINE_OUT = ((4, 1536), (4, 512), (16, 128))


def scatter_kernel(*refs):
    given, outs, scratch = refs[:6], refs[6:13], refs[13:]
    place, core = position()
    greet(place, core)
    results = scatter_steps(place, core, given, *scatter_groups(scratch, 6))
    write_coarse(results[:3], *outs[:4])
    write_fine(results[3:], *outs[4:])


def scatter_sum(arrays, identity):
    arrays = [array.reshape(4, 2, 4, 2, 2, 16, array.shape[-1]) for array in arrays]
    widths = [array.shape[-1] for array in arrays]
    return pl.pallas_call(
        scatter_kernel,
        out_shape=[jax.ShapeDtypeStruct(shape, FULL) for shape in COARSE_OUT + FINE_OUT],
        in_specs=[ANYWHERE] * 6,
        out_specs=[VMEM] * 7,
        scratch_shapes=scatter_scratch(widths),
        compiler_params=pltpu.CompilerParams(
            collective_id=identity, has_side_effects=True, vmem_limit_bytes=LIMIT
        ),
    )(*arrays)


def local(*args):
    coarse_tokens, tokens_grad, coarse_shares, fine_shares = device_parts(*args)
    merge, qkv_c, proj_c, gains_c, qkv_f, proj_f, gains_f = scatter_sum(
        list(coarse_shares) + list(fine_shares), 5
    )
    return (
        coarse_tokens,
        tokens_grad,
        gains_f[:4, 0],
        qkv_f,
        proj_f,
        gains_c[:, 0],
        merge,
        gains_c[:8, HD],
        qkv_c,
        proj_c,
    )


def solution(mesh):
    grid = P(None, "lat", "lon", None)
    vector, matrix = P(("lat", "lon")), P(("lat", "lon"), None)
    return jax.shard_map(
        local,
        mesh=mesh,
        in_specs=(grid, grid) + (P(),) * 8,
        out_specs=(grid, grid, vector, matrix, matrix, vector, matrix, vector, matrix, matrix),
        check_vma=False,
    )
```

```python
import functools
from types import SimpleNamespace

import jax
import jax.numpy as jnp
import numpy as np
from jax import lax
from jax.experimental import pallas as pl
from jax.experimental.pallas import tpu as pltpu
from jax.sharding import PartitionSpec as P

MESH = pl.DeviceIdType.MESH
HALF = jnp.bfloat16
FULL = jnp.float32
HD = 64
WH = 6
WW = 12
CELLS = 144
EPSILON = 1e-05
MASKED = -1e30
PIECES = (0, 128, 256)
PACKED = 304
LIMIT = 62 * 1024 * 1024
VMEM = pl.BlockSpec(memory_space=pltpu.VMEM)
SMEM = pl.BlockSpec(memory_space=pltpu.SMEM)
ANYWHERE = pl.BlockSpec(memory_space=pl.ANY)


def dot(left, right):
    return jnp.dot(left, right, preferred_element_type=FULL)


def dot_nt(left, right):
    return lax.dot_general(left, right, (((1,), (1,)), ((), ())), preferred_element_type=FULL)


def dot_tn(left, right):
    return lax.dot_general(left, right, (((0,), (0,)), ((), ())), preferred_element_type=FULL)


def natural_order(rows, cols):
    return lambda level, i, j: (level * rows + i) * cols + j


def window_order(rows, cols):
    def place(level, i, j):
        window = i // WH * (cols // WW) + j // WW
        return window * CELLS + ((i % WH // 3 * 2 + level) * 3 + i % 3) * WW + j % WW

    return place


def patch_order(rows, cols):
    coarse = window_order(rows // 2, cols // 2)

    def place(level, i, j):
        return (j % 2 * 2 + i % 2) * CELLS + coarse(level, i // 2, j // 2)

    return place


@functools.lru_cache(maxsize=None)
def roll_matrices(rows, cols, source, target, sign):
    orders = {"natural": natural_order, "window": window_order, "patch": patch_order}
    from_place, to_place = orders[source](rows, cols), orders[target](rows, cols)
    count = 2 * rows * cols
    pieces = ([], [], [])
    own = np.zeros((count, count), np.float32)
    for level in range(2):
        for i in range(rows):
            for j in range(cols):
                far_i, far_j = i + 3 * sign, j + 6 * sign
                across = (far_i // rows != 0, far_j // cols != 0)
                here = from_place(level, far_i % rows, far_j % cols)
                there = to_place(level, i, j)
                if across == (False, False):
                    own[there, here] = 1
                else:
                    slot = {(False, True): 0, (True, False): 1, (True, True): 2}[across]
                    pieces[slot].append((there, here))
    sizes = tuple((len(piece) + 15) // 16 * 16 for piece in pieces)
    pack = np.zeros((PACKED, count), np.float32)
    halo = np.zeros((count, PACKED), np.float32)
    for slot, piece in enumerate(pieces):
        for k, (there, here) in enumerate(piece):
            pack[PIECES[slot] + k, here] = 1
            halo[there, PIECES[slot] + k] = 1
    return pack, own, halo, sizes


def norm_parts(values):
    centre = jnp.mean(values, axis=-1, keepdims=True)
    offset = values - centre
    spread = jnp.mean(offset * offset, axis=-1, keepdims=True)
    scale = lax.rsqrt(spread + EPSILON)
    return offset * scale, scale


def norm_back(grad, normal, scale, gain):
    inner = grad * gain
    mean = jnp.mean(inner, axis=-1, keepdims=True)
    along = jnp.mean(inner * normal, axis=-1, keepdims=True)
    return (inner - mean - normal * along) * scale


def two_heads(pair):
    first = lax.broadcasted_iota(jnp.int32, pair.shape, 1) < HD
    zero = jnp.zeros_like(pair)
    return jnp.concatenate([jnp.where(first, pair, zero), jnp.where(first, zero, pair)], axis=0)


def one_pair(stack):
    half = stack.shape[0] // 2
    first = lax.broadcasted_iota(jnp.int32, (half, 2 * HD), 1) < HD
    return jnp.where(first, stack[:half], stack[half:])


def pair_mask(edge):
    shape = (CELLS, 2 * CELLS)
    key = lax.broadcasted_iota(jnp.int32, shape, 0)
    query = lax.broadcasted_iota(jnp.int32, shape, 1)
    query = jnp.where(query >= CELLS, query - CELLS, query)
    apart = (key < CELLS // 2) != (query < CELLS // 2)
    return jnp.where(apart, edge, 0) > 0


def pair_weights(queries, keys, mask):
    scores = dot_nt(keys, queries * 0.125)
    scores = jnp.where(mask, MASKED, scores)
    powers = jnp.exp(scores - jnp.max(scores, axis=0, keepdims=True))
    return powers * (1.0 / jnp.sum(powers, axis=0, keepdims=True))


def pair_forward(weights, values):
    return one_pair(dot_tn(weights.astype(HALF), values)).astype(HALF)


def pair_back(weights, queries, keys, values, upstream):
    weight_grad = dot_nt(values, upstream)
    inner = jnp.sum(weights * weight_grad, axis=0, keepdims=True)
    score_grad = (weights * (weight_grad - inner) * 0.125).astype(HALF)
    query_grad = one_pair(dot_tn(score_grad, keys)).astype(HALF)
    key_grad = dot(score_grad, queries).astype(HALF)
    value_grad = dot(weights.astype(HALF), upstream).astype(HALF)
    return query_grad, key_grad, value_grad


def four_stacked(pieces):
    rows, width = pieces[0].shape
    shaped = [piece.reshape(rows // 8, 8, width) for piece in pieces]
    upper = lax.broadcasted_iota(jnp.int32, shaped[0].shape, 1) < 4
    turned = [pltpu.roll(piece, 4, 1) for piece in shaped]
    even = [jnp.where(upper, shaped[n], turned[n + 1]) for n in (0, 2)]
    odd = [jnp.where(upper, turned[n], shaped[n + 1]) for n in (0, 2)]
    return [jnp.concatenate(pair, axis=1).astype(HALF) for pair in (even, odd)]


ORDERS = (("x", "y", "z"), ("y", "z", "x"), ("z", "x", "y"))
LEADS = (((4, 2, 2), (2, 2)), ((2, 4, 2), (4,)), ((4, 4), (4,)))
WIDTHS = (1152, 1024, 1024, 256, 256, 128)
LON, LAT, DIAG = 0, 1, 2
STEPS = ((0, 1), (1, 0), (1, 1))


def device_at(place, core):
    lat = place["y"] * 2 + place["z"] // 2
    lon = place["x"] * 4 + place["z"] % 2 * 2 + core
    return (lat, lon)


def along(place, axis, steps):
    moved = dict(place)
    moved[axis] = lax.rem(place[axis] + steps, 4)
    return moved


def first_cut(kind, ref, index):
    if kind == 0:
        return ref.at[:, :, index]
    if kind == 1:
        return ref.at[index]
    return ref.at[:, index // 2, :, index % 2]


def second_cut(kind, ref, index):
    if kind == 0:
        return ref.at[index]
    if kind == 1:
        return ref.at[index // 2, :, index % 2]
    return ref.at[:, index]


def third_cut(kind, ref, index):
    if kind == 0:
        return ref.at[index // 2, index % 2]
    return ref.at[index]


def spots(lead, i):
    found = []
    for size in reversed(lead):
        found.insert(0, i % size)
        i = i // size
    return tuple(found)


def added(base, arrivals):
    total = base.astype(FULL)
    for arrival in arrivals:
        total = total + arrival.astype(FULL)
    return total


def of(r, name, p):
    return getattr(r, name + str(p))


def owner_pick(rows_each, core):
    shift = rows_each.bit_length() - 1
    feature = lax.broadcasted_iota(jnp.int32, (256, 128), 0)
    place = lax.broadcasted_iota(jnp.int32, (256, 128), 1)
    wanted = ((place >> shift) << (shift + 1)) + (place & (rows_each - 1)) + core * rows_each
    return jnp.where(feature == wanted, 1.0, 0.0).astype(HALF)


def in_two(row):
    high = row.astype(HALF)
    low = (row - high.astype(FULL)).astype(HALF)
    place = lax.broadcasted_iota(jnp.int32, (16, row.shape[1]), 0)
    wide_high = jnp.broadcast_to(high.astype(FULL), place.shape)
    wide_low = jnp.broadcast_to(low.astype(FULL), place.shape)
    return jnp.where(place == 0, wide_high, jnp.where(place == 1, wide_low, 0.0)).astype(HALF)


def whole_kernel(names, summing, *refs):
    r = SimpleNamespace(**dict(zip(names, refs)))
    lat, lon = lax.axis_index("lat"), lax.axis_index("lon")
    lats, lons = lax.axis_size("lat"), lax.axis_size("lon")
    core = lon % 2
    place = {"y": lat // 2, "x": lon // 4, "z": lat % 2 * 2 + lon // 2 % 2}
    sibling = (lat, lon + 1 - 2 * core)
    edge = jnp.where(lat == lats - 1, 1, 0)
    used = [0]

    def remote(source, target, device):
        slot = used[0]
        used[0] += 1
        copy = pltpu.make_async_remote_copy(
            src_ref=source,
            dst_ref=target,
            send_sem=r.send_sem.at[slot],
            recv_sem=r.recv_sem.at[slot],
            device_id=device,
            device_id_type=MESH,
        )
        copy.start()
        return copy

    def neighbour(step, way):
        return (
            lax.rem(lat + lats + way * step[0], lats),
            lax.rem(lon + lons + way * step[1], lons),
        )

    loads = {}

    def load(name):
        slot = LOADED.index(name)
        loads[name] = pltpu.make_async_copy(getattr(r, name + "_any"), getattr(r, name), r.load_sem.at[slot])
        loads[name].start()

    for kind, held in (("back", "in"), ("end", "mid")):
        for matrix in ("_pack", "_own", "_halo"):
            setattr(r, kind + matrix, getattr(r, held + matrix))
    r.patches_grad = r.fine_out
    for name in LOADED[:11]:
        load(name)

    barrier = pltpu.get_barrier_semaphore()
    partners = [neighbour(step, way) for step in STEPS for way in (1, -1)] + [sibling]
    if summing:
        partners += [
            device_at(along(place, axis, k), core) for axis in ("x", "y", "z") for k in (1, 2, 3)
        ]
    for partner in partners:
        pl.semaphore_signal(barrier, inc=1, device_id=partner, device_id_type=MESH)

    def pack_piece(kind, value, slot, size):
        rows = slice(PIECES[slot], PIECES[slot] + size)
        getattr(r, kind + "_packed")[rows, :] = dot(getattr(r, kind + "_pack")[rows, :], value).astype(HALF)

    def send_piece(kind, slot, size, sign):
        rows = pl.ds(PIECES[slot], size)
        return remote(
            getattr(r, kind + "_packed").at[rows],
            getattr(r, kind + "_landed").at[rows],
            neighbour(STEPS[slot], -sign),
        )

    def gathered(kind, rows, value, sizes, needed):
        total = dot(getattr(r, kind + "_own")[rows, :], value)
        for slot in needed:
            piece = slice(PIECES[slot], PIECES[slot] + sizes[slot])
            total = total + dot(getattr(r, kind + "_halo")[rows, piece], getattr(r, kind + "_landed")[piece, :])
        return total

    fine_sizes, coarse_sizes = (112, 112, 48), (48, 48, 48)
    loads["in_pack"].wait()
    for slot in (LAT, DIAG, LON):
        pack_piece("in", r.tokens[...], slot, fine_sizes[slot])
    for slot in (LAT, DIAG, LON):
        pack_piece("cot", r.cotangent[...], slot, coarse_sizes[slot])
    pl.semaphore_wait(barrier, len(partners))
    arrive = {slot: send_piece("in", slot, fine_sizes[slot], 1) for slot in (LAT, DIAG, LON)}
    cot_arrive = [send_piece("cot", slot, coarse_sizes[slot], 1) for slot in (LAT, DIAG, LON)]
    r.fine_out[...] = jnp.zeros_like(r.fine_out)
    r.tokens_back[...] = jnp.zeros_like(r.tokens_back)

    keep4, give4 = owner_pick(4, core), owner_pick(4, 1 - core)
    keep8, give8 = owner_pick(8, core), owner_pick(8, 1 - core)
    keep16, give16 = owner_pick(16, core), owner_pick(16, 1 - core)

    def split(value, keep, give, name, rows):
        for block in range(value.shape[1] // 256):
            part = value[:, 256 * block : 256 * block + 256]
            cols = slice(128 * block, 128 * block + 128)
            getattr(r, name + "_left")[rows, cols] = dot(part, keep).astype(HALF)
            getattr(r, name + "_give")[rows, cols] = dot(part, give).astype(HALF)

    def hand_left(name):
        count = getattr(r, name + "_give").shape[0]
        return remote(getattr(r, name + "_give"), getattr(r, name + "_left").at[pl.ds(count, count)], sibling)

    def hand_right(name, start, size):
        half = getattr(r, name).shape[0] // 2
        held = getattr(r, name)
        return remote(held.at[pl.ds(start, size)], held.at[pl.ds(half + start, size)], sibling)

    handed_fine, handed_coarse, late = [], [], []

    needs = ((), (LON,), (LAT,), (LON, LAT, DIAG))
    waited = set()
    mid_arrive = []
    for name in ("in_own", "in_halo", "qkv_f", "proj_f", "mid_pack"):
        loads[name].wait()
    for w in range(4):
        for slot in needs[w]:
            if slot not in waited:
                arrive[slot].wait()
                waited.add(slot)
        rows = slice(CELLS * w, CELLS * w + CELLS)
        values = gathered("in", rows, r.tokens[...], fine_sizes, needs[w])
        r.rolled[rows, :] = values.astype(HALF)
        unit, _ = norm_parts(values)
        normed = (unit * r.gain_f[...]).astype(HALF)
        split(normed, keep4, give4, "normal", rows)
        qkv = r.qkv
        for n in range(3):
            cols = slice(512 * n, 512 * n + 512)
            qkv[rows, cols] = dot(normed, r.qkv_f[:, cols]).astype(HALF)
        mask = pair_mask(edge if w >= 2 else 0)
        for p in range(4):
            at = 128 * p
            queries = two_heads(qkv[rows, at : at + 128])
            weights = pair_weights(queries, qkv[rows, 512 + at : 640 + at], mask)
            r.attended[rows, at : at + 128] = pair_forward(
                weights, qkv[rows, 1024 + at : 1152 + at]
            )
        attended = r.attended[rows, :]
        split(attended, keep4, give4, "attended", rows)
        r.fine_out[rows, :] = (values + dot(attended, r.proj_f[...])).astype(HALF)
        for slot in {1: (LAT,), 2: (DIAG, LON)}.get(w, ()):
            pack_piece("mid", r.fine_out[...], slot, fine_sizes[slot])
            mid_arrive.append(send_piece("mid", slot, fine_sizes[slot], 1))
    handed_fine += [hand_left("normal"), hand_left("attended")]
    for name in LOADED[11:14]:
        load(name)

    for copy in cot_arrive:
        copy.wait()
    every = slice(None)
    cot = gathered("cot", every, r.cotangent[...], coarse_sizes, (LON, LAT, DIAG)).astype(HALF)
    own = slice(0, CELLS)
    r.cot_right[own, :] = cot
    handed_coarse.append(hand_right("cot_right", 0, CELLS))
    loads["proj_c"].wait()
    r.cot_attended[...] = dot_nt(cot, r.proj_c[...]).astype(HALF)
    loads["mid_own"].wait()
    loads["mid_halo"].wait()
    for copy in mid_arrive:
        copy.wait()
    values = jnp.concatenate(
        [
            gathered(
                "mid",
                slice(CELLS * g, CELLS * g + CELLS),
                r.fine_out[...],
                fine_sizes,
                (LON, LAT, DIAG),
            )
            for g in range(4)
        ],
        axis=1,
    )
    for name in LOADED[14:]:
        load(name)
    unit, scale_merge = norm_parts(values)
    r.unit_merge[...] = unit
    merged = (unit * r.gain_m[...]).astype(HALF)
    loads["merge_w"].wait()
    coarse_in = dot(merged, r.merge_w[...]).astype(HALF).astype(FULL)
    split(merged, keep16, give16, "merged", own)
    merged_handed = hand_left("merged")
    unit, scale_coarse = norm_parts(coarse_in)
    r.unit_coarse[...] = unit
    normed = (unit * r.gain_c[...]).astype(HALF)
    loads["qkv_c"].wait()
    for n in range(3):
        cols = slice(1024 * n, 1024 * (n + 1))
        r.qkv_coarse[:, cols] = dot(normed, r.qkv_c[:, cols]).astype(HALF)
    split(normed, keep8, give8, "normed", own)
    handed_coarse.append(hand_left("normed"))
    qkv = r.qkv_coarse
    mask = pair_mask(edge)
    for p in range(8):
        at = 128 * p
        queries = two_heads(qkv[:, at : at + 128])
        keys, worth = qkv[:, 1024 + at : 1152 + at], qkv[:, 2048 + at : 2176 + at]
        weights = pair_weights(queries, keys, mask)
        r.coarse_attended[:, at : at + 128] = pair_forward(weights, worth)
        upstream = two_heads(r.cot_attended[:, at : at + 128])
        grads = pair_back(weights, queries, keys, worth, upstream)
        for n in range(3):
            r.qkv_right[own, 1024 * n + at : 1024 * n + at + 128] = grads[n]
    handed_coarse.append(hand_right("qkv_right", 0, CELLS))
    attended = r.coarse_attended[...]
    split(attended, keep8, give8, "coarse", own)
    handed_coarse.append(hand_left("coarse"))
    normed_grad = dot_nt(r.qkv_right[own, :], r.qkv_c[...]).astype(HALF).astype(FULL)
    gain_row = jnp.sum(normed_grad * r.unit_coarse[...], axis=0, keepdims=True)
    split(in_two(gain_row), keep8, give8, "gain_coarse", slice(0, 16))
    gains_handed = [hand_left("gain_coarse")]
    coarse_grad = r.cot_right[own, :].astype(FULL) + norm_back(
        normed_grad, r.unit_coarse[...], scale_coarse, r.gain_c[...]
    )
    r.inner_right[own, :] = coarse_grad.astype(HALF)
    inner_handed = hand_right("inner_right", 0, CELLS)
    merged_grad = dot_nt(r.inner_right[own, :], r.merge_w[...]).astype(HALF).astype(FULL)
    gain_row = jnp.sum(merged_grad * r.unit_merge[...], axis=0, keepdims=True)
    split(in_two(gain_row), keep16, give16, "gain_merge", slice(0, 16))
    gains_handed.append(hand_left("gain_merge"))
    back = norm_back(merged_grad, r.unit_merge[...], scale_merge, r.gain_m[...]).astype(HALF)
    for g in range(4):
        r.patches_grad[CELLS * g : CELLS * (g + 1), :] = back[:, 512 * g : 512 * (g + 1)]
    for name in ("back_pack", "back_own", "back_halo"):
        loads[name].wait()
    back_arrive = {}
    for slot in (LAT, DIAG, LON):
        pack_piece("back", r.patches_grad[...], slot, fine_sizes[slot])
        back_arrive[slot] = send_piece("back", slot, fine_sizes[slot], -1)
    r.coarse_out[...] = (coarse_in + dot(attended, r.proj_c[...])).astype(HALF)
    for slot in (LAT, DIAG, LON):
        pack_piece("out", r.coarse_out[...], slot, coarse_sizes[slot])
    out_arrive = [send_piece("out", slot, coarse_sizes[slot], -1) for slot in (LAT, DIAG, LON)]

    sums = {}

    def start_first(p):
        axis = ORDERS[p % 3][0]
        sums[p] = []
        for k in (2, 1, 3):
            moved = along(place, axis, k)
            sums[p].append(
                remote(
                    first_cut(p % 3, of(r, "share", p), moved[axis]),
                    of(r, "landed0_", p).at[k - 1],
                    device_at(moved, core),
                )
            )

    def start_second(p):
        for copy in sums[p]:
            copy.wait()
        mine = first_cut(p % 3, of(r, "share", p), place[ORDERS[p % 3][0]])

        def add(i, carry):
            at = spots(LEADS[p % 3][0], i)
            total = added(mine[at], [of(r, "landed0_", p)[(k,) + at] for k in range(3)])
            of(r, "landed0_", p)[(0,) + at] = total.astype(HALF)
            return carry

        lax.fori_loop(0, 16, add, 0)
        axis = ORDERS[p % 3][1]
        sums[p] = []
        for k in (2, 1, 3):
            moved = along(place, axis, k)
            sums[p].append(
                remote(
                    second_cut(p % 3, of(r, "landed0_", p).at[0], moved[axis]),
                    of(r, "landed1_", p).at[k - 1],
                    device_at(moved, core),
                )
            )

    def start_third(p):
        for copy in sums[p]:
            copy.wait()
        mine = second_cut(p % 3, of(r, "landed0_", p).at[0], place[ORDERS[p % 3][1]])
        total = added(mine[...], [of(r, "landed1_", p)[k] for k in range(3)])
        of(r, "summed1_", p)[...] = total.astype(HALF)
        axis = ORDERS[p % 3][2]
        sums[p] = []
        for k in (2, 1, 3):
            moved = along(place, axis, k)
            sums[p].append(
                remote(
                    third_cut(p % 3, of(r, "summed1_", p), moved[axis]),
                    of(r, "landed2_", p).at[k - 1],
                    device_at(moved, core),
                )
            )

    def finish(p):
        for copy in sums[p]:
            copy.wait()
        mine = third_cut(p % 3, of(r, "summed1_", p), place[ORDERS[p % 3][2]])
        total = added(mine[...], [of(r, "landed2_", p)[k] for k in range(3)])
        of(r, "sum", p)[...] = total

    for copy in handed_coarse:
        copy.wait()

    def paired(grad, lead):
        width = grad.shape[1] // 2
        rows = grad.shape[0] // 8
        pieces = [grad[:, :width].reshape(rows, 8, width), grad[:, width:].reshape(rows, 8, width)]
        return jnp.concatenate(pieces, axis=1).astype(HALF).reshape(lead + (16, width))

    def qkv_rows(n, carry):
        cols = pl.ds(pl.multiple_of(n * 256, 256), 256)
        left = r.normed_left[:, cols]
        for low, share, at in ((0, 1, 0), (512, 1, 512), (1024, 2, 0)):
            right = jnp.concatenate(
                [
                    r.qkv_right[:, low : low + 512],
                    r.qkv_right[:, low + 1536 : low + 2048],
                ],
                axis=1,
            )
            of(r, "share", share)[pl.ds(n * 2, 2), :, :, :, :, at : at + 512] = paired(
                dot_tn(left, right), (2, 2, 4, 2)
            )
        grad = dot_tn(r.coarse_left[:, cols], r.cot_right[...])
        r.share2[pl.ds(n * 2, 2), :, :, :, :, 512:] = paired(grad, (2, 2, 4, 2))
        return carry

    lax.fori_loop(0, 2, qkv_rows, 0)
    if summing:
        start_first(1)
        start_first(2)
    for copy in gains_handed + [merged_handed, inner_handed]:
        copy.wait()
    ones = jnp.ones((32, 128), HALF)
    left_lane = lax.broadcasted_iota(jnp.int32, (64, 16, 128), 2) < HD
    by_merge = dot_tn(r.gain_merge_left[...], ones).reshape(64, 16, 128)
    by_coarse = dot_tn(r.gain_coarse_left[...], ones).reshape(64, 8, 128)
    by_coarse = jnp.concatenate([by_coarse, by_coarse], axis=1)
    gains = jnp.where(left_lane, by_merge, by_coarse).astype(HALF)
    r.share0[:, :, :, :, :, 1024:] = gains.reshape(4, 2, 4, 2, 16, 128)

    def merge_rows(n, carry):
        left = r.merged_left[:, pl.ds(pl.multiple_of(n * 256, 256), 256)]
        grad = dot_tn(left, r.inner_right[...])
        r.share0[n, :, :, :, :, :1024] = grad.astype(HALF).reshape(2, 4, 2, 16, 1024)
        return carry

    lax.fori_loop(0, 4, merge_rows, 0)
    if summing:
        start_first(0)

    needs = ((LON, LAT, DIAG), (LAT,), (LON,), ())
    waited = set()
    end_arrive = []
    gain_row = jnp.zeros((1, 512), FULL)
    for w in (3, 2, 1, 0):
        for slot in needs[w]:
            if slot not in waited:
                back_arrive[slot].wait()
                waited.add(slot)
        rows = slice(CELLS * w, CELLS * w + CELLS)
        grad = gathered("back", rows, r.patches_grad[...], fine_sizes, needs[w]).astype(HALF)
        r.fine_right[rows, :] = grad
        handed_fine.append(hand_right("fine_right", CELLS * w, CELLS))
        attended_grad = dot_nt(grad, r.proj_f[...]).astype(HALF)
        qkv = r.qkv
        mask = pair_mask(edge if w >= 2 else 0)
        for p in range(4):
            at = 128 * p
            queries = two_heads(qkv[rows, at : at + 128])
            keys, worth = qkv[rows, 512 + at : 640 + at], qkv[rows, 1024 + at : 1152 + at]
            weights = pair_weights(queries, keys, mask)
            upstream = two_heads(attended_grad[:, at : at + 128])
            grads = pair_back(weights, queries, keys, worth, upstream)
            for n in range(3):
                r.triple_right[rows, 512 * n + at : 512 * n + at + 128] = grads[n]
        handed_fine.append(hand_right("triple_right", CELLS * w, CELLS))
        normed_grad = dot_nt(r.triple_right[rows, :], r.qkv_f[...]).astype(HALF).astype(FULL)
        unit, scale = norm_parts(r.rolled[rows, :].astype(FULL))
        gain_row = gain_row + jnp.sum(normed_grad * unit, axis=0, keepdims=True)
        back = norm_back(normed_grad, unit, scale, r.gain_f[...])
        r.tokens_back[rows, :] = (grad.astype(FULL) + back).astype(HALF)
        for slot in {2: (LAT,), 1: (DIAG, LON)}.get(w, ()):
            if not end_arrive:
                loads["end_pack"].wait()
            pack_piece("end", r.tokens_back[...], slot, fine_sizes[slot])
            end_arrive.append(send_piece("end", slot, fine_sizes[slot], -1))
    split(in_two(gain_row), keep4, give4, "gain_fine", slice(0, 16))
    handed_fine.append(hand_left("gain_fine"))
    for copy in handed_fine:
        copy.wait()

    def fine_rows(n, carry):
        cols = pl.ds(pl.multiple_of(n * 128, 128), 128)

        def store(p, at, pieces):
            width = pieces[0].shape[1]
            for side, value in enumerate(four_stacked(pieces)):
                of(r, "share", p)[pl.ds(n * 2, 2), :, :, side, :, at : at + width] = value.reshape(
                    2, 2, 4, 16, width
                )

        grad = dot_tn(r.normal_left[:, cols], r.triple_right[...])
        store(3, 0, [grad[:, 384 * m : 384 * m + 256] for m in range(4)])
        store(4, 0, [grad[:, 384 * m + 256 : 384 * m + 384] for m in range(4)])
        grad = dot_tn(r.attended_left[:, cols], r.fine_right[...])
        store(4, 128, [grad[:, 128 * m : 128 * m + 128] for m in range(4)])
        store(5, 0, [dot_tn(r.gain_fine_left[:, cols], ones)] * 4)
        return carry

    lax.fori_loop(0, 2, fine_rows, 0)
    if summing:
        for p in (3, 4, 5):
            start_first(p)
        for p in (1, 2, 0):
            start_second(p)
    for copy in out_arrive:
        copy.wait()
    for name in ("end_own", "end_halo"):
        loads[name].wait()
    r.coarse_tokens[...] = gathered(
        "out", every, r.coarse_out[...], coarse_sizes, (LON, LAT, DIAG)
    ).astype(HALF)
    if summing:
        for p in (3, 4, 5):
            start_second(p)
    for copy in end_arrive:
        copy.wait()
    r.tokens_grad[...] = gathered(
        "end", every, r.tokens_back[...], fine_sizes, (LON, LAT, DIAG)
    ).astype(HALF)
    if summing:
        for p in (1, 2, 0, 3, 4, 5):
            start_third(p)
        for p in (1, 2, 0, 3, 4, 5):
            finish(p)
    else:
        for p in range(6):
            of(r, "sum", p)[...] = of(r, "share", p)[...].reshape(64, 16, WIDTHS[p])


LOADED = tuple(
    dict(
        in_pack=0,
        in_own=0,
        in_halo=0,
        qkv_f=0,
        proj_f=0,
        mid_pack=0,
        proj_c=0,
        mid_own=0,
        mid_halo=0,
        merge_w=0,
        qkv_c=0,
        back_pack=0,
        back_own=0,
        back_halo=0,
        end_pack=0,
        end_own=0,
        end_halo=0,
    )
)


def whole(values, summing):
    inputs, scratch, outputs = [], [], []

    def matrices(kind, rows, cols, source, target, sign):
        pack, own, halo, _ = roll_matrices(rows, cols, source, target, sign)
        return {
            kind + "_pack": jnp.asarray(pack, HALF),
            kind + "_own": jnp.asarray(own, HALF),
            kind + "_halo": jnp.asarray(halo, HALF),
        }

    values = dict(values)
    values.update(matrices("in", 12, 24, "natural", "window", 1))
    values.update(matrices("cot", 6, 12, "natural", "window", 1))
    values.update(matrices("mid", 12, 24, "window", "patch", 1))
    values.update(matrices("back", 12, 24, "patch", "window", -1))
    values.update(matrices("end", 12, 24, "window", "natural", -1))
    values.update(matrices("out", 6, 12, "window", "natural", -1))
    specs, operands = [], []
    for name, value in values.items():
        loaded = name in LOADED
        inputs.append(name + "_any" if loaded else name)
        specs.append(ANYWHERE if loaded else VMEM)
        operands.append(value)
    half = {name: values[name].shape for name in LOADED[:11]}
    for kind, width in (("in", 512), ("cot", 1024), ("mid", 512), ("back", 512), ("end", 512), ("out", 1024)):
        half[kind + "_packed"] = half[kind + "_landed"] = (PACKED, width)
    lefts = dict(
        normal=(576, 256),
        attended=(576, 256),
        merged=(CELLS, 1024),
        normed=(CELLS, 512),
        coarse=(CELLS, 512),
        gain_coarse=(16, 512),
        gain_merge=(16, 1024),
        gain_fine=(16, 256),
    )
    for name, (count, width) in lefts.items():
        half[name + "_left"] = (2 * count, width)
        half[name + "_give"] = (count, width)
    half.update(
        rolled=(576, 512),
        qkv=(576, 1536),
        attended=(576, 512),
        fine_out=(576, 512),
        tokens_back=(576, 512),
        cot_right=(2 * CELLS, 1024),
        cot_attended=(CELLS, 1024),
        qkv_coarse=(CELLS, 3072),
        coarse_attended=(CELLS, 1024),
        coarse_out=(CELLS, 1024),
        qkv_right=(2 * CELLS, 3072),
        inner_right=(2 * CELLS, 1024),
        fine_right=(1152, 512),
        triple_right=(1152, 1536),
    )
    for p, width in enumerate(WIDTHS):
        half["share" + str(p)] = (4, 2, 4, 2, 16, width)
        if summing:
            first, second = LEADS[p % 3]
            half["landed0_" + str(p)] = (3,) + first + (16, width)
            half["landed1_" + str(p)] = (3,) + second + (16, width)
            half["landed2_" + str(p)] = (3, 16, width)
            half["summed1_" + str(p)] = second + (16, width)
    memory = {name: pltpu.VMEM(shape, HALF) for name, shape in half.items()}
    memory["unit_merge"] = pltpu.VMEM((CELLS, 2048), FULL)
    memory["unit_coarse"] = pltpu.VMEM((CELLS, 1024), FULL)
    memory["send_sem"] = pltpu.SemaphoreType.DMA((100,))
    memory["recv_sem"] = pltpu.SemaphoreType.DMA((100,))
    memory["load_sem"] = pltpu.SemaphoreType.DMA((len(LOADED),))
    outputs = {
        "coarse_tokens": jax.ShapeDtypeStruct((CELLS, 1024), HALF),
        "tokens_grad": jax.ShapeDtypeStruct((576, 512), HALF),
    }
    for p, width in enumerate(WIDTHS):
        outputs["sum" + str(p)] = (
            jax.ShapeDtypeStruct((16, width), FULL)
            if summing
            else jax.ShapeDtypeStruct((64, 16, width), HALF)
        )
    names = tuple(inputs) + tuple(outputs) + tuple(memory)
    results = pl.pallas_call(
        functools.partial(whole_kernel, names, summing),
        out_shape=list(outputs.values()),
        in_specs=specs,
        out_specs=[VMEM] * len(outputs),
        scratch_shapes=list(memory.values()),
        compiler_params=pltpu.CompilerParams(
            collective_id=1, has_side_effects=True, vmem_limit_bytes=LIMIT
        ),
    )(*operands)
    return dict(zip(outputs, results))


def prepared(
    tokens,
    cotangent,
    gain_fine,
    qkv_fine,
    proj_fine,
    gain_merge,
    merge_weight,
    gain_coarse,
    qkv_coarse,
    proj_coarse,
):
    return dict(
        tokens=tokens.reshape(576, 512),
        cotangent=cotangent.reshape(CELLS, 1024),
        gain_f=gain_fine.reshape(1, 512),
        gain_m=gain_merge.reshape(1, 2048),
        gain_c=gain_coarse.reshape(1, 1024),
        qkv_f=qkv_fine,
        proj_f=proj_fine,
        merge_w=merge_weight,
        qkv_c=qkv_coarse,
        proj_c=proj_coarse,
    )


def last_kernel(*refs):
    coarse, tokens, a, b, c, d, e, f = refs[:8]
    coarse_out, tokens_out, fine_gain, qkv_f, proj_f, merge_gain, merge, coarse_gain, qkv_c, proj_c = refs[8:]
    coarse_out[...] = coarse[...]
    tokens_out[...] = tokens[...]

    def across(column, count):
        row = lax.broadcasted_iota(jnp.int32, (16, 128), 0)
        lane = lax.broadcasted_iota(jnp.int32, (16, 128), 1)
        line = jnp.sum(jnp.where(row == lane, column, 0.0), axis=0, keepdims=True)
        return line[:, :count]

    block = a[:, 1024:]
    merge_gain[...] = across(jnp.broadcast_to(block[:, :1], (16, 128)), 16)
    coarse_gain[...] = across(jnp.broadcast_to(block[:, HD : HD + 1], (16, 128)), 8)
    fine_gain[...] = across(f[...], 4)
    merge[...] = a[:, :1024]
    for n in range(2):
        rows = slice(8 * n, 8 * n + 8)
        qkv_c[:, 1536 * n : 1536 * n + 1024] = b[rows, :]
        qkv_c[:, 1536 * n + 1024 : 1536 * n + 1536] = c[rows, :512]
        proj_c[:, 512 * n : 512 * n + 512] = c[rows, 512:]
    for n in range(4):
        rows = slice(4 * n, 4 * n + 4)
        qkv_f[:, 384 * n : 384 * n + 256] = d[rows, :]
        qkv_f[:, 384 * n + 256 : 384 * n + 384] = e[rows, :128]
        proj_f[:, 128 * n : 128 * n + 128] = e[rows, 128:]


def last(found):
    shapes = [jax.ShapeDtypeStruct((CELLS, 1024), HALF), jax.ShapeDtypeStruct((576, 512), HALF)]
    shapes += [
        jax.ShapeDtypeStruct(shape, FULL)
        for shape in (
            (1, 4),
            (4, 1536),
            (4, 512),
            (1, 16),
            (16, 1024),
            (1, 8),
            (8, 3072),
            (8, 1024),
        )
    ]
    outs = pl.pallas_call(
        last_kernel, out_shape=shapes, in_specs=[VMEM] * 8, out_specs=[VMEM] * 10
    )(*found)
    outs = list(outs)
    outs[0] = outs[0].reshape(2, 6, 12, 1024)
    outs[1] = outs[1].reshape(2, 12, 24, 512)
    for n in (2, 5, 7):
        outs[n] = outs[n].reshape(-1)
    return tuple(outs)


def local(*args):
    found = whole(prepared(*args), True)
    return last(tuple(found.values()))


def solution(mesh):
    grid = P(None, "lat", "lon", None)
    vector, matrix = P(("lat", "lon")), P(("lat", "lon"), None)
    return jax.shard_map(
        local,
        mesh=mesh,
        in_specs=(grid, grid) + (P(),) * 8,
        out_specs=(grid, grid, vector, matrix, matrix, vector, matrix, vector, matrix, matrix),
        check_vma=False,
    )
```

```python
import functools
from types import SimpleNamespace

import jax
import jax.numpy as jnp
import numpy as np
from jax import lax
from jax.experimental import pallas as pl
from jax.experimental.pallas import tpu as pltpu
from jax.sharding import PartitionSpec as P

MESH = pl.DeviceIdType.MESH
HALF = jnp.bfloat16
FULL = jnp.float32
HD = 64
WH = 6
WW = 12
CELLS = 144
EPSILON = 1e-05
MASKED = -1e30
PIECES = (0, 128, 256)
PACKED = 304
LIMIT = 62 * 1024 * 1024
VMEM = pl.BlockSpec(memory_space=pltpu.VMEM)
SMEM = pl.BlockSpec(memory_space=pltpu.SMEM)
ANYWHERE = pl.BlockSpec(memory_space=pl.ANY)


def dot(left, right):
    return jnp.dot(left, right, preferred_element_type=FULL)


def dot_nt(left, right):
    return lax.dot_general(left, right, (((1,), (1,)), ((), ())), preferred_element_type=FULL)


def dot_tn(left, right):
    return lax.dot_general(left, right, (((0,), (0,)), ((), ())), preferred_element_type=FULL)


def natural_order(rows, cols):
    return lambda level, i, j: (level * rows + i) * cols + j


def level_last_order(rows, cols):
    return lambda level, i, j: (i * cols + j) * 2 + level


def window_order(rows, cols):
    def place(level, i, j):
        window = i // WH * (cols // WW) + j // WW
        return window * CELLS + ((i % WH // 3 * 2 + level) * 3 + i % 3) * WW + j % WW

    return place


def patch_order(rows, cols):
    coarse = window_order(rows // 2, cols // 2)

    def place(level, i, j):
        return (j % 2 * 2 + i % 2) * CELLS + coarse(level, i // 2, j // 2)

    return place


@functools.lru_cache(maxsize=None)
def roll_matrices(rows, cols, source, target, sign):
    orders = {"last": level_last_order, "natural": natural_order, "window": window_order, "patch": patch_order}
    from_place, to_place = orders[source](rows, cols), orders[target](rows, cols)
    count = 2 * rows * cols
    pieces = ([], [], [])
    own = np.zeros((count, count), np.float32)
    for level in range(2):
        for i in range(rows):
            for j in range(cols):
                far_i, far_j = i + 3 * sign, j + 6 * sign
                across = (far_i // rows != 0, far_j // cols != 0)
                here = from_place(level, far_i % rows, far_j % cols)
                there = to_place(level, i, j)
                if across == (False, False):
                    own[there, here] = 1
                else:
                    slot = {(False, True): 0, (True, False): 1, (True, True): 2}[across]
                    pieces[slot].append((there, here))
    sizes = tuple((len(piece) + 15) // 16 * 16 for piece in pieces)
    pack = np.zeros((PACKED, count), np.float32)
    halo = np.zeros((count, PACKED), np.float32)
    for slot, piece in enumerate(pieces):
        for k, (there, here) in enumerate(piece):
            pack[PIECES[slot] + k, here] = 1
            halo[there, PIECES[slot] + k] = 1
    return pack, own, halo, sizes


def norm_parts(values):
    centre = jnp.mean(values, axis=-1, keepdims=True)
    offset = values - centre
    spread = jnp.mean(offset * offset, axis=-1, keepdims=True)
    scale = lax.rsqrt(spread + EPSILON)
    return offset * scale, scale


def norm_back(grad, normal, scale, gain):
    inner = grad * gain
    mean = jnp.mean(inner, axis=-1, keepdims=True)
    along = jnp.mean(inner * normal, axis=-1, keepdims=True)
    return (inner - mean - normal * along) * scale


def two_heads(pair):
    first = lax.broadcasted_iota(jnp.int32, pair.shape, 1) < HD
    zero = jnp.zeros_like(pair)
    return jnp.concatenate([jnp.where(first, pair, zero), jnp.where(first, zero, pair)], axis=0)


def one_pair(stack):
    half = stack.shape[0] // 2
    first = lax.broadcasted_iota(jnp.int32, (half, 2 * HD), 1) < HD
    return jnp.where(first, stack[:half], stack[half:])


def pair_mask(edge):
    shape = (CELLS, 2 * CELLS)
    key = lax.broadcasted_iota(jnp.int32, shape, 0)
    query = lax.broadcasted_iota(jnp.int32, shape, 1)
    query = jnp.where(query >= CELLS, query - CELLS, query)
    apart = (key < CELLS // 2) != (query < CELLS // 2)
    return jnp.where(apart, edge, 0) > 0


def pair_weights(queries, keys, mask):
    scores = dot_nt(keys, queries * 0.125)
    scores = jnp.where(mask, MASKED, scores)
    powers = jnp.exp(scores - jnp.max(scores, axis=0, keepdims=True))
    return powers * (1.0 / jnp.sum(powers, axis=0, keepdims=True))


def pair_forward(rounded, values):
    return one_pair(dot_tn(rounded, values)).astype(HALF)


def pair_back(weights, rounded, queries, keys, values, upstream):
    weight_grad = dot_nt(values, upstream)
    inner = jnp.sum(weights * weight_grad, axis=0, keepdims=True)
    score_grad = (weights * (weight_grad - inner) * 0.125).astype(HALF)
    query_grad = one_pair(dot_tn(score_grad, keys)).astype(HALF)
    key_grad = dot(score_grad, queries).astype(HALF)
    value_grad = dot(rounded, upstream).astype(HALF)
    return query_grad, key_grad, value_grad


def four_stacked(pieces):
    rows, width = pieces[0].shape
    shaped = [piece.reshape(rows // 8, 8, width) for piece in pieces]
    upper = lax.broadcasted_iota(jnp.int32, shaped[0].shape, 1) < 4
    turned = [pltpu.roll(piece, 4, 1) for piece in shaped]
    even = [jnp.where(upper, shaped[n], turned[n + 1]) for n in (0, 2)]
    odd = [jnp.where(upper, turned[n], shaped[n + 1]) for n in (0, 2)]
    return [jnp.concatenate(pair, axis=1).astype(HALF) for pair in (even, odd)]


ORDERS = (("x", "y", "z"), ("y", "z", "x"), ("z", "x", "y"))
LEADS = (((4, 2, 2), (2, 2)), ((2, 4, 2), (4,)), ((4, 4), (4,)))
WIDTHS = (1152, 1024, 1024, 256, 256, 128)
LON, LAT, DIAG = 0, 1, 2
STEPS = ((0, 1), (1, 0), (1, 1))


def device_at(place, core):
    lat = place["y"] * 2 + place["z"] // 2
    lon = place["x"] * 4 + place["z"] % 2 * 2 + core
    return (lat, lon)


def along(place, axis, steps):
    moved = dict(place)
    moved[axis] = lax.rem(place[axis] + steps, 4)
    return moved


def first_cut(kind, ref, index):
    if kind == 0:
        return ref.at[:, :, index]
    if kind == 1:
        return ref.at[index]
    return ref.at[:, index // 2, :, index % 2]


def second_cut(kind, ref, index):
    if kind == 0:
        return ref.at[index]
    if kind == 1:
        return ref.at[index // 2, :, index % 2]
    return ref.at[:, index]


def third_cut(kind, ref, index):
    if kind == 0:
        return ref.at[index // 2, index % 2]
    return ref.at[index]


def spots(lead, i):
    found = []
    for size in reversed(lead):
        found.insert(0, i % size)
        i = i // size
    return tuple(found)


def added(base, arrivals):
    total = base.astype(FULL)
    for arrival in arrivals:
        total = total + arrival.astype(FULL)
    return total


def of(r, name, p):
    return getattr(r, name + str(p))


def owner_pick(rows_each, core):
    shift = rows_each.bit_length() - 1
    feature = lax.broadcasted_iota(jnp.int32, (256, 128), 0)
    place = lax.broadcasted_iota(jnp.int32, (256, 128), 1)
    wanted = ((place >> shift) << (shift + 1)) + (place & (rows_each - 1)) + core * rows_each
    return jnp.where(feature == wanted, 1.0, 0.0).astype(HALF)


def in_two(row):
    high = row.astype(HALF)
    low = (row - high.astype(FULL)).astype(HALF)
    place = lax.broadcasted_iota(jnp.int32, (16, row.shape[1]), 0)
    wide_high = jnp.broadcast_to(high.astype(FULL), place.shape)
    wide_low = jnp.broadcast_to(low.astype(FULL), place.shape)
    return jnp.where(place == 0, wide_high, jnp.where(place == 1, wide_low, 0.0)).astype(HALF)


def whole_kernel(names, summing, *refs):
    r = SimpleNamespace(**dict(zip(names, refs)))
    lat, lon = lax.axis_index("lat"), lax.axis_index("lon")
    lats, lons = lax.axis_size("lat"), lax.axis_size("lon")
    core = lon % 2
    place = {"y": lat // 2, "x": lon // 4, "z": lat % 2 * 2 + lon // 2 % 2}
    sibling = (lat, lon + 1 - 2 * core)
    edge = jnp.where(lat == lats - 1, 1, 0)
    used = [0]

    def remote(source, target, device):
        slot = used[0]
        used[0] += 1
        copy = pltpu.make_async_remote_copy(
            src_ref=source,
            dst_ref=target,
            send_sem=r.send_sem.at[slot],
            recv_sem=r.recv_sem.at[slot],
            device_id=device,
            device_id_type=MESH,
        )
        copy.start()
        return copy

    def neighbour(step, way):
        return (
            lax.rem(lat + lats + way * step[0], lats),
            lax.rem(lon + lons + way * step[1], lons),
        )

    loads = {}

    def load(name):
        slot = LOADED.index(name)
        loads[name] = pltpu.make_async_copy(getattr(r, name + "_any"), getattr(r, name), r.load_sem.at[slot])
        loads[name].start()

    for kind, held in (("back", "in"), ("end", "mid")):
        for matrix in ("_pack", "_own", "_halo"):
            setattr(r, kind + matrix, getattr(r, held + matrix))
    r.patches_grad = r.fine_out
    for name in LOADED[:6]:
        load(name)

    barrier = pltpu.get_barrier_semaphore()
    partners = [neighbour(step, way) for step in STEPS for way in (1, -1)] + [sibling]
    if summing:
        partners += [
            device_at(along(place, axis, k), core) for axis in ("x", "y", "z") for k in (1, 2, 3)
        ]
    for partner in partners:
        pl.semaphore_signal(barrier, inc=1, device_id=partner, device_id_type=MESH)

    def pack_piece(kind, value, slot, size):
        rows = slice(PIECES[slot], PIECES[slot] + size)
        getattr(r, kind + "_packed")[rows, :] = dot(getattr(r, kind + "_pack")[rows, :], value).astype(HALF)

    def send_piece(kind, slot, size, sign):
        rows = pl.ds(PIECES[slot], size)
        return remote(
            getattr(r, kind + "_packed").at[rows],
            getattr(r, kind + "_landed").at[rows],
            neighbour(STEPS[slot], -sign),
        )

    def gathered(kind, rows, value, sizes, needed):
        total = dot(getattr(r, kind + "_own")[rows, :], value)
        for slot in needed:
            piece = slice(PIECES[slot], PIECES[slot] + sizes[slot])
            total = total + dot(getattr(r, kind + "_halo")[rows, piece], getattr(r, kind + "_landed")[piece, :])
        return total

    fine_sizes, coarse_sizes = (112, 112, 48), (48, 48, 48)
    loads["in_pack"].wait()
    for slot in (LAT, DIAG, LON):
        pack_piece("in", r.tokens[...], slot, fine_sizes[slot])
    for slot in (LAT, DIAG, LON):
        pack_piece("cot", r.cotangent[...], slot, coarse_sizes[slot])
    pl.semaphore_wait(barrier, len(partners))
    arrive = {slot: send_piece("in", slot, fine_sizes[slot], 1) for slot in (LAT, DIAG, LON)}
    cot_arrive = [send_piece("cot", slot, coarse_sizes[slot], 1) for slot in (LAT, DIAG, LON)]
    r.fine_out[...] = jnp.zeros_like(r.fine_out)
    r.tokens_back[...] = jnp.zeros_like(r.tokens_back)

    keep4, give4 = owner_pick(4, core), owner_pick(4, 1 - core)
    keep8, give8 = owner_pick(8, core), owner_pick(8, 1 - core)
    keep16, give16 = owner_pick(16, core), owner_pick(16, 1 - core)

    def split(value, keep, give, name, rows):
        for block in range(value.shape[1] // 256):
            part = value[:, 256 * block : 256 * block + 256]
            cols = slice(128 * block, 128 * block + 128)
            getattr(r, name + "_left")[rows, cols] = dot(part, keep).astype(HALF)
            getattr(r, name + "_give")[rows, cols] = dot(part, give).astype(HALF)

    def hand_left(name):
        count = getattr(r, name + "_give").shape[0]
        return remote(getattr(r, name + "_give"), getattr(r, name + "_left").at[pl.ds(count, count)], sibling)

    def hand_right(name, start, size):
        half = getattr(r, name).shape[0] // 2
        held = getattr(r, name)
        return remote(held.at[pl.ds(start, size)], held.at[pl.ds(half + start, size)], sibling)

    handed_fine, handed_coarse, late = [], [], []

    needs = ((), (LON,), (LAT,), (LON, LAT, DIAG))
    waited = set()
    mid_arrive = []
    for name in LOADED[1:6]:
        loads[name].wait()
    for name in LOADED[6:11]:
        load(name)
    for w in range(4):
        for slot in needs[w]:
            if slot not in waited:
                arrive[slot].wait()
                waited.add(slot)
        rows = slice(CELLS * w, CELLS * w + CELLS)
        values = gathered("in", rows, r.tokens[...], fine_sizes, needs[w])
        r.rolled[rows, :] = values.astype(HALF)
        unit, _ = norm_parts(values)
        normed = (unit * r.gain_f[...]).astype(HALF)
        split(normed, keep4, give4, "normal", rows)
        qkv = r.qkv
        for n in range(3):
            cols = slice(512 * n, 512 * n + 512)
            qkv[rows, cols] = dot(normed, r.qkv_f[:, cols]).astype(HALF)
        mask = pair_mask(edge if w >= 2 else 0)
        for p in range(4):
            at = 128 * p
            queries = two_heads(qkv[rows, at : at + 128])
            weights = pair_weights(queries, qkv[rows, 512 + at : 640 + at], mask)
            rounded = weights.astype(HALF)
            r.kept[4 * w + p] = rounded
            r.attended[rows, at : at + 128] = pair_forward(
                rounded, qkv[rows, 1024 + at : 1152 + at]
            )
        attended = r.attended[rows, :]
        split(attended, keep4, give4, "attended", rows)
        r.fine_out[rows, :] = (values + dot(attended, r.proj_f[...])).astype(HALF)
        for slot in {1: (LAT,), 2: (DIAG, LON)}.get(w, ()):
            pack_piece("mid", r.fine_out[...], slot, fine_sizes[slot])
            mid_arrive.append(send_piece("mid", slot, fine_sizes[slot], 1))
    handed_fine += [hand_left("normal"), hand_left("attended")]
    for name in LOADED[11:14]:
        load(name)

    for copy in cot_arrive:
        copy.wait()
    every = slice(None)
    cot = gathered("cot", every, r.cotangent[...], coarse_sizes, (LON, LAT, DIAG)).astype(HALF)
    own = slice(0, CELLS)
    r.cot_right[own, :] = cot
    handed_coarse.append(hand_right("cot_right", 0, CELLS))
    loads["proj_c"].wait()
    r.cot_attended[...] = dot_nt(cot, r.proj_c[...]).astype(HALF)
    loads["mid_own"].wait()
    loads["mid_halo"].wait()
    for copy in mid_arrive:
        copy.wait()
    values = jnp.concatenate(
        [
            gathered(
                "mid",
                slice(CELLS * g, CELLS * g + CELLS),
                r.fine_out[...],
                fine_sizes,
                (LON, LAT, DIAG),
            )
            for g in range(4)
        ],
        axis=1,
    )
    for name in LOADED[14:]:
        load(name)
    unit, scale_merge = norm_parts(values)
    r.unit_merge[...] = unit
    merged = (unit * r.gain_m[...]).astype(HALF)
    loads["merge_w"].wait()
    coarse_in = dot(merged, r.merge_w[...]).astype(HALF).astype(FULL)
    split(merged, keep16, give16, "merged", own)
    merged_handed = hand_left("merged")
    unit, scale_coarse = norm_parts(coarse_in)
    r.unit_coarse[...] = unit
    normed = (unit * r.gain_c[...]).astype(HALF)
    loads["qkv_c"].wait()
    for n in range(3):
        cols = slice(1024 * n, 1024 * (n + 1))
        r.qkv_coarse[:, cols] = dot(normed, r.qkv_c[:, cols]).astype(HALF)
    split(normed, keep8, give8, "normed", own)
    handed_coarse.append(hand_left("normed"))
    qkv = r.qkv_coarse
    mask = pair_mask(edge)
    for p in range(8):
        at = 128 * p
        queries = two_heads(qkv[:, at : at + 128])
        keys, worth = qkv[:, 1024 + at : 1152 + at], qkv[:, 2048 + at : 2176 + at]
        weights = pair_weights(queries, keys, mask)
        rounded = weights.astype(HALF)
        r.coarse_attended[:, at : at + 128] = pair_forward(rounded, worth)
        upstream = two_heads(r.cot_attended[:, at : at + 128])
        grads = pair_back(weights, rounded, queries, keys, worth, upstream)
        for n in range(3):
            r.qkv_right[own, 1024 * n + at : 1024 * n + at + 128] = grads[n]
    handed_coarse.append(hand_right("qkv_right", 0, CELLS))
    attended = r.coarse_attended[...]
    split(attended, keep8, give8, "coarse", own)
    handed_coarse.append(hand_left("coarse"))
    normed_grad = dot_nt(r.qkv_right[own, :], r.qkv_c[...]).astype(HALF).astype(FULL)
    gain_row = jnp.sum(normed_grad * r.unit_coarse[...], axis=0, keepdims=True)
    split(in_two(gain_row), keep8, give8, "gain_coarse", slice(0, 16))
    gains_handed = [hand_left("gain_coarse")]
    coarse_grad = r.cot_right[own, :].astype(FULL) + norm_back(
        normed_grad, r.unit_coarse[...], scale_coarse, r.gain_c[...]
    )
    r.inner_right[own, :] = coarse_grad.astype(HALF)
    inner_handed = hand_right("inner_right", 0, CELLS)
    merged_grad = dot_nt(r.inner_right[own, :], r.merge_w[...]).astype(HALF).astype(FULL)
    gain_row = jnp.sum(merged_grad * r.unit_merge[...], axis=0, keepdims=True)
    split(in_two(gain_row), keep16, give16, "gain_merge", slice(0, 16))
    gains_handed.append(hand_left("gain_merge"))
    back = norm_back(merged_grad, r.unit_merge[...], scale_merge, r.gain_m[...]).astype(HALF)
    for g in range(4):
        r.patches_grad[CELLS * g : CELLS * (g + 1), :] = back[:, 512 * g : 512 * (g + 1)]
    for name in ("back_pack", "back_own", "back_halo"):
        loads[name].wait()
    back_arrive = {}
    for slot in (LAT, DIAG, LON):
        pack_piece("back", r.patches_grad[...], slot, fine_sizes[slot])
        back_arrive[slot] = send_piece("back", slot, fine_sizes[slot], -1)
    r.coarse_out[...] = (coarse_in + dot(attended, r.proj_c[...])).astype(HALF)
    for slot in (LAT, DIAG, LON):
        pack_piece("out", r.coarse_out[...], slot, coarse_sizes[slot])
    out_arrive = [send_piece("out", slot, coarse_sizes[slot], -1) for slot in (LAT, DIAG, LON)]

    sums = {}

    def across(axis):
        mine = place[axis]
        near, far = mine + 1 - 2 * (mine % 2), 3 - mine
        return mine, ((near, far), (far, near))

    def there(axis, index):
        return device_at({**place, axis: index}, core)

    def stage_of(p, stage):
        landed = of(r, ("landed0_", "landed1_")[stage], p)
        lead = LEADS[p % 3][stage]
        size = int(np.prod(lead))
        if stage == 0:
            source = lambda index: first_cut(p % 3, of(r, "share", p), index)
        else:
            source = lambda index: second_cut(p % 3, of(r, "landed0_", p).at[1], index)
        return source, landed, lead, size, ORDERS[p % 3][stage]

    def halves(lead):
        return [pl.ds(h * (lead[0] // 2), lead[0] // 2) for h in range(2)]

    def begin(p, stage):
        source, landed, lead, size, axis = stage_of(p, stage)
        mine, pairs = across(axis)
        sums[p] = {}
        for slot in range(2):
            for h, rows in enumerate(halves(lead)):
                one = pairs[h][0]
                quarter = lax.rem(mine + 2, 4) if slot == 0 else one
                sums[p][h, slot] = remote(
                    source(quarter).at[rows], landed.at[slot, rows], there(axis, one)
                )

    def forward(p, stage):
        source, landed, lead, size, axis = stage_of(p, stage)
        mine, pairs = across(axis)
        for h, rows in enumerate(halves(lead)):
            two = pairs[h][1]
            theirs = source(two)
            sums[p][h, 0].wait()

            def add(i, carry, h=h, theirs=theirs):
                at = spots(lead, i + h * (size // 2))
                landed[(0,) + at] = added(theirs[at], [landed[(0,) + at]]).astype(HALF)
                return carry

            lax.fori_loop(0, size // 2, add, 0)
            sums[p][h, 2] = remote(landed.at[0, rows], landed.at[2, rows], there(axis, two))

    def collect(p, stage):
        source, landed, lead, size, axis = stage_of(p, stage)
        mine = source(place[axis])
        for h in range(2):
            sums[p][h, 1].wait()
            sums[p][h, 2].wait()

        def add(i, carry):
            at = spots(lead, i)
            total = added(mine[at], [landed[(1,) + at], landed[(2,) + at]])
            landed[(1,) + at] = total.astype(HALF)
            return carry

        lax.fori_loop(0, size, add, 0)

    def start_second(p):
        source, landed, lead, size, axis = stage_of(p, 1)
        sums[p] = []
        for k in (2, 1, 3):
            moved = along(place, axis, k)
            sums[p].append(
                remote(source(moved[axis]), landed.at[k - 1], device_at(moved, core))
            )

    def collect_second(p):
        source, landed, lead, size, axis = stage_of(p, 1)
        for copy in sums[p]:
            copy.wait()
        total = added(source(place[axis])[...], [landed[k] for k in range(3)])
        landed[1] = total.astype(HALF)

    def start_third(p):
        axis = ORDERS[p % 3][2]
        sums[p] = []
        for k in (2, 1, 3):
            moved = along(place, axis, k)
            sums[p].append(
                remote(
                    third_cut(p % 3, of(r, "landed1_", p).at[1], moved[axis]),
                    of(r, "landed2_", p).at[k - 1],
                    device_at(moved, core),
                )
            )

    def finish(p):
        for copy in sums[p]:
            copy.wait()
        mine = third_cut(p % 3, of(r, "landed1_", p).at[1], place[ORDERS[p % 3][2]])
        total = added(mine[...], [of(r, "landed2_", p)[k] for k in range(3)])
        of(r, "sum", p)[...] = total

    for copy in handed_coarse:
        copy.wait()

    def paired(grad, lead):
        width = grad.shape[1] // 2
        rows = grad.shape[0] // 8
        pieces = [grad[:, :width].reshape(rows, 8, width), grad[:, width:].reshape(rows, 8, width)]
        return jnp.concatenate(pieces, axis=1).astype(HALF).reshape(lead + (16, width))

    def qkv_rows(n, carry):
        cols = pl.ds(pl.multiple_of(n * 256, 256), 256)
        left = r.normed_left[:, cols]
        for low, share, at in ((0, 1, 0), (512, 1, 512), (1024, 2, 0)):
            right = jnp.concatenate(
                [
                    r.qkv_right[:, low : low + 512],
                    r.qkv_right[:, low + 1536 : low + 2048],
                ],
                axis=1,
            )
            of(r, "share", share)[pl.ds(n * 2, 2), :, :, :, :, at : at + 512] = paired(
                dot_tn(left, right), (2, 2, 4, 2)
            )
        grad = dot_tn(r.coarse_left[:, cols], r.cot_right[...])
        r.share2[pl.ds(n * 2, 2), :, :, :, :, 512:] = paired(grad, (2, 2, 4, 2))
        return carry

    lax.fori_loop(0, 2, qkv_rows, 0)
    if summing:
        begin(1, 0)
        begin(2, 0)
    for copy in gains_handed + [merged_handed, inner_handed]:
        copy.wait()
    ones = jnp.ones((32, 128), HALF)
    left_lane = lax.broadcasted_iota(jnp.int32, (64, 16, 128), 2) < HD
    by_merge = dot_tn(r.gain_merge_left[...], ones).reshape(64, 16, 128)
    by_coarse = dot_tn(r.gain_coarse_left[...], ones).reshape(64, 8, 128)
    by_coarse = jnp.concatenate([by_coarse, by_coarse], axis=1)
    gains = jnp.where(left_lane, by_merge, by_coarse).astype(HALF)
    r.share0[:, :, :, :, :, 1024:] = gains.reshape(4, 2, 4, 2, 16, 128)

    def merge_rows(n, carry):
        left = r.merged_left[:, pl.ds(pl.multiple_of(n * 256, 256), 256)]
        grad = dot_tn(left, r.inner_right[...])
        r.share0[n, :, :, :, :, :1024] = grad.astype(HALF).reshape(2, 4, 2, 16, 1024)
        return carry

    lax.fori_loop(0, 4, merge_rows, 0)
    if summing:
        begin(0, 0)

    needs = ((LON, LAT, DIAG), (LAT,), (LON,), ())
    waited = set()
    end_arrive = []
    gain_row = jnp.zeros((1, 512), FULL)
    for w in (3, 2, 1, 0):
        for slot in needs[w]:
            if slot not in waited:
                back_arrive[slot].wait()
                waited.add(slot)
        rows = slice(CELLS * w, CELLS * w + CELLS)
        grad = gathered("back", rows, r.patches_grad[...], fine_sizes, needs[w]).astype(HALF)
        r.fine_right[rows, :] = grad
        handed_fine.append(hand_right("fine_right", CELLS * w, CELLS))
        attended_grad = dot_nt(grad, r.proj_f[...]).astype(HALF)
        qkv = r.qkv
        for p in range(4):
            at = 128 * p
            queries = two_heads(qkv[rows, at : at + 128])
            keys, worth = qkv[rows, 512 + at : 640 + at], qkv[rows, 1024 + at : 1152 + at]
            rounded = r.kept[4 * w + p]
            upstream = two_heads(attended_grad[:, at : at + 128])
            grads = pair_back(rounded.astype(FULL), rounded, queries, keys, worth, upstream)
            for n in range(3):
                r.triple_right[rows, 512 * n + at : 512 * n + at + 128] = grads[n]
        handed_fine.append(hand_right("triple_right", CELLS * w, CELLS))
        normed_grad = dot_nt(r.triple_right[rows, :], r.qkv_f[...]).astype(HALF).astype(FULL)
        unit, scale = norm_parts(r.rolled[rows, :].astype(FULL))
        gain_row = gain_row + jnp.sum(normed_grad * unit, axis=0, keepdims=True)
        back = norm_back(normed_grad, unit, scale, r.gain_f[...])
        r.tokens_back[rows, :] = (grad.astype(FULL) + back).astype(HALF)
        for slot in {2: (LAT,), 1: (DIAG, LON)}.get(w, ()):
            if not end_arrive:
                loads["end_pack"].wait()
            pack_piece("end", r.tokens_back[...], slot, fine_sizes[slot])
            end_arrive.append(send_piece("end", slot, fine_sizes[slot], -1))
        if summing:
            for p in {3: (1, 2), 2: (0,)}.get(w, ()):
                forward(p, 0)
    split(in_two(gain_row), keep4, give4, "gain_fine", slice(0, 16))
    handed_fine.append(hand_left("gain_fine"))
    if summing:
        for p in (1, 2):
            collect(p, 0)
            begin(p, 1)
    for copy in handed_fine:
        copy.wait()

    def fine_rows(n, carry):
        cols = pl.ds(pl.multiple_of(n * 128, 128), 128)

        def store(p, at, pieces):
            width = pieces[0].shape[1]
            for side, value in enumerate(four_stacked(pieces)):
                of(r, "share", p)[pl.ds(n * 2, 2), :, :, side, :, at : at + width] = value.reshape(
                    2, 2, 4, 16, width
                )

        grad = dot_tn(r.normal_left[:, cols], r.triple_right[...])
        store(3, 0, [grad[:, 384 * m : 384 * m + 256] for m in range(4)])
        store(4, 0, [grad[:, 384 * m + 256 : 384 * m + 384] for m in range(4)])
        grad = dot_tn(r.attended_left[:, cols], r.fine_right[...])
        store(4, 128, [grad[:, 128 * m : 128 * m + 128] for m in range(4)])
        store(5, 0, [dot_tn(r.gain_fine_left[:, cols], ones)] * 4)
        return carry

    lax.fori_loop(0, 2, fine_rows, 0)
    if summing:
        for p in (3, 4, 5):
            begin(p, 0)
        collect(0, 0)
        begin(0, 1)
        forward(1, 1)
        forward(2, 1)
    for copy in out_arrive:
        copy.wait()
    r.coarse_tokens[...] = gathered(
        "out", every, r.coarse_out[...], coarse_sizes, (LON, LAT, DIAG)
    ).astype(HALF)
    if summing:
        for p in (3, 4, 5):
            forward(p, 0)
        forward(0, 1)
    for name in ("end_own", "end_halo"):
        loads[name].wait()
    for copy in end_arrive:
        copy.wait()
    r.tokens_grad[...] = gathered(
        "end", every, r.tokens_back[...], fine_sizes, (LON, LAT, DIAG)
    ).astype(HALF)
    if summing:
        for p in (1, 2):
            collect(p, 1)
            start_third(p)
        for p in (3, 4, 5):
            collect(p, 0)
            start_second(p)
        collect(0, 1)
        start_third(0)
        for p in (3, 4, 5):
            collect_second(p)
            start_third(p)
        for p in (1, 2, 0, 3, 4, 5):
            finish(p)
    else:
        for p in range(6):
            of(r, "sum", p)[...] = of(r, "share", p)[...].reshape(64, 16, WIDTHS[p])


LOADED = tuple(
    dict(
        in_pack=0,
        in_own=0,
        in_halo=0,
        qkv_f=0,
        proj_f=0,
        mid_pack=0,
        proj_c=0,
        mid_own=0,
        mid_halo=0,
        merge_w=0,
        qkv_c=0,
        back_pack=0,
        back_own=0,
        back_halo=0,
        end_pack=0,
        end_own=0,
        end_halo=0,
    )
)


def whole(values, summing):
    inputs, scratch, outputs = [], [], []

    def matrices(kind, rows, cols, source, target, sign):
        pack, own, halo, _ = roll_matrices(rows, cols, source, target, sign)
        return {
            kind + "_pack": jnp.asarray(pack, HALF),
            kind + "_own": jnp.asarray(own, HALF),
            kind + "_halo": jnp.asarray(halo, HALF),
        }

    values = dict(values)
    values.update(matrices("in", 12, 24, "natural", "window", 1))
    values.update(matrices("cot", 6, 12, "last", "window", 1))
    values.update(matrices("mid", 12, 24, "window", "patch", 1))
    values.update(matrices("back", 12, 24, "patch", "window", -1))
    values.update(matrices("end", 12, 24, "window", "natural", -1))
    values.update(matrices("out", 6, 12, "window", "last", -1))
    specs, operands = [], []
    for name, value in values.items():
        loaded = name in LOADED
        inputs.append(name + "_any" if loaded else name)
        specs.append(ANYWHERE if loaded else VMEM)
        operands.append(value)
    half = {name: values[name].shape for name in LOADED[:11]}
    for kind, width in (("in", 512), ("cot", 1024), ("mid", 512), ("back", 512), ("end", 512), ("out", 1024)):
        half[kind + "_packed"] = half[kind + "_landed"] = (PACKED, width)
    lefts = dict(
        normal=(576, 256),
        attended=(576, 256),
        merged=(CELLS, 1024),
        normed=(CELLS, 512),
        coarse=(CELLS, 512),
        gain_coarse=(16, 512),
        gain_merge=(16, 1024),
        gain_fine=(16, 256),
    )
    for name, (count, width) in lefts.items():
        half[name + "_left"] = (2 * count, width)
        half[name + "_give"] = (count, width)
    half.update(
        kept=(16, CELLS, 2 * CELLS),
        rolled=(576, 512),
        qkv=(576, 1536),
        attended=(576, 512),
        fine_out=(576, 512),
        tokens_back=(576, 512),
        cot_right=(2 * CELLS, 1024),
        cot_attended=(CELLS, 1024),
        qkv_coarse=(CELLS, 3072),
        coarse_attended=(CELLS, 1024),
        coarse_out=(CELLS, 1024),
        qkv_right=(2 * CELLS, 3072),
        inner_right=(2 * CELLS, 1024),
        fine_right=(1152, 512),
        triple_right=(1152, 1536),
    )
    for p, width in enumerate(WIDTHS):
        half["share" + str(p)] = (4, 2, 4, 2, 16, width)
        if summing:
            first, second = LEADS[p % 3]
            half["landed0_" + str(p)] = (3,) + first + (16, width)
            half["landed1_" + str(p)] = (3,) + second + (16, width)
            half["landed2_" + str(p)] = (3, 16, width)
    memory = {name: pltpu.VMEM(shape, HALF) for name, shape in half.items()}
    memory["unit_merge"] = pltpu.VMEM((CELLS, 2048), FULL)
    memory["unit_coarse"] = pltpu.VMEM((CELLS, 1024), FULL)
    memory["send_sem"] = pltpu.SemaphoreType.DMA((150,))
    memory["recv_sem"] = pltpu.SemaphoreType.DMA((150,))
    memory["load_sem"] = pltpu.SemaphoreType.DMA((len(LOADED),))
    outputs = {
        "coarse_tokens": jax.ShapeDtypeStruct((CELLS, 1024), HALF),
        "tokens_grad": jax.ShapeDtypeStruct((576, 512), HALF),
    }
    for p, width in enumerate(WIDTHS):
        outputs["sum" + str(p)] = (
            jax.ShapeDtypeStruct((16, width), FULL)
            if summing
            else jax.ShapeDtypeStruct((64, 16, width), HALF)
        )
    names = tuple(inputs) + tuple(outputs) + tuple(memory)
    results = pl.pallas_call(
        functools.partial(whole_kernel, names, summing),
        out_shape=list(outputs.values()),
        in_specs=specs,
        out_specs=[VMEM] * len(outputs),
        scratch_shapes=list(memory.values()),
        compiler_params=pltpu.CompilerParams(
            collective_id=1, has_side_effects=True, vmem_limit_bytes=LIMIT
        ),
    )(*operands)
    return dict(zip(outputs, results))


def prepared(
    tokens,
    cotangent,
    gain_fine,
    qkv_fine,
    proj_fine,
    gain_merge,
    merge_weight,
    gain_coarse,
    qkv_coarse,
    proj_coarse,
):
    return dict(
        tokens=tokens.reshape(576, 512),
        cotangent=cotangent.transpose(1, 2, 0, 3).reshape(CELLS, 1024),
        gain_f=gain_fine.reshape(1, 512),
        gain_m=gain_merge.reshape(1, 2048),
        gain_c=gain_coarse.reshape(1, 1024),
        qkv_f=qkv_fine,
        proj_f=proj_fine,
        merge_w=merge_weight,
        qkv_c=qkv_coarse,
        proj_c=proj_coarse,
    )


def last_kernel(*refs):
    coarse, tokens, a, b, c, d, e, f = refs[:8]
    coarse_out, tokens_out, fine_gain, qkv_f, proj_f, merge_gain, merge, coarse_gain, qkv_c, proj_c = refs[8:]
    coarse_out[...] = coarse[...]
    tokens_out[...] = tokens[...]

    def across(column, count):
        row = lax.broadcasted_iota(jnp.int32, (16, 128), 0)
        lane = lax.broadcasted_iota(jnp.int32, (16, 128), 1)
        line = jnp.sum(jnp.where(row == lane, column, 0.0), axis=0, keepdims=True)
        return line[:, :count]

    block = a[:, 1024:]
    merge_gain[...] = across(jnp.broadcast_to(block[:, :1], (16, 128)), 16)
    coarse_gain[...] = across(jnp.broadcast_to(block[:, HD : HD + 1], (16, 128)), 8)
    fine_gain[...] = across(f[...], 4)
    merge[...] = a[:, :1024]
    for n in range(2):
        rows = slice(8 * n, 8 * n + 8)
        qkv_c[:, 1536 * n : 1536 * n + 1024] = b[rows, :]
        qkv_c[:, 1536 * n + 1024 : 1536 * n + 1536] = c[rows, :512]
        proj_c[:, 512 * n : 512 * n + 512] = c[rows, 512:]
    for n in range(4):
        rows = slice(4 * n, 4 * n + 4)
        qkv_f[:, 384 * n : 384 * n + 256] = d[rows, :]
        qkv_f[:, 384 * n + 256 : 384 * n + 384] = e[rows, :128]
        proj_f[:, 128 * n : 128 * n + 128] = e[rows, 128:]


def last(found):
    shapes = [jax.ShapeDtypeStruct((CELLS, 1024), HALF), jax.ShapeDtypeStruct((576, 512), HALF)]
    shapes += [
        jax.ShapeDtypeStruct(shape, FULL)
        for shape in (
            (1, 4),
            (4, 1536),
            (4, 512),
            (1, 16),
            (16, 1024),
            (1, 8),
            (8, 3072),
            (8, 1024),
        )
    ]
    outs = pl.pallas_call(
        last_kernel, out_shape=shapes, in_specs=[VMEM] * 8, out_specs=[VMEM] * 10
    )(*found)
    outs = list(outs)
    outs[0] = outs[0].reshape(6, 12, 2, 1024).transpose(2, 0, 1, 3)
    outs[1] = outs[1].reshape(2, 12, 24, 512)
    for n in (2, 5, 7):
        outs[n] = outs[n].reshape(-1)
    return tuple(outs)


def local(*args):
    found = whole(prepared(*args), True)
    return last(tuple(found.values()))


def solution(mesh):
    grid = P(None, "lat", "lon", None)
    vector, matrix = P(("lat", "lon")), P(("lat", "lon"), None)
    return jax.shard_map(
        local,
        mesh=mesh,
        in_specs=(grid, grid) + (P(),) * 8,
        out_specs=(grid, grid, vector, matrix, matrix, vector, matrix, vector, matrix, matrix),
        check_vma=False,
    )
```

```python
import functools
from types import SimpleNamespace

import jax
import jax.numpy as jnp
import numpy as np
from jax import lax
from jax.experimental import pallas as pl
from jax.experimental.pallas import tpu as pltpu
from jax.sharding import PartitionSpec as P

MESH = pl.DeviceIdType.MESH
HALF = jnp.bfloat16
FULL = jnp.float32
HD = 64
WH = 6
WW = 12
CELLS = 144
EPSILON = 1e-05
MASKED = -1e30
PIECES = (0, 128, 256)
PACKED = 304
LIMIT = 62 * 1024 * 1024
VMEM = pl.BlockSpec(memory_space=pltpu.VMEM)
SMEM = pl.BlockSpec(memory_space=pltpu.SMEM)
ANYWHERE = pl.BlockSpec(memory_space=pl.ANY)


def dot(left, right):
    return jnp.dot(left, right, preferred_element_type=FULL)


def dot_nt(left, right):
    return lax.dot_general(left, right, (((1,), (1,)), ((), ())), preferred_element_type=FULL)


def dot_tn(left, right):
    return lax.dot_general(left, right, (((0,), (0,)), ((), ())), preferred_element_type=FULL)


def natural_order(rows, cols):
    return lambda level, i, j: (level * rows + i) * cols + j


def level_last_order(rows, cols):
    return lambda level, i, j: (i * cols + j) * 2 + level


def window_order(rows, cols):
    def place(level, i, j):
        window = i // WH * (cols // WW) + j // WW
        return window * CELLS + ((i % WH // 3 * 2 + level) * 3 + i % 3) * WW + j % WW

    return place


def patch_order(rows, cols):
    coarse = window_order(rows // 2, cols // 2)

    def place(level, i, j):
        return (j % 2 * 2 + i % 2) * CELLS + coarse(level, i // 2, j // 2)

    return place


@functools.lru_cache(maxsize=None)
def roll_matrices(rows, cols, source, target, sign):
    orders = {"last": level_last_order, "natural": natural_order, "window": window_order, "patch": patch_order}
    from_place, to_place = orders[source](rows, cols), orders[target](rows, cols)
    count = 2 * rows * cols
    pieces = ([], [], [])
    own = np.zeros((count, count), np.float32)
    for level in range(2):
        for i in range(rows):
            for j in range(cols):
                far_i, far_j = i + 3 * sign, j + 6 * sign
                across = (far_i // rows != 0, far_j // cols != 0)
                here = from_place(level, far_i % rows, far_j % cols)
                there = to_place(level, i, j)
                if across == (False, False):
                    own[there, here] = 1
                else:
                    slot = {(False, True): 0, (True, False): 1, (True, True): 2}[across]
                    pieces[slot].append((there, here))
    sizes = tuple((len(piece) + 15) // 16 * 16 for piece in pieces)
    pack = np.zeros((PACKED, count), np.float32)
    halo = np.zeros((count, PACKED), np.float32)
    for slot, piece in enumerate(pieces):
        for k, (there, here) in enumerate(piece):
            pack[PIECES[slot] + k, here] = 1
            halo[there, PIECES[slot] + k] = 1
    return pack, own, halo, sizes


def norm_parts(values):
    centre = jnp.mean(values, axis=-1, keepdims=True)
    offset = values - centre
    spread = jnp.mean(offset * offset, axis=-1, keepdims=True)
    scale = lax.rsqrt(spread + EPSILON)
    return offset * scale, scale


def norm_back(grad, normal, scale, gain):
    inner = grad * gain
    mean = jnp.mean(inner, axis=-1, keepdims=True)
    along = jnp.mean(inner * normal, axis=-1, keepdims=True)
    return (inner - mean - normal * along) * scale


def two_heads(pair):
    first = lax.broadcasted_iota(jnp.int32, pair.shape, 1) < HD
    zero = jnp.zeros_like(pair)
    return jnp.concatenate([jnp.where(first, pair, zero), jnp.where(first, zero, pair)], axis=0)


def one_pair(stack):
    half = stack.shape[0] // 2
    first = lax.broadcasted_iota(jnp.int32, (half, 2 * HD), 1) < HD
    return jnp.where(first, stack[:half], stack[half:])


def pair_mask(edge):
    shape = (CELLS, 2 * CELLS)
    key = lax.broadcasted_iota(jnp.int32, shape, 0)
    query = lax.broadcasted_iota(jnp.int32, shape, 1)
    query = jnp.where(query >= CELLS, query - CELLS, query)
    apart = (key < CELLS // 2) != (query < CELLS // 2)
    return jnp.where(apart, edge, 0) > 0


def pair_weights(queries, keys, mask):
    scores = dot_nt(keys, queries * 0.125)
    scores = jnp.where(mask, MASKED, scores)
    powers = jnp.exp(scores - jnp.max(scores, axis=0, keepdims=True))
    return powers * (1.0 / jnp.sum(powers, axis=0, keepdims=True))


def pair_forward(rounded, values):
    return one_pair(dot_tn(rounded, values)).astype(HALF)


def pair_back(weights, rounded, queries, keys, values, upstream):
    weight_grad = dot_nt(values, upstream)
    inner = jnp.sum(weights * weight_grad, axis=0, keepdims=True)
    score_grad = (weights * (weight_grad - inner) * 0.125).astype(HALF)
    query_grad = one_pair(dot_tn(score_grad, keys)).astype(HALF)
    key_grad = dot(score_grad, queries).astype(HALF)
    value_grad = dot(rounded, upstream).astype(HALF)
    return query_grad, key_grad, value_grad


def four_stacked(pieces):
    rows, width = pieces[0].shape
    shaped = [piece.reshape(rows // 8, 8, width) for piece in pieces]
    upper = lax.broadcasted_iota(jnp.int32, shaped[0].shape, 1) < 4
    turned = [pltpu.roll(piece, 4, 1) for piece in shaped]
    even = [jnp.where(upper, shaped[n], turned[n + 1]) for n in (0, 2)]
    odd = [jnp.where(upper, turned[n], shaped[n + 1]) for n in (0, 2)]
    return [jnp.concatenate(pair, axis=1).astype(HALF) for pair in (even, odd)]


ORDERS = (("x", "y", "z"), ("y", "z", "x"), ("z", "x", "y"))
LEADS = (((4, 2, 2), (2, 2)), ((2, 4, 2), (4,)), ((4, 4), (4,)))
WIDTHS = (1152, 1024, 1024, 256, 256, 128)
LON, LAT, DIAG = 0, 1, 2
STEPS = ((0, 1), (1, 0), (1, 1))


def device_at(place, core):
    lat = place["y"] * 2 + place["z"] // 2
    lon = place["x"] * 4 + place["z"] % 2 * 2 + core
    return (lat, lon)


def along(place, axis, steps):
    moved = dict(place)
    moved[axis] = lax.rem(place[axis] + steps, 4)
    return moved


def first_cut(kind, ref, index):
    if kind == 0:
        return ref.at[:, :, index]
    if kind == 1:
        return ref.at[index]
    return ref.at[:, index // 2, :, index % 2]


def second_cut(kind, ref, index):
    if kind == 0:
        return ref.at[index]
    if kind == 1:
        return ref.at[index // 2, :, index % 2]
    return ref.at[:, index]


def third_cut(kind, ref, index):
    if kind == 0:
        return ref.at[index // 2, index % 2]
    return ref.at[index]


def spots(lead, i):
    found = []
    for size in reversed(lead):
        found.insert(0, i % size)
        i = i // size
    return tuple(found)


def added(base, arrivals):
    total = base.astype(FULL)
    for arrival in arrivals:
        total = total + arrival.astype(FULL)
    return total


def of(r, name, p):
    return getattr(r, name + str(p))


def owner_pick(rows_each, core):
    shift = rows_each.bit_length() - 1
    feature = lax.broadcasted_iota(jnp.int32, (256, 128), 0)
    place = lax.broadcasted_iota(jnp.int32, (256, 128), 1)
    wanted = ((place >> shift) << (shift + 1)) + (place & (rows_each - 1)) + core * rows_each
    return jnp.where(feature == wanted, 1.0, 0.0).astype(HALF)


def in_two(row):
    high = row.astype(HALF)
    low = (row - high.astype(FULL)).astype(HALF)
    place = lax.broadcasted_iota(jnp.int32, (16, row.shape[1]), 0)
    wide_high = jnp.broadcast_to(high.astype(FULL), place.shape)
    wide_low = jnp.broadcast_to(low.astype(FULL), place.shape)
    return jnp.where(place == 0, wide_high, jnp.where(place == 1, wide_low, 0.0)).astype(HALF)


def whole_kernel(names, summing, *refs):
    r = SimpleNamespace(**dict(zip(names, refs)))
    lat, lon = lax.axis_index("lat"), lax.axis_index("lon")
    lats, lons = lax.axis_size("lat"), lax.axis_size("lon")
    core = lon % 2
    place = {"y": lat // 2, "x": lon // 4, "z": lat % 2 * 2 + lon // 2 % 2}
    sibling = (lat, lon + 1 - 2 * core)
    edge = jnp.where(lat == lats - 1, 1, 0)
    used = [0]

    def remote(source, target, device):
        slot = used[0]
        used[0] += 1
        copy = pltpu.make_async_remote_copy(
            src_ref=source,
            dst_ref=target,
            send_sem=r.send_sem.at[slot],
            recv_sem=r.recv_sem.at[slot],
            device_id=device,
            device_id_type=MESH,
        )
        copy.start()
        return copy

    def neighbour(step, way):
        return (
            lax.rem(lat + lats + way * step[0], lats),
            lax.rem(lon + lons + way * step[1], lons),
        )

    loads = {}

    def load(name):
        slot = LOADED.index(name)
        loads[name] = pltpu.make_async_copy(getattr(r, name + "_any"), getattr(r, name), r.load_sem.at[slot])
        loads[name].start()

    for kind, held in (("back", "in"), ("end", "mid")):
        for matrix in ("_pack", "_own", "_halo"):
            setattr(r, kind + matrix, getattr(r, held + matrix))
    r.patches_grad = r.fine_out
    r.normal, r.cot_flat, r.wide = r.tokens_back, r.coarse_attended, r.unit_coarse
    for name in LOADED[:6]:
        load(name)

    barrier = pltpu.get_barrier_semaphore()
    partners = [neighbour(step, way) for step in STEPS for way in (1, -1)] + [sibling]
    if summing:
        partners += [
            device_at(along(place, axis, k), core) for axis in ("x", "y", "z") for k in (1, 2, 3)
        ]
    for partner in partners:
        pl.semaphore_signal(barrier, inc=1, device_id=partner, device_id_type=MESH)

    def pack_piece(kind, value, slot, size):
        rows = slice(PIECES[slot], PIECES[slot] + size)
        getattr(r, kind + "_packed")[rows, :] = dot(getattr(r, kind + "_pack")[rows, :], value).astype(HALF)

    def send_piece(kind, slot, size, sign):
        rows = pl.ds(PIECES[slot], size)
        return remote(
            getattr(r, kind + "_packed").at[rows],
            getattr(r, kind + "_landed").at[rows],
            neighbour(STEPS[slot], -sign),
        )

    def gathered(kind, rows, value, sizes, needed):
        total = dot(getattr(r, kind + "_own")[rows, :], value)
        for slot in needed:
            piece = slice(PIECES[slot], PIECES[slot] + sizes[slot])
            total = total + dot(getattr(r, kind + "_halo")[rows, piece], getattr(r, kind + "_landed")[piece, :])
        return total

    fine_sizes, coarse_sizes = (112, 112, 48), (48, 48, 48)
    loads["in_pack"].wait()
    for slot in (LAT, DIAG, LON):
        pack_piece("in", r.tokens[...], slot, fine_sizes[slot])
    pl.semaphore_wait(barrier, len(partners))
    arrive = {slot: send_piece("in", slot, fine_sizes[slot], 1) for slot in (LAT, DIAG, LON)}
    for n in range(12):
        r.wide[WW * n : WW * n + WW, :] = r.cotangent[n // 6, n % 6].astype(FULL)
    cotangent = r.wide[...].astype(HALF)
    r.cot_flat[...] = cotangent
    for slot in (LAT, DIAG, LON):
        pack_piece("cot", cotangent, slot, coarse_sizes[slot])
    r.fine_out[...] = jnp.zeros_like(r.fine_out)

    keep4, give4 = owner_pick(4, core), owner_pick(4, 1 - core)
    keep8, give8 = owner_pick(8, core), owner_pick(8, 1 - core)
    keep16, give16 = owner_pick(16, core), owner_pick(16, 1 - core)

    def split(value, keep, give, name, rows):
        for block in range(value.shape[1] // 256):
            part = value[:, 256 * block : 256 * block + 256]
            cols = slice(128 * block, 128 * block + 128)
            getattr(r, name + "_left")[rows, cols] = dot(part, keep).astype(HALF)
            getattr(r, name + "_give")[rows, cols] = dot(part, give).astype(HALF)

    def hand_left(name):
        count = getattr(r, name + "_give").shape[0]
        return remote(getattr(r, name + "_give"), getattr(r, name + "_left").at[pl.ds(count, count)], sibling)

    def hand_right(name, start, size):
        half = getattr(r, name).shape[0] // 2
        held = getattr(r, name)
        return remote(held.at[pl.ds(start, size)], held.at[pl.ds(half + start, size)], sibling)

    handed_fine, handed_coarse, late = [], [], []

    needs = ((), (LON,), (LAT,), (LON, LAT, DIAG))
    waited = set()
    mid_arrive = []
    for name in LOADED[1:6]:
        loads[name].wait()
    for name in LOADED[6:11]:
        load(name)
    for w in range(4):
        for slot in needs[w]:
            if slot not in waited:
                arrive[slot].wait()
                waited.add(slot)
        rows = slice(CELLS * w, CELLS * w + CELLS)
        values = gathered("in", rows, r.tokens[...], fine_sizes, needs[w])
        r.rolled[rows, :] = values.astype(HALF)
        unit, _ = norm_parts(values)
        normed = (unit * r.gain_f[...]).astype(HALF)
        r.normal[rows, :] = normed
        qkv = r.qkv
        for n in range(3):
            cols = slice(512 * n, 512 * n + 512)
            qkv[rows, cols] = dot(normed, r.qkv_f[:, cols]).astype(HALF)
        mask = pair_mask(edge if w >= 2 else 0)
        for p in range(4):
            at = 128 * p
            queries = two_heads(qkv[rows, at : at + 128])
            weights = pair_weights(queries, qkv[rows, 512 + at : 640 + at], mask)
            rounded = weights.astype(HALF)
            r.kept[4 * w + p] = rounded
            r.attended[rows, at : at + 128] = pair_forward(
                rounded, qkv[rows, 1024 + at : 1152 + at]
            )
        attended = r.attended[rows, :]
        r.fine_out[rows, :] = (values + dot(attended, r.proj_f[...])).astype(HALF)
        for slot in {1: (LAT,), 2: (DIAG, LON)}.get(w, ()):
            pack_piece("mid", r.fine_out[...], slot, fine_sizes[slot])
            mid_arrive.append(send_piece("mid", slot, fine_sizes[slot], 1))
        if w == 2:
            cot_arrive = [send_piece("cot", n, coarse_sizes[n], 1) for n in (LAT, DIAG, LON)]
    for w in range(4):
        rows = slice(CELLS * w, CELLS * w + CELLS)
        split(r.normal[rows, :], keep4, give4, "normal", rows)
        split(r.attended[rows, :], keep4, give4, "attended", rows)
    handed_fine += [hand_left("normal"), hand_left("attended")]
    for name in LOADED[11:14]:
        load(name)

    every, own = slice(None), slice(0, CELLS)
    loads["mid_own"].wait()
    loads["mid_halo"].wait()
    for copy in mid_arrive:
        copy.wait()
    values = jnp.concatenate(
        [
            gathered(
                "mid",
                slice(CELLS * g, CELLS * g + CELLS),
                r.fine_out[...],
                fine_sizes,
                (LON, LAT, DIAG),
            )
            for g in range(4)
        ],
        axis=1,
    )
    for name in LOADED[14:]:
        load(name)
    unit, scale_merge = norm_parts(values)
    r.unit_merge[...] = unit
    merged = (unit * r.gain_m[...]).astype(HALF)
    loads["merge_w"].wait()
    coarse_in = dot(merged, r.merge_w[...]).astype(HALF).astype(FULL)
    split(merged, keep16, give16, "merged", own)
    merged_handed = hand_left("merged")
    unit, scale_coarse = norm_parts(coarse_in)
    r.unit_coarse[...] = unit
    normed = (unit * r.gain_c[...]).astype(HALF)
    loads["qkv_c"].wait()
    for n in range(3):
        cols = slice(1024 * n, 1024 * (n + 1))
        r.qkv_coarse[:, cols] = dot(normed, r.qkv_c[:, cols]).astype(HALF)
    split(normed, keep8, give8, "normed", own)
    handed_coarse.append(hand_left("normed"))
    for copy in cot_arrive:
        copy.wait()
    cot = gathered("cot", every, r.cot_flat[...], coarse_sizes, (LON, LAT, DIAG)).astype(HALF)
    r.cot_right[own, :] = cot
    handed_coarse.append(hand_right("cot_right", 0, CELLS))
    loads["proj_c"].wait()
    r.cot_attended[...] = dot_nt(cot, r.proj_c[...]).astype(HALF)
    qkv = r.qkv_coarse
    mask = pair_mask(edge)
    for p in range(8):
        at = 128 * p
        queries = two_heads(qkv[:, at : at + 128])
        keys, worth = qkv[:, 1024 + at : 1152 + at], qkv[:, 2048 + at : 2176 + at]
        weights = pair_weights(queries, keys, mask)
        rounded = weights.astype(HALF)
        r.coarse_attended[:, at : at + 128] = pair_forward(rounded, worth)
        upstream = two_heads(r.cot_attended[:, at : at + 128])
        grads = pair_back(weights, rounded, queries, keys, worth, upstream)
        for n in range(3):
            r.qkv_right[own, 1024 * n + at : 1024 * n + at + 128] = grads[n]
    handed_coarse.append(hand_right("qkv_right", 0, CELLS))
    attended = r.coarse_attended[...]
    split(attended, keep8, give8, "coarse", own)
    handed_coarse.append(hand_left("coarse"))
    normed_grad = dot_nt(r.qkv_right[own, :], r.qkv_c[...]).astype(HALF).astype(FULL)
    gain_row = jnp.sum(normed_grad * r.unit_coarse[...], axis=0, keepdims=True)
    split(in_two(gain_row), keep8, give8, "gain_coarse", slice(0, 16))
    gains_handed = [hand_left("gain_coarse")]
    coarse_grad = r.cot_right[own, :].astype(FULL) + norm_back(
        normed_grad, r.unit_coarse[...], scale_coarse, r.gain_c[...]
    )
    r.inner_right[own, :] = coarse_grad.astype(HALF)
    inner_handed = hand_right("inner_right", 0, CELLS)
    merged_grad = dot_nt(r.inner_right[own, :], r.merge_w[...]).astype(HALF).astype(FULL)
    gain_row = jnp.sum(merged_grad * r.unit_merge[...], axis=0, keepdims=True)
    split(in_two(gain_row), keep16, give16, "gain_merge", slice(0, 16))
    gains_handed.append(hand_left("gain_merge"))
    back = norm_back(merged_grad, r.unit_merge[...], scale_merge, r.gain_m[...]).astype(HALF)
    for g in range(4):
        r.patches_grad[CELLS * g : CELLS * (g + 1), :] = back[:, 512 * g : 512 * (g + 1)]
    for name in ("back_pack", "back_own", "back_halo"):
        loads[name].wait()
    back_arrive = {}
    for slot in (LAT, DIAG, LON):
        pack_piece("back", r.patches_grad[...], slot, fine_sizes[slot])
        back_arrive[slot] = send_piece("back", slot, fine_sizes[slot], -1)
    r.coarse_out[...] = (coarse_in + dot(attended, r.proj_c[...])).astype(HALF)
    for slot in (LAT, DIAG, LON):
        pack_piece("out", r.coarse_out[...], slot, coarse_sizes[slot])

    sums = {}

    def across(axis):
        mine = place[axis]
        near, far = mine + 1 - 2 * (mine % 2), 3 - mine
        return mine, ((near, far), (far, near))

    def there(axis, index):
        return device_at({**place, axis: index}, core)

    def stage_of(p, stage):
        landed = of(r, ("landed0_", "landed1_")[stage], p)
        lead = LEADS[p % 3][stage]
        size = int(np.prod(lead))
        if stage == 0:
            source = lambda index: first_cut(p % 3, of(r, "share", p), index)
        else:
            source = lambda index: second_cut(p % 3, of(r, "landed0_", p).at[1], index)
        return source, landed, lead, size, ORDERS[p % 3][stage]

    def halves(lead):
        return [pl.ds(h * (lead[0] // 2), lead[0] // 2) for h in range(2)]

    def begin(p, stage):
        source, landed, lead, size, axis = stage_of(p, stage)
        mine, pairs = across(axis)
        sums[p] = {}
        for slot in range(2):
            for h, rows in enumerate(halves(lead)):
                one = pairs[h][0]
                quarter = lax.rem(mine + 2, 4) if slot == 0 else one
                sums[p][h, slot] = remote(
                    source(quarter).at[rows], landed.at[slot, rows], there(axis, one)
                )

    def forward(p, stage):
        source, landed, lead, size, axis = stage_of(p, stage)
        mine, pairs = across(axis)
        for h, rows in enumerate(halves(lead)):
            two = pairs[h][1]
            theirs = source(two)
            sums[p][h, 0].wait()

            def add(i, carry, h=h, theirs=theirs):
                at = spots(lead, i + h * (size // 2))
                landed[(0,) + at] = added(theirs[at], [landed[(0,) + at]]).astype(HALF)
                return carry

            lax.fori_loop(0, size // 2, add, 0, unroll=2)
            sums[p][h, 2] = remote(landed.at[0, rows], landed.at[2, rows], there(axis, two))

    def collect(p, stage):
        source, landed, lead, size, axis = stage_of(p, stage)
        mine = source(place[axis])
        for h in range(2):
            sums[p][h, 1].wait()
            sums[p][h, 2].wait()

        def add(i, carry):
            at = spots(lead, i)
            total = added(mine[at], [landed[(1,) + at], landed[(2,) + at]])
            landed[(1,) + at] = total.astype(HALF)
            return carry

        lax.fori_loop(0, size, add, 0, unroll=4)

    def start_first(p):
        axis = ORDERS[p % 3][0]
        sums[p] = []
        for k in (2, 1, 3):
            moved = along(place, axis, k)
            sums[p].append(
                remote(
                    first_cut(p % 3, of(r, "share", p), moved[axis]),
                    of(r, "landed0_", p).at[k - 1],
                    device_at(moved, core),
                )
            )

    def collect_first(p):
        source, landed, lead, size, axis = stage_of(p, 0)
        mine = source(place[axis])
        for copy in sums[p]:
            copy.wait()

        def add(i, carry):
            at = spots(lead, i)
            total = added(mine[at], [landed[(k,) + at] for k in range(3)])
            landed[(1,) + at] = total.astype(HALF)
            return carry

        lax.fori_loop(0, size, add, 0, unroll=4)

    def start_second(p):
        source, landed, lead, size, axis = stage_of(p, 1)
        sums[p] = []
        for k in (2, 1, 3):
            moved = along(place, axis, k)
            sums[p].append(
                remote(source(moved[axis]), landed.at[k - 1], device_at(moved, core))
            )

    def collect_second(p):
        source, landed, lead, size, axis = stage_of(p, 1)
        for copy in sums[p]:
            copy.wait()
        total = added(source(place[axis])[...], [landed[k] for k in range(3)])
        landed[1] = total.astype(HALF)

    def start_third(p):
        axis = ORDERS[p % 3][2]
        sums[p] = []
        for k in (2, 1, 3):
            moved = along(place, axis, k)
            sums[p].append(
                remote(
                    third_cut(p % 3, of(r, "landed1_", p).at[1], moved[axis]),
                    of(r, "landed2_", p).at[k - 1],
                    device_at(moved, core),
                )
            )

    def finish(p):
        for copy in sums[p]:
            copy.wait()
        mine = third_cut(p % 3, of(r, "landed1_", p).at[1], place[ORDERS[p % 3][2]])
        total = added(mine[...], [of(r, "landed2_", p)[k] for k in range(3)])
        of(r, "sum", p)[...] = total

    for copy in handed_coarse:
        copy.wait()

    def paired(grad, lead):
        width = grad.shape[1] // 2
        rows = grad.shape[0] // 8
        pieces = [grad[:, :width].reshape(rows, 8, width), grad[:, width:].reshape(rows, 8, width)]
        return jnp.concatenate(pieces, axis=1).astype(HALF).reshape(lead + (16, width))

    def qkv_rows(n, carry):
        cols = pl.ds(pl.multiple_of(n * 256, 256), 256)
        left = r.normed_left[:, cols]
        for low, share, at in ((0, 1, 0), (512, 1, 512), (1024, 2, 0)):
            right = jnp.concatenate(
                [
                    r.qkv_right[:, low : low + 512],
                    r.qkv_right[:, low + 1536 : low + 2048],
                ],
                axis=1,
            )
            of(r, "share", share)[pl.ds(n * 2, 2), :, :, :, :, at : at + 512] = paired(
                dot_tn(left, right), (2, 2, 4, 2)
            )
        grad = dot_tn(r.coarse_left[:, cols], r.cot_right[...])
        r.share2[pl.ds(n * 2, 2), :, :, :, :, 512:] = paired(grad, (2, 2, 4, 2))
        return carry

    lax.fori_loop(0, 2, qkv_rows, 0)
    if summing:
        begin(1, 0)
        begin(2, 0)
    for copy in gains_handed + [merged_handed, inner_handed]:
        copy.wait()
    ones = jnp.ones((32, 128), HALF)
    left_lane = lax.broadcasted_iota(jnp.int32, (64, 16, 128), 2) < HD
    by_merge = dot_tn(r.gain_merge_left[...], ones).reshape(64, 16, 128)
    by_coarse = dot_tn(r.gain_coarse_left[...], ones).reshape(64, 8, 128)
    by_coarse = jnp.concatenate([by_coarse, by_coarse], axis=1)
    gains = jnp.where(left_lane, by_merge, by_coarse).astype(HALF)
    r.share0[:, :, :, :, :, 1024:] = gains.reshape(4, 2, 4, 2, 16, 128)

    def merge_rows(n, carry):
        left = r.merged_left[:, pl.ds(pl.multiple_of(n * 256, 256), 256)]
        grad = dot_tn(left, r.inner_right[...])
        r.share0[n, :, :, :, :, :1024] = grad.astype(HALF).reshape(2, 4, 2, 16, 1024)
        return carry

    lax.fori_loop(0, 4, merge_rows, 0)
    if summing:
        begin(0, 0)

    needs = ((LON, LAT, DIAG), (LAT,), (LON,), ())
    waited = set()
    end_arrive = []
    for w in (3, 2, 1, 0):
        for slot in needs[w]:
            if slot not in waited:
                back_arrive[slot].wait()
                waited.add(slot)
        rows = slice(CELLS * w, CELLS * w + CELLS)
        grad = gathered("back", rows, r.patches_grad[...], fine_sizes, needs[w]).astype(HALF)
        r.fine_right[rows, :] = grad
        handed_fine.append(hand_right("fine_right", CELLS * w, CELLS))
        attended_grad = dot_nt(grad, r.proj_f[...]).astype(HALF)
        qkv = r.qkv
        for p in range(4):
            at = 128 * p
            queries = two_heads(qkv[rows, at : at + 128])
            keys, worth = qkv[rows, 512 + at : 640 + at], qkv[rows, 1024 + at : 1152 + at]
            rounded = r.kept[4 * w + p]
            upstream = two_heads(attended_grad[:, at : at + 128])
            grads = pair_back(rounded.astype(FULL), rounded, queries, keys, worth, upstream)
            for n in range(3):
                r.triple_right[rows, 512 * n + at : 512 * n + at + 128] = grads[n]
        handed_fine.append(hand_right("triple_right", CELLS * w, CELLS))
        if w == 3:
            out_arrive = [send_piece("out", n, coarse_sizes[n], -1) for n in (LAT, DIAG, LON)]
        if summing:
            for p in {2: (1, 2), 0: (0,)}.get(w, ()):
                forward(p, 0)
    for copy in handed_fine:
        copy.wait()

    def store(n, p, at, pieces):
        width = pieces[0].shape[1]
        for side, value in enumerate(four_stacked(pieces)):
            of(r, "share", p)[pl.ds(n * 2, 2), :, :, side, :, at : at + width] = value.reshape(
                2, 2, 4, 16, width
            )

    def fine_rows(n, carry):
        cols = pl.ds(pl.multiple_of(n * 128, 128), 128)
        grad = dot_tn(r.normal_left[:, cols], r.triple_right[...])
        store(n, 3, 0, [grad[:, 384 * m : 384 * m + 256] for m in range(4)])
        store(n, 4, 0, [grad[:, 384 * m + 256 : 384 * m + 384] for m in range(4)])
        grad = dot_tn(r.attended_left[:, cols], r.fine_right[...])
        store(n, 4, 128, [grad[:, 128 * m : 128 * m + 128] for m in range(4)])
        return carry

    lax.fori_loop(0, 2, fine_rows, 0)
    if summing:
        for p in (3, 4):
            start_first(p)
        for p in (1, 2):
            collect(p, 0)
            begin(p, 1)
    gain_row = jnp.zeros((1, 512), FULL)
    r.tokens_back[...] = jnp.zeros_like(r.tokens_back)
    for w in (3, 2, 1, 0):
        rows = slice(CELLS * w, CELLS * w + CELLS)
        normed_grad = dot_nt(r.triple_right[rows, :], r.qkv_f[...]).astype(HALF).astype(FULL)
        unit, scale = norm_parts(r.rolled[rows, :].astype(FULL))
        gain_row = gain_row + jnp.sum(normed_grad * unit, axis=0, keepdims=True)
        back = norm_back(normed_grad, unit, scale, r.gain_f[...])
        r.tokens_back[rows, :] = (r.fine_right[rows, :].astype(FULL) + back).astype(HALF)
        for slot in {2: (LAT,), 1: (DIAG, LON)}.get(w, ()):
            if not end_arrive:
                loads["end_pack"].wait()
            pack_piece("end", r.tokens_back[...], slot, fine_sizes[slot])
            end_arrive.append(send_piece("end", slot, fine_sizes[slot], -1))
        if summing and w == 2:
            collect(0, 0)
            begin(0, 1)
            forward(1, 1)
            forward(2, 1)
    split(in_two(gain_row), keep4, give4, "gain_fine", slice(0, 16))
    gain_handed = hand_left("gain_fine")
    if summing:
        for p in (3, 4):
            collect_first(p)
            start_second(p)
        forward(0, 1)
    gain_handed.wait()
    for n in range(2):
        cols = slice(128 * n, 128 * n + 128)
        store(n, 5, 0, [dot_tn(r.gain_fine_left[:, cols], ones)] * 4)
    if summing:
        start_first(5)
    for copy in out_arrive:
        copy.wait()
    r.coarse_tokens[...] = gathered(
        "out", every, r.coarse_out[...], coarse_sizes, (LON, LAT, DIAG)
    ).astype(HALF)
    if summing:
        for p in (1, 2):
            collect(p, 1)
            start_third(p)
        collect_first(5)
        start_second(5)
        for p in (3, 4):
            collect_second(p)
            start_third(p)
        collect(0, 1)
        start_third(0)
    for name in ("end_own", "end_halo"):
        loads[name].wait()
    for copy in end_arrive:
        copy.wait()
    r.tokens_grad[...] = gathered(
        "end", every, r.tokens_back[...], fine_sizes, (LON, LAT, DIAG)
    ).astype(HALF)
    if summing:
        collect_second(5)
        start_third(5)
        for p in (1, 2, 0, 3, 4, 5):
            finish(p)
    else:
        for p in range(6):
            of(r, "sum", p)[...] = of(r, "share", p)[...].reshape(64, 16, WIDTHS[p])


LOADED = tuple(
    dict(
        in_pack=0,
        in_own=0,
        in_halo=0,
        qkv_f=0,
        proj_f=0,
        mid_pack=0,
        proj_c=0,
        mid_own=0,
        mid_halo=0,
        merge_w=0,
        qkv_c=0,
        back_pack=0,
        back_own=0,
        back_halo=0,
        end_pack=0,
        end_own=0,
        end_halo=0,
    )
)


def whole(values, summing):
    inputs, scratch, outputs = [], [], []

    def matrices(kind, rows, cols, source, target, sign):
        pack, own, halo, _ = roll_matrices(rows, cols, source, target, sign)
        return {
            kind + "_pack": jnp.asarray(pack, HALF),
            kind + "_own": jnp.asarray(own, HALF),
            kind + "_halo": jnp.asarray(halo, HALF),
        }

    values = dict(values)
    values.update(matrices("in", 12, 24, "natural", "window", 1))
    values.update(matrices("cot", 6, 12, "natural", "window", 1))
    values.update(matrices("mid", 12, 24, "window", "patch", 1))
    values.update(matrices("back", 12, 24, "patch", "window", -1))
    values.update(matrices("end", 12, 24, "window", "natural", -1))
    values.update(matrices("out", 6, 12, "window", "natural", -1))
    specs, operands = [], []
    for name, value in values.items():
        loaded = name in LOADED
        inputs.append(name + "_any" if loaded else name)
        specs.append(ANYWHERE if loaded else VMEM)
        operands.append(value)
    half = {name: values[name].shape for name in LOADED[:11]}
    for kind, width in (("in", 512), ("cot", 1024), ("mid", 512), ("back", 512), ("end", 512), ("out", 1024)):
        half[kind + "_packed"] = half[kind + "_landed"] = (PACKED, width)
    lefts = dict(
        normal=(576, 256),
        attended=(576, 256),
        merged=(CELLS, 1024),
        normed=(CELLS, 512),
        coarse=(CELLS, 512),
        gain_coarse=(16, 512),
        gain_merge=(16, 1024),
        gain_fine=(16, 256),
    )
    for name, (count, width) in lefts.items():
        half[name + "_left"] = (2 * count, width)
        half[name + "_give"] = (count, width)
    half.update(
        kept=(16, CELLS, 2 * CELLS),
        rolled=(576, 512),
        qkv=(576, 1536),
        attended=(576, 512),
        fine_out=(576, 512),
        tokens_back=(576, 512),
        cot_right=(2 * CELLS, 1024),
        cot_attended=(CELLS, 1024),
        qkv_coarse=(CELLS, 3072),
        coarse_attended=(CELLS, 1024),
        coarse_out=(CELLS, 1024),
        qkv_right=(2 * CELLS, 3072),
        inner_right=(2 * CELLS, 1024),
        fine_right=(1152, 512),
        triple_right=(1152, 1536),
    )
    for p, width in enumerate(WIDTHS):
        half["share" + str(p)] = (4, 2, 4, 2, 16, width)
        if summing:
            first, second = LEADS[p % 3]
            half["landed0_" + str(p)] = (3,) + first + (16, width)
            half["landed1_" + str(p)] = (3,) + second + (16, width)
            half["landed2_" + str(p)] = (3, 16, width)
    memory = {name: pltpu.VMEM(shape, HALF) for name, shape in half.items()}
    memory["unit_merge"] = pltpu.VMEM((CELLS, 2048), FULL)
    memory["unit_coarse"] = pltpu.VMEM((CELLS, 1024), FULL)
    memory["send_sem"] = pltpu.SemaphoreType.DMA((150,))
    memory["recv_sem"] = pltpu.SemaphoreType.DMA((150,))
    memory["load_sem"] = pltpu.SemaphoreType.DMA((len(LOADED),))
    outputs = {
        "coarse_tokens": jax.ShapeDtypeStruct((CELLS, 1024), HALF),
        "tokens_grad": jax.ShapeDtypeStruct((576, 512), HALF),
    }
    for p, width in enumerate(WIDTHS):
        outputs["sum" + str(p)] = (
            jax.ShapeDtypeStruct((16, width), FULL)
            if summing
            else jax.ShapeDtypeStruct((64, 16, width), HALF)
        )
    names = tuple(inputs) + tuple(outputs) + tuple(memory)
    results = pl.pallas_call(
        functools.partial(whole_kernel, names, summing),
        out_shape=list(outputs.values()),
        in_specs=specs,
        out_specs=[VMEM] * len(outputs),
        scratch_shapes=list(memory.values()),
        compiler_params=pltpu.CompilerParams(
            collective_id=1, has_side_effects=True, vmem_limit_bytes=LIMIT
        ),
    )(*operands)
    return dict(zip(outputs, results))


def prepared(
    tokens,
    cotangent,
    gain_fine,
    qkv_fine,
    proj_fine,
    gain_merge,
    merge_weight,
    gain_coarse,
    qkv_coarse,
    proj_coarse,
):
    return dict(
        tokens=tokens.reshape(576, 512),
        cotangent=cotangent,
        gain_f=gain_fine.reshape(1, 512),
        gain_m=gain_merge.reshape(1, 2048),
        gain_c=gain_coarse.reshape(1, 1024),
        qkv_f=qkv_fine,
        proj_f=proj_fine,
        merge_w=merge_weight,
        qkv_c=qkv_coarse,
        proj_c=proj_coarse,
    )


def last_kernel(*refs):
    coarse, tokens, a, b, c, d, e, f = refs[:8]
    coarse_out, tokens_out, fine_gain, qkv_f, proj_f, merge_gain, merge, coarse_gain, qkv_c, proj_c = refs[8:]
    cells = coarse[...].astype(FULL)
    for n in range(12):
        coarse_out[n // 6, n % 6] = cells[WW * n : WW * n + WW].astype(HALF)
    tokens_out[...] = tokens[...]

    def across(column, count):
        row = lax.broadcasted_iota(jnp.int32, (16, 128), 0)
        lane = lax.broadcasted_iota(jnp.int32, (16, 128), 1)
        line = jnp.sum(jnp.where(row == lane, column, 0.0), axis=0, keepdims=True)
        return line[:, :count]

    block = a[:, 1024:]
    merge_gain[...] = across(jnp.broadcast_to(block[:, :1], (16, 128)), 16)
    coarse_gain[...] = across(jnp.broadcast_to(block[:, HD : HD + 1], (16, 128)), 8)
    fine_gain[...] = across(f[...], 4)
    merge[...] = a[:, :1024]
    for n in range(2):
        rows = slice(8 * n, 8 * n + 8)
        qkv_c[:, 1536 * n : 1536 * n + 1024] = b[rows, :]
        qkv_c[:, 1536 * n + 1024 : 1536 * n + 1536] = c[rows, :512]
        proj_c[:, 512 * n : 512 * n + 512] = c[rows, 512:]
    for n in range(4):
        rows = slice(4 * n, 4 * n + 4)
        qkv_f[:, 384 * n : 384 * n + 256] = d[rows, :]
        qkv_f[:, 384 * n + 256 : 384 * n + 384] = e[rows, :128]
        proj_f[:, 128 * n : 128 * n + 128] = e[rows, 128:]


def last(found):
    shapes = [jax.ShapeDtypeStruct((2, 6, WW, 1024), HALF), jax.ShapeDtypeStruct((576, 512), HALF)]
    shapes += [
        jax.ShapeDtypeStruct(shape, FULL)
        for shape in (
            (1, 4),
            (4, 1536),
            (4, 512),
            (1, 16),
            (16, 1024),
            (1, 8),
            (8, 3072),
            (8, 1024),
        )
    ]
    outs = pl.pallas_call(
        last_kernel, out_shape=shapes, in_specs=[VMEM] * 8, out_specs=[VMEM] * 10
    )(*found)
    outs = list(outs)
    outs[1] = outs[1].reshape(2, 12, 24, 512)
    for n in (2, 5, 7):
        outs[n] = outs[n].reshape(-1)
    return tuple(outs)


def local(*args):
    found = whole(prepared(*args), True)
    return last(tuple(found.values()))


def solution(mesh):
    grid = P(None, "lat", "lon", None)
    vector, matrix = P(("lat", "lon")), P(("lat", "lon"), None)
    return jax.shard_map(
        local,
        mesh=mesh,
        in_specs=(grid, grid) + (P(),) * 8,
        out_specs=(grid, grid, vector, matrix, matrix, vector, matrix, vector, matrix, matrix),
        check_vma=False,
    )
```

```python
import functools
from types import SimpleNamespace

import jax
import jax.numpy as jnp
import numpy as np
from jax import lax
from jax.experimental import pallas as pl
from jax.experimental.pallas import tpu as pltpu
from jax.sharding import PartitionSpec as P

MESH = pl.DeviceIdType.MESH
HALF = jnp.bfloat16
FULL = jnp.float32
HD = 64
WH = 6
WW = 12
CELLS = 144
EPSILON = 1e-05
MASKED = -1e30
PIECES = (0, 128, 256)
PACKED = 304
LIMIT = 62 * 1024 * 1024
VMEM = pl.BlockSpec(memory_space=pltpu.VMEM)
SMEM = pl.BlockSpec(memory_space=pltpu.SMEM)
ANYWHERE = pl.BlockSpec(memory_space=pl.ANY)


def dot(left, right):
    return jnp.dot(left, right, preferred_element_type=FULL)


def dot_nt(left, right):
    return lax.dot_general(left, right, (((1,), (1,)), ((), ())), preferred_element_type=FULL)


def dot_tn(left, right):
    return lax.dot_general(left, right, (((0,), (0,)), ((), ())), preferred_element_type=FULL)


def natural_order(rows, cols):
    return lambda level, i, j: (level * rows + i) * cols + j


def level_last_order(rows, cols):
    return lambda level, i, j: (i * cols + j) * 2 + level


def window_order(rows, cols):
    def place(level, i, j):
        window = i // WH * (cols // WW) + j // WW
        return window * CELLS + ((i % WH // 3 * 2 + level) * 3 + i % 3) * WW + j % WW

    return place


def patch_order(rows, cols):
    coarse = window_order(rows // 2, cols // 2)

    def place(level, i, j):
        return (j % 2 * 2 + i % 2) * CELLS + coarse(level, i // 2, j // 2)

    return place


@functools.lru_cache(maxsize=None)
def roll_matrices(rows, cols, source, target, sign):
    orders = {"last": level_last_order, "natural": natural_order, "window": window_order, "patch": patch_order}
    from_place, to_place = orders[source](rows, cols), orders[target](rows, cols)
    count = 2 * rows * cols
    pieces = ([], [], [])
    own = np.zeros((count, count), np.float32)
    for level in range(2):
        for i in range(rows):
            for j in range(cols):
                far_i, far_j = i + 3 * sign, j + 6 * sign
                across = (far_i // rows != 0, far_j // cols != 0)
                here = from_place(level, far_i % rows, far_j % cols)
                there = to_place(level, i, j)
                if across == (False, False):
                    own[there, here] = 1
                else:
                    slot = {(False, True): 0, (True, False): 1, (True, True): 2}[across]
                    pieces[slot].append((there, here))
    sizes = tuple((len(piece) + 15) // 16 * 16 for piece in pieces)
    pack = np.zeros((PACKED, count), np.float32)
    halo = np.zeros((count, PACKED), np.float32)
    for slot, piece in enumerate(pieces):
        for k, (there, here) in enumerate(piece):
            pack[PIECES[slot] + k, here] = 1
            halo[there, PIECES[slot] + k] = 1
    return pack, own, halo, sizes


def norm_parts(values):
    centre = jnp.mean(values, axis=-1, keepdims=True)
    offset = values - centre
    spread = jnp.mean(offset * offset, axis=-1, keepdims=True)
    scale = lax.rsqrt(spread + EPSILON)
    return offset * scale, scale


def norm_back(grad, normal, scale, gain):
    inner = grad * gain
    mean = jnp.mean(inner, axis=-1, keepdims=True)
    along = jnp.mean(inner * normal, axis=-1, keepdims=True)
    return (inner - mean - normal * along) * scale


def two_heads(pair):
    first = lax.broadcasted_iota(jnp.int32, pair.shape, 1) < HD
    zero = jnp.zeros_like(pair)
    return jnp.concatenate([jnp.where(first, pair, zero), jnp.where(first, zero, pair)], axis=0)


def one_pair(stack):
    half = stack.shape[0] // 2
    first = lax.broadcasted_iota(jnp.int32, (half, 2 * HD), 1) < HD
    return jnp.where(first, stack[:half], stack[half:])


def pair_mask(edge):
    shape = (CELLS, 2 * CELLS)
    key = lax.broadcasted_iota(jnp.int32, shape, 0)
    query = lax.broadcasted_iota(jnp.int32, shape, 1)
    query = jnp.where(query >= CELLS, query - CELLS, query)
    apart = (key < CELLS // 2) != (query < CELLS // 2)
    return jnp.where(apart, edge, 0) > 0


def pair_weights(queries, keys, mask):
    scores = dot_nt(keys, queries * 0.125)
    scores = jnp.where(mask, MASKED, scores)
    powers = jnp.exp(scores - jnp.max(scores, axis=0, keepdims=True))
    return powers * (1.0 / jnp.sum(powers, axis=0, keepdims=True))


def pair_forward(rounded, values):
    return one_pair(dot_tn(rounded, values)).astype(HALF)


def pair_back(weights, rounded, queries, keys, values, upstream):
    weight_grad = dot_nt(values, upstream)
    inner = jnp.sum(weights * weight_grad, axis=0, keepdims=True)
    score_grad = (weights * (weight_grad - inner) * 0.125).astype(HALF)
    query_grad = one_pair(dot_tn(score_grad, keys)).astype(HALF)
    key_grad = dot(score_grad, queries).astype(HALF)
    value_grad = dot(rounded, upstream).astype(HALF)
    return query_grad, key_grad, value_grad


def four_stacked(pieces):
    rows, width = pieces[0].shape
    shaped = [piece.reshape(rows // 8, 8, width) for piece in pieces]
    upper = lax.broadcasted_iota(jnp.int32, shaped[0].shape, 1) < 4
    turned = [pltpu.roll(piece, 4, 1) for piece in shaped]
    even = [jnp.where(upper, shaped[n], turned[n + 1]) for n in (0, 2)]
    odd = [jnp.where(upper, turned[n], shaped[n + 1]) for n in (0, 2)]
    return [jnp.concatenate(pair, axis=1).astype(HALF) for pair in (even, odd)]


ORDERS = (("x", "y", "z"), ("y", "z", "x"), ("z", "x", "y"))
LEADS = (((4, 2, 2), (2, 2)), ((2, 4, 2), (4,)), ((4, 4), (4,)))
WIDTHS = (1152, 1024, 1024, 256, 256, 128)
LON, LAT, DIAG = 0, 1, 2
STEPS = ((0, 1), (1, 0), (1, 1))


def device_at(place, core):
    lat = place["y"] * 2 + place["z"] // 2
    lon = place["x"] * 4 + place["z"] % 2 * 2 + core
    return (lat, lon)


def along(place, axis, steps):
    moved = dict(place)
    moved[axis] = lax.rem(place[axis] + steps, 4)
    return moved


def first_cut(kind, ref, index):
    if kind == 0:
        return ref.at[:, :, index]
    if kind == 1:
        return ref.at[index]
    return ref.at[:, index // 2, :, index % 2]


def second_cut(kind, ref, index):
    if kind == 0:
        return ref.at[index]
    if kind == 1:
        return ref.at[index // 2, :, index % 2]
    return ref.at[:, index]


def third_cut(kind, ref, index):
    if kind == 0:
        return ref.at[index // 2, index % 2]
    return ref.at[index]


def spots(lead, i):
    found = []
    for size in reversed(lead):
        found.insert(0, i % size)
        i = i // size
    return tuple(found)


def added(base, arrivals):
    total = base.astype(FULL)
    for arrival in arrivals:
        total = total + arrival.astype(FULL)
    return total


def of(r, name, p):
    return getattr(r, name + str(p))


def owner_pick(rows_each, core):
    shift = rows_each.bit_length() - 1
    feature = lax.broadcasted_iota(jnp.int32, (256, 128), 0)
    place = lax.broadcasted_iota(jnp.int32, (256, 128), 1)
    wanted = ((place >> shift) << (shift + 1)) + (place & (rows_each - 1)) + core * rows_each
    return jnp.where(feature == wanted, 1.0, 0.0).astype(HALF)


def in_two(row):
    high = row.astype(HALF)
    low = (row - high.astype(FULL)).astype(HALF)
    place = lax.broadcasted_iota(jnp.int32, (16, row.shape[1]), 0)
    wide_high = jnp.broadcast_to(high.astype(FULL), place.shape)
    wide_low = jnp.broadcast_to(low.astype(FULL), place.shape)
    return jnp.where(place == 0, wide_high, jnp.where(place == 1, wide_low, 0.0)).astype(HALF)


def whole_kernel(names, summing, *refs):
    r = SimpleNamespace(**dict(zip(names, refs)))
    lat, lon = lax.axis_index("lat"), lax.axis_index("lon")
    lats, lons = lax.axis_size("lat"), lax.axis_size("lon")
    core = lon % 2
    place = {"y": lat // 2, "x": lon // 4, "z": lat % 2 * 2 + lon // 2 % 2}
    sibling = (lat, lon + 1 - 2 * core)
    edge = jnp.where(lat == lats - 1, 1, 0)
    used = [0]

    def remote(source, target, device):
        slot = used[0]
        used[0] += 1
        copy = pltpu.make_async_remote_copy(
            src_ref=source,
            dst_ref=target,
            send_sem=r.send_sem.at[slot],
            recv_sem=r.recv_sem.at[slot],
            device_id=device,
            device_id_type=MESH,
        )
        copy.start()
        return copy

    def neighbour(step, way):
        return (
            lax.rem(lat + lats + way * step[0], lats),
            lax.rem(lon + lons + way * step[1], lons),
        )

    loads = {}

    def load(name):
        slot = LOADED.index(name)
        loads[name] = pltpu.make_async_copy(getattr(r, name + "_any"), getattr(r, name), r.load_sem.at[slot])
        loads[name].start()

    for kind, held in (("back", "in"), ("end", "mid")):
        for matrix in ("_pack", "_own", "_halo"):
            setattr(r, kind + matrix, getattr(r, held + matrix))
    r.patches_grad = r.fine_out
    r.normal, r.wide, r.coarse_in = r.tokens_back, r.unit_coarse, r.coarse_out
    r.cot_flat = r.inner_right.at[pl.ds(0, CELLS)]
    r.back_packed, r.end_packed, r.out_packed = r.in_packed, r.mid_packed, r.cot_packed
    for name in LOADED[:6]:
        load(name)

    barrier = pltpu.get_barrier_semaphore()
    partners = [neighbour(step, way) for step in STEPS for way in (1, -1)] + [sibling]
    if summing:
        partners += [
            device_at(along(place, axis, k), core) for axis in ("x", "y", "z") for k in (1, 2, 3)
        ]
    for partner in partners:
        pl.semaphore_signal(barrier, inc=1, device_id=partner, device_id_type=MESH)

    def pack_piece(kind, value, slot, size):
        rows = slice(PIECES[slot], PIECES[slot] + size)
        getattr(r, kind + "_packed")[rows, :] = dot(getattr(r, kind + "_pack")[rows, :], value).astype(HALF)

    def send_piece(kind, slot, size, sign):
        rows = pl.ds(PIECES[slot], size)
        return remote(
            getattr(r, kind + "_packed").at[rows],
            getattr(r, kind + "_landed").at[rows],
            neighbour(STEPS[slot], -sign),
        )

    def gathered(kind, rows, value, sizes, needed):
        total = dot(getattr(r, kind + "_own")[rows, :], value)
        for slot in needed:
            piece = slice(PIECES[slot], PIECES[slot] + sizes[slot])
            total = total + dot(getattr(r, kind + "_halo")[rows, piece], getattr(r, kind + "_landed")[piece, :])
        return total

    fine_sizes, coarse_sizes = (112, 112, 48), (48, 48, 48)
    loads["in_pack"].wait()
    for slot in (LAT, DIAG, LON):
        pack_piece("in", r.tokens[...], slot, fine_sizes[slot])
    pl.semaphore_wait(barrier, len(partners))
    arrive = {slot: send_piece("in", slot, fine_sizes[slot], 1) for slot in (LAT, DIAG, LON)}
    for n in range(12):
        r.wide[WW * n : WW * n + WW, :] = r.cotangent[n // 6, n % 6].astype(FULL)
    cotangent = r.wide[...].astype(HALF)
    r.cot_flat[...] = cotangent
    for slot in (LAT, DIAG, LON):
        pack_piece("cot", cotangent, slot, coarse_sizes[slot])

    keep4, give4 = owner_pick(4, core), owner_pick(4, 1 - core)
    keep8, give8 = owner_pick(8, core), owner_pick(8, 1 - core)
    keep16, give16 = owner_pick(16, core), owner_pick(16, 1 - core)

    def split(value, keep, give, name, rows):
        for block in range(value.shape[1] // 256):
            part = value[:, 256 * block : 256 * block + 256]
            cols = slice(128 * block, 128 * block + 128)
            getattr(r, name + "_left")[rows, cols] = dot(part, keep).astype(HALF)
            getattr(r, name + "_give")[rows, cols] = dot(part, give).astype(HALF)

    def hand_left(name):
        count = getattr(r, name + "_give").shape[0]
        return remote(getattr(r, name + "_give"), getattr(r, name + "_left").at[pl.ds(count, count)], sibling)

    def hand_right(name, start, size):
        half = getattr(r, name).shape[0] // 2
        held = getattr(r, name)
        return remote(held.at[pl.ds(start, size)], held.at[pl.ds(half + start, size)], sibling)

    def hand_rows(name, w, base):
        held = getattr(r, name)
        half = held.shape[0] // 2
        start = pl.multiple_of(w * CELLS, 16)
        return pltpu.make_async_remote_copy(
            src_ref=held.at[pl.ds(start, CELLS)],
            dst_ref=held.at[pl.ds(pl.multiple_of(half + w * CELLS, 16), CELLS)],
            send_sem=r.send_sem.at[base + w],
            recv_sem=r.recv_sem.at[base + w],
            device_id=sibling,
            device_id_type=MESH,
        )

    def fill(target, left, weight, width):
        def columns(n, carry):
            cols = pl.ds(pl.multiple_of(n * width, width), width)
            target[:, cols] = dot(left(), weight[:, cols]).astype(HALF)
            return carry

        lax.fori_loop(0, weight.shape[1] // width, columns, 0)

    def fill_nt(target, left, weight, width):
        def columns(n, carry):
            cols = pl.ds(pl.multiple_of(n * width, width), width)
            target[:, cols] = dot_nt(left(), weight[cols, :]).astype(HALF)
            return carry

        lax.fori_loop(0, weight.shape[0] // width, columns, 0)

    handed_fine, handed_coarse, late = [], [], []

    every, own = slice(None), slice(0, CELLS)
    all_pieces = (LON, LAT, DIAG)
    for name in LOADED[1:6]:
        loads[name].wait()
    for name in LOADED[6:11]:
        load(name)
    for slot in all_pieces:
        arrive[slot].wait()

    def forward_window(w, carry):
        rows = pl.ds(pl.multiple_of(w * CELLS, 16), CELLS)
        values = gathered("in", rows, r.tokens[...], fine_sizes, all_pieces)
        r.rolled[rows, :] = values.astype(HALF)
        unit, _ = norm_parts(values)
        normed = (unit * r.gain_f[...]).astype(HALF)
        r.normal[rows, :] = normed
        for n in range(3):
            cols = slice(512 * n, 512 * n + 512)
            r.qkv[rows, cols] = dot(normed, r.qkv_f[:, cols]).astype(HALF)
        mask = pair_mask(jnp.where(w >= 2, edge, 0))
        for p in range(4):
            at = 128 * p
            queries = two_heads(r.qkv[rows, at : at + 128])
            weights = pair_weights(queries, r.qkv[rows, 512 + at : 640 + at], mask)
            rounded = weights.astype(HALF)
            r.kept[4 * w + p] = rounded
            r.attended[rows, at : at + 128] = pair_forward(
                rounded, r.qkv[rows, 1024 + at : 1152 + at]
            )
        r.fine_out[rows, :] = (values + dot(r.attended[rows, :], r.proj_f[...])).astype(HALF)
        return carry

    lax.fori_loop(0, 4, forward_window, 0)
    mid_arrive = []
    for slot in (LAT, DIAG, LON):
        pack_piece("mid", r.fine_out[...], slot, fine_sizes[slot])
        mid_arrive.append(send_piece("mid", slot, fine_sizes[slot], 1))
    cot_arrive = [send_piece("cot", n, coarse_sizes[n], 1) for n in (LAT, DIAG, LON)]

    def split_window(w, carry):
        rows = pl.ds(pl.multiple_of(w * CELLS, 16), CELLS)
        split(r.normal[rows, :], keep4, give4, "normal", rows)
        split(r.attended[rows, :], keep4, give4, "attended", rows)
        return carry

    lax.fori_loop(0, 4, split_window, 0)
    handed_fine += [hand_left("normal"), hand_left("attended")]
    for name in LOADED[11:14]:
        load(name)

    loads["mid_own"].wait()
    loads["mid_halo"].wait()
    for copy in mid_arrive:
        copy.wait()
    for g in range(4):
        rows = slice(CELLS * g, CELLS * g + CELLS)
        r.merged[:, 512 * g : 512 * g + 512] = gathered(
            "mid", rows, r.fine_out[...], fine_sizes, all_pieces
        ).astype(HALF)
    for name in LOADED[14:]:
        load(name)

    def merge_norm(n, carry):
        rows = pl.ds(pl.multiple_of(n * 48, 16), 48)
        unit, scale = norm_parts(r.merged[rows, :].astype(FULL))
        r.unit_merge[rows, :] = unit
        r.scale_merge[rows, :] = scale
        r.merged[rows, :] = (unit * r.gain_m[...]).astype(HALF)
        return carry

    lax.fori_loop(0, 3, merge_norm, 0)
    loads["merge_w"].wait()
    fill(r.coarse_in, lambda: r.merged[...], r.merge_w, 512)
    coarse_in = r.coarse_in[...].astype(FULL)
    split(r.merged[...], keep16, give16, "merged", own)
    merged_handed = hand_left("merged")
    unit, scale_coarse = norm_parts(coarse_in)
    r.unit_coarse[...] = unit
    normed = (unit * r.gain_c[...]).astype(HALF)
    r.coarse_attended[...] = normed
    loads["qkv_c"].wait()
    fill(r.qkv_coarse, lambda: r.coarse_attended[...], r.qkv_c, 512)
    split(normed, keep8, give8, "normed", own)
    handed_coarse.append(hand_left("normed"))
    for copy in cot_arrive:
        copy.wait()
    cot = gathered("cot", every, r.cot_flat[...], coarse_sizes, (LON, LAT, DIAG)).astype(HALF)
    r.cot_right[own, :] = cot
    handed_coarse.append(hand_right("cot_right", 0, CELLS))
    loads["proj_c"].wait()
    r.cot_attended[...] = dot_nt(cot, r.proj_c[...]).astype(HALF)
    qkv = r.qkv_coarse
    mask = pair_mask(edge)

    def coarse_pairs(n, carry):
        for side in range(2):
            start = n * 256 + side * 128

            def part(base):
                return pl.ds(pl.multiple_of(base + start, 128), 128)

            queries = two_heads(qkv[:, part(0)])
            keys, worth = qkv[:, part(1024)], qkv[:, part(2048)]
            weights = pair_weights(queries, keys, mask)
            rounded = weights.astype(HALF)
            r.coarse_attended[:, part(0)] = pair_forward(rounded, worth)
            upstream = two_heads(r.cot_attended[:, part(0)])
            grads = pair_back(weights, rounded, queries, keys, worth, upstream)
            for m in range(3):
                r.qkv_right[own, part(1024 * m)] = grads[m]
        return carry

    lax.fori_loop(0, 4, coarse_pairs, 0)
    handed_coarse.append(hand_right("qkv_right", 0, CELLS))
    attended = r.coarse_attended[...]
    split(attended, keep8, give8, "coarse", own)
    handed_coarse.append(hand_left("coarse"))
    fill_nt(r.cot_attended, lambda: r.qkv_right[own, :], r.qkv_c, 256)
    normed_grad = r.cot_attended[...].astype(FULL)
    gain_row = jnp.sum(normed_grad * r.unit_coarse[...], axis=0, keepdims=True)
    split(in_two(gain_row), keep8, give8, "gain_coarse", slice(0, 16))
    gains_handed = [hand_left("gain_coarse")]
    coarse_grad = r.cot_right[own, :].astype(FULL) + norm_back(
        normed_grad, r.unit_coarse[...], scale_coarse, r.gain_c[...]
    )
    r.inner_right[own, :] = coarse_grad.astype(HALF)
    inner_handed = hand_right("inner_right", 0, CELLS)
    fill_nt(r.merged, lambda: r.inner_right[own, :], r.merge_w, 512)

    def merge_back(n, gain_row):
        rows = pl.ds(pl.multiple_of(n * 48, 16), 48)
        merged_grad = r.merged[rows, :].astype(FULL)
        unit = r.unit_merge[rows, :]
        back = norm_back(merged_grad, unit, r.scale_merge[rows, :], r.gain_m[...]).astype(HALF)
        for g in range(4):
            place_at = pl.ds(pl.multiple_of(CELLS * g + n * 48, 16), 48)
            r.patches_grad[place_at, :] = back[:, 512 * g : 512 * (g + 1)]
        return gain_row + jnp.sum(merged_grad * unit, axis=0, keepdims=True)

    gain_row = lax.fori_loop(0, 3, merge_back, jnp.zeros((1, 2048), FULL))
    split(in_two(gain_row), keep16, give16, "gain_merge", slice(0, 16))
    gains_handed.append(hand_left("gain_merge"))
    for name in ("back_pack", "back_own", "back_halo"):
        loads[name].wait()
    back_arrive = {}
    for slot in (LAT, DIAG, LON):
        pack_piece("back", r.patches_grad[...], slot, fine_sizes[slot])
        back_arrive[slot] = send_piece("back", slot, fine_sizes[slot], -1)
    r.coarse_out[...] = (
        r.coarse_in[...].astype(FULL) + dot(r.coarse_attended[...], r.proj_c[...])
    ).astype(HALF)
    for slot in (LAT, DIAG, LON):
        pack_piece("out", r.coarse_out[...], slot, coarse_sizes[slot])

    sums = {}

    def across(axis):
        mine = place[axis]
        near, far = mine + 1 - 2 * (mine % 2), 3 - mine
        return mine, ((near, far), (far, near))

    def there(axis, index):
        return device_at({**place, axis: index}, core)

    def stage_of(p, stage):
        landed = of(r, ("landed0_", "landed1_")[stage], p)
        lead = LEADS[p % 3][stage]
        size = int(np.prod(lead))
        if stage == 0:
            source = lambda index: first_cut(p % 3, of(r, "share", p), index)
        else:
            source = lambda index: second_cut(p % 3, of(r, "landed0_", p).at[1], index)
        return source, landed, lead, size, ORDERS[p % 3][stage]

    def halves(lead):
        return [pl.ds(h * (lead[0] // 2), lead[0] // 2) for h in range(2)]

    def begin(p, stage):
        source, landed, lead, size, axis = stage_of(p, stage)
        mine, pairs = across(axis)
        sums[p] = {}
        for slot in range(2):
            for h, rows in enumerate(halves(lead)):
                one = pairs[h][0]
                quarter = lax.rem(mine + 2, 4) if slot == 0 else one
                sums[p][h, slot] = remote(
                    source(quarter).at[rows], landed.at[slot, rows], there(axis, one)
                )

    def forward(p, stage):
        source, landed, lead, size, axis = stage_of(p, stage)
        mine, pairs = across(axis)
        for h, rows in enumerate(halves(lead)):
            two = pairs[h][1]
            theirs = source(two)
            sums[p][h, 0].wait()

            def add(i, carry, h=h, theirs=theirs):
                at = spots(lead, i + h * (size // 2))
                landed[(0,) + at] = added(theirs[at], [landed[(0,) + at]]).astype(HALF)
                return carry

            lax.fori_loop(0, size // 2, add, 0)
            sums[p][h, 2] = remote(landed.at[0, rows], landed.at[2, rows], there(axis, two))

    def collect(p, stage):
        source, landed, lead, size, axis = stage_of(p, stage)
        mine = source(place[axis])
        for h in range(2):
            sums[p][h, 1].wait()
            sums[p][h, 2].wait()

        def add(i, carry):
            at = spots(lead, i)
            total = added(mine[at], [landed[(1,) + at], landed[(2,) + at]])
            landed[(1,) + at] = total.astype(HALF)
            return carry

        lax.fori_loop(0, size, add, 0)

    def start_first(p):
        axis = ORDERS[p % 3][0]
        sums[p] = []
        for k in (2, 1, 3):
            moved = along(place, axis, k)
            sums[p].append(
                remote(
                    first_cut(p % 3, of(r, "share", p), moved[axis]),
                    of(r, "landed0_", p).at[k - 1],
                    device_at(moved, core),
                )
            )

    def collect_first(p):
        source, landed, lead, size, axis = stage_of(p, 0)
        mine = source(place[axis])
        for copy in sums[p]:
            copy.wait()

        def add(i, carry):
            at = spots(lead, i)
            total = added(mine[at], [landed[(k,) + at] for k in range(3)])
            landed[(1,) + at] = total.astype(HALF)
            return carry

        lax.fori_loop(0, size, add, 0)

    def start_second(p):
        source, landed, lead, size, axis = stage_of(p, 1)
        sums[p] = []
        for k in (2, 1, 3):
            moved = along(place, axis, k)
            sums[p].append(
                remote(source(moved[axis]), landed.at[k - 1], device_at(moved, core))
            )

    def collect_second(p):
        source, landed, lead, size, axis = stage_of(p, 1)
        for copy in sums[p]:
            copy.wait()
        total = added(source(place[axis])[...], [landed[k] for k in range(3)])
        landed[1] = total.astype(HALF)

    def start_third(p):
        axis = ORDERS[p % 3][2]
        sums[p] = []
        for k in (2, 1, 3):
            moved = along(place, axis, k)
            sums[p].append(
                remote(
                    third_cut(p % 3, of(r, "landed1_", p).at[1], moved[axis]),
                    of(r, "landed2_", p).at[k - 1],
                    device_at(moved, core),
                )
            )

    def finish(p):
        for copy in sums[p]:
            copy.wait()
        mine = third_cut(p % 3, of(r, "landed1_", p).at[1], place[ORDERS[p % 3][2]])
        total = added(mine[...], [of(r, "landed2_", p)[k] for k in range(3)])
        of(r, "sum", p)[...] = total

    for copy in handed_coarse:
        copy.wait()

    def paired(grad, lead):
        width = grad.shape[1] // 2
        rows = grad.shape[0] // 8
        pieces = [grad[:, :width].reshape(rows, 8, width), grad[:, width:].reshape(rows, 8, width)]
        return jnp.concatenate(pieces, axis=1).astype(HALF).reshape(lead + (16, width))

    def qkv_rows(n, carry):
        cols = pl.ds(pl.multiple_of(n * 256, 256), 256)
        left = r.normed_left[:, cols]
        for low, share, at in ((0, 1, 0), (512, 1, 512), (1024, 2, 0)):
            right = jnp.concatenate(
                [
                    r.qkv_right[:, low : low + 512],
                    r.qkv_right[:, low + 1536 : low + 2048],
                ],
                axis=1,
            )
            of(r, "share", share)[pl.ds(n * 2, 2), :, :, :, :, at : at + 512] = paired(
                dot_tn(left, right), (2, 2, 4, 2)
            )
        grad = dot_tn(r.coarse_left[:, cols], r.cot_right[...])
        r.share2[pl.ds(n * 2, 2), :, :, :, :, 512:] = paired(grad, (2, 2, 4, 2))
        return carry

    lax.fori_loop(0, 2, qkv_rows, 0)
    if summing:
        begin(1, 0)
        begin(2, 0)
    for copy in gains_handed + [merged_handed, inner_handed]:
        copy.wait()
    ones = jnp.ones((32, 128), HALF)
    left_lane = lax.broadcasted_iota(jnp.int32, (64, 16, 128), 2) < HD
    by_merge = dot_tn(r.gain_merge_left[...], ones).reshape(64, 16, 128)
    by_coarse = dot_tn(r.gain_coarse_left[...], ones).reshape(64, 8, 128)
    by_coarse = jnp.concatenate([by_coarse, by_coarse], axis=1)
    gains = jnp.where(left_lane, by_merge, by_coarse).astype(HALF)
    r.share0[:, :, :, :, :, 1024:] = gains.reshape(4, 2, 4, 2, 16, 128)

    def merge_rows(n, carry):
        left = r.merged_left[:, pl.ds(pl.multiple_of(n * 256, 256), 256)]
        grad = dot_tn(left, r.inner_right[...])
        r.share0[n, :, :, :, :, :1024] = grad.astype(HALF).reshape(2, 4, 2, 16, 1024)
        return carry

    lax.fori_loop(0, 4, merge_rows, 0)
    if summing:
        begin(0, 0)

    for slot in all_pieces:
        back_arrive[slot].wait()
    fine_base, triple_base = used[0], used[0] + 4
    used[0] += 8

    def backward_window(w, carry):
        rows = pl.ds(pl.multiple_of(w * CELLS, 16), CELLS)
        grad = gathered("back", rows, r.patches_grad[...], fine_sizes, all_pieces).astype(HALF)
        r.fine_right[rows, :] = grad
        hand_rows("fine_right", w, fine_base).start()
        attended_grad = dot_nt(grad, r.proj_f[...]).astype(HALF)
        for p in range(4):
            at = 128 * p
            queries = two_heads(r.qkv[rows, at : at + 128])
            keys, worth = r.qkv[rows, 512 + at : 640 + at], r.qkv[rows, 1024 + at : 1152 + at]
            rounded = r.kept[4 * w + p]
            upstream = two_heads(attended_grad[:, at : at + 128])
            grads = pair_back(rounded.astype(FULL), rounded, queries, keys, worth, upstream)
            for n in range(3):
                r.triple_right[rows, 512 * n + at : 512 * n + at + 128] = grads[n]
        hand_rows("triple_right", w, triple_base).start()
        return carry

    lax.fori_loop(0, 4, backward_window, 0)
    out_arrive = [send_piece("out", n, coarse_sizes[n], -1) for n in (LAT, DIAG, LON)]
    if summing:
        for p in (1, 2, 0):
            forward(p, 0)
    for w in range(4):
        hand_rows("fine_right", w, fine_base).wait()
        hand_rows("triple_right", w, triple_base).wait()
    for copy in handed_fine:
        copy.wait()

    def store(n, p, at, pieces):
        width = pieces[0].shape[1]
        for side, value in enumerate(four_stacked(pieces)):
            of(r, "share", p)[pl.ds(n * 2, 2), :, :, side, :, at : at + width] = value.reshape(
                2, 2, 4, 16, width
            )

    def fine_rows(n, carry):
        cols = pl.ds(pl.multiple_of(n * 128, 128), 128)
        grad = dot_tn(r.normal_left[:, cols], r.triple_right[...])
        store(n, 3, 0, [grad[:, 384 * m : 384 * m + 256] for m in range(4)])
        store(n, 4, 0, [grad[:, 384 * m + 256 : 384 * m + 384] for m in range(4)])
        grad = dot_tn(r.attended_left[:, cols], r.fine_right[...])
        store(n, 4, 128, [grad[:, 128 * m : 128 * m + 128] for m in range(4)])
        return carry

    lax.fori_loop(0, 2, fine_rows, 0)
    if summing:
        for p in (3, 4):
            start_first(p)
        for p in (1, 2):
            collect(p, 0)
            begin(p, 1)

    def norm_window(w, gain_row):
        rows = pl.ds(pl.multiple_of(w * CELLS, 16), CELLS)
        normed_grad = dot_nt(r.triple_right[rows, :], r.qkv_f[...]).astype(HALF).astype(FULL)
        unit, scale = norm_parts(r.rolled[rows, :].astype(FULL))
        back = norm_back(normed_grad, unit, scale, r.gain_f[...])
        r.tokens_back[rows, :] = (r.fine_right[rows, :].astype(FULL) + back).astype(HALF)
        return gain_row + jnp.sum(normed_grad * unit, axis=0, keepdims=True)

    gain_row = lax.fori_loop(0, 4, norm_window, jnp.zeros((1, 512), FULL))
    loads["end_pack"].wait()
    end_arrive = []
    for slot in (LAT, DIAG, LON):
        pack_piece("end", r.tokens_back[...], slot, fine_sizes[slot])
        end_arrive.append(send_piece("end", slot, fine_sizes[slot], -1))
    if summing:
        collect(0, 0)
        begin(0, 1)
        forward(1, 1)
        forward(2, 1)
    split(in_two(gain_row), keep4, give4, "gain_fine", slice(0, 16))
    gain_handed = hand_left("gain_fine")
    if summing:
        for p in (3, 4):
            collect_first(p)
            start_second(p)
        forward(0, 1)
    gain_handed.wait()
    for n in range(2):
        cols = slice(128 * n, 128 * n + 128)
        store(n, 5, 0, [dot_tn(r.gain_fine_left[:, cols], ones)] * 4)
    if summing:
        start_first(5)
    for copy in out_arrive:
        copy.wait()
    r.coarse_tokens[...] = gathered(
        "out", every, r.coarse_out[...], coarse_sizes, (LON, LAT, DIAG)
    ).astype(HALF)
    if summing:
        for p in (1, 2):
            collect(p, 1)
            start_third(p)
        collect_first(5)
        start_second(5)
        for p in (3, 4):
            collect_second(p)
            start_third(p)
        collect(0, 1)
        start_third(0)
    for name in ("end_own", "end_halo"):
        loads[name].wait()
    for copy in end_arrive:
        copy.wait()
    r.tokens_grad[...] = gathered(
        "end", every, r.tokens_back[...], fine_sizes, (LON, LAT, DIAG)
    ).astype(HALF)
    if summing:
        collect_second(5)
        start_third(5)
        for p in (1, 2, 0, 3, 4, 5):
            finish(p)
    else:
        for p in range(6):
            of(r, "sum", p)[...] = of(r, "share", p)[...].reshape(64, 16, WIDTHS[p])


LOADED = tuple(
    dict(
        in_pack=0,
        in_own=0,
        in_halo=0,
        qkv_f=0,
        proj_f=0,
        mid_pack=0,
        proj_c=0,
        mid_own=0,
        mid_halo=0,
        merge_w=0,
        qkv_c=0,
        back_pack=0,
        back_own=0,
        back_halo=0,
        end_pack=0,
        end_own=0,
        end_halo=0,
    )
)


def whole(values, summing):
    inputs, scratch, outputs = [], [], []

    def matrices(kind, rows, cols, source, target, sign):
        pack, own, halo, _ = roll_matrices(rows, cols, source, target, sign)
        return {
            kind + "_pack": jnp.asarray(pack, HALF),
            kind + "_own": jnp.asarray(own, HALF),
            kind + "_halo": jnp.asarray(halo, HALF),
        }

    values = dict(values)
    values.update(matrices("in", 12, 24, "natural", "window", 1))
    values.update(matrices("cot", 6, 12, "natural", "window", 1))
    values.update(matrices("mid", 12, 24, "window", "patch", 1))
    values.update(matrices("back", 12, 24, "patch", "window", -1))
    values.update(matrices("end", 12, 24, "window", "natural", -1))
    values.update(matrices("out", 6, 12, "window", "natural", -1))
    specs, operands = [], []
    for name, value in values.items():
        loaded = name in LOADED
        inputs.append(name + "_any" if loaded else name)
        specs.append(ANYWHERE if loaded else VMEM)
        operands.append(value)
    half = {name: values[name].shape for name in LOADED[:11]}
    for kind, width in (("in", 512), ("cot", 1024), ("mid", 512), ("back", 512), ("end", 512), ("out", 1024)):
        half[kind + "_landed"] = (PACKED, width)
    half.update(in_packed=(PACKED, 512), cot_packed=(PACKED, 1024), mid_packed=(PACKED, 512))
    lefts = dict(
        normal=(576, 256),
        attended=(576, 256),
        merged=(CELLS, 1024),
        normed=(CELLS, 512),
        coarse=(CELLS, 512),
        gain_coarse=(16, 512),
        gain_merge=(16, 1024),
        gain_fine=(16, 256),
    )
    for name, (count, width) in lefts.items():
        half[name + "_left"] = (2 * count, width)
        half[name + "_give"] = (count, width)
    half.update(
        kept=(16, CELLS, 2 * CELLS),
        rolled=(576, 512),
        qkv=(576, 1536),
        attended=(576, 512),
        fine_out=(576, 512),
        tokens_back=(576, 512),
        cot_right=(2 * CELLS, 1024),
        cot_attended=(CELLS, 1024),
        qkv_coarse=(CELLS, 3072),
        coarse_attended=(CELLS, 1024),
        coarse_out=(CELLS, 1024),
        merged=(CELLS, 2048),
        qkv_right=(2 * CELLS, 3072),
        inner_right=(2 * CELLS, 1024),
        fine_right=(1152, 512),
        triple_right=(1152, 1536),
    )
    for p, width in enumerate(WIDTHS):
        half["share" + str(p)] = (4, 2, 4, 2, 16, width)
        if summing:
            first, second = LEADS[p % 3]
            half["landed0_" + str(p)] = (3,) + first + (16, width)
            half["landed1_" + str(p)] = (3,) + second + (16, width)
            half["landed2_" + str(p)] = (3, 16, width)
    memory = {name: pltpu.VMEM(shape, HALF) for name, shape in half.items()}
    memory["unit_merge"] = pltpu.VMEM((CELLS, 2048), FULL)
    memory["scale_merge"] = pltpu.VMEM((CELLS, 1), FULL)
    memory["unit_coarse"] = pltpu.VMEM((CELLS, 1024), FULL)
    memory["send_sem"] = pltpu.SemaphoreType.DMA((150,))
    memory["recv_sem"] = pltpu.SemaphoreType.DMA((150,))
    memory["load_sem"] = pltpu.SemaphoreType.DMA((len(LOADED),))
    outputs = {
        "coarse_tokens": jax.ShapeDtypeStruct((CELLS, 1024), HALF),
        "tokens_grad": jax.ShapeDtypeStruct((576, 512), HALF),
    }
    for p, width in enumerate(WIDTHS):
        outputs["sum" + str(p)] = (
            jax.ShapeDtypeStruct((16, width), FULL)
            if summing
            else jax.ShapeDtypeStruct((64, 16, width), HALF)
        )
    names = tuple(inputs) + tuple(outputs) + tuple(memory)
    results = pl.pallas_call(
        functools.partial(whole_kernel, names, summing),
        out_shape=list(outputs.values()),
        in_specs=specs,
        out_specs=[VMEM] * len(outputs),
        scratch_shapes=list(memory.values()),
        compiler_params=pltpu.CompilerParams(
            collective_id=1, has_side_effects=True, vmem_limit_bytes=LIMIT
        ),
    )(*operands)
    return dict(zip(outputs, results))


def prepared(
    tokens,
    cotangent,
    gain_fine,
    qkv_fine,
    proj_fine,
    gain_merge,
    merge_weight,
    gain_coarse,
    qkv_coarse,
    proj_coarse,
):
    return dict(
        tokens=tokens.reshape(576, 512),
        cotangent=cotangent,
        gain_f=gain_fine.reshape(1, 512),
        gain_m=gain_merge.reshape(1, 2048),
        gain_c=gain_coarse.reshape(1, 1024),
        qkv_f=qkv_fine,
        proj_f=proj_fine,
        merge_w=merge_weight,
        qkv_c=qkv_coarse,
        proj_c=proj_coarse,
    )


def last_kernel(*refs):
    coarse, tokens, a, b, c, d, e, f = refs[:8]
    coarse_out, tokens_out, fine_gain, qkv_f, proj_f, merge_gain, merge, coarse_gain, qkv_c, proj_c = refs[8:]
    cells = coarse[...].astype(FULL)
    for n in range(12):
        coarse_out[n // 6, n % 6] = cells[WW * n : WW * n + WW].astype(HALF)
    tokens_out[...] = tokens[...]

    def across(column, count):
        row = lax.broadcasted_iota(jnp.int32, (16, 128), 0)
        lane = lax.broadcasted_iota(jnp.int32, (16, 128), 1)
        line = jnp.sum(jnp.where(row == lane, column, 0.0), axis=0, keepdims=True)
        return line[:, :count]

    block = a[:, 1024:]
    merge_gain[...] = across(jnp.broadcast_to(block[:, :1], (16, 128)), 16)
    coarse_gain[...] = across(jnp.broadcast_to(block[:, HD : HD + 1], (16, 128)), 8)
    fine_gain[...] = across(f[...], 4)
    merge[...] = a[:, :1024]
    for n in range(2):
        rows = slice(8 * n, 8 * n + 8)
        qkv_c[:, 1536 * n : 1536 * n + 1024] = b[rows, :]
        qkv_c[:, 1536 * n + 1024 : 1536 * n + 1536] = c[rows, :512]
        proj_c[:, 512 * n : 512 * n + 512] = c[rows, 512:]
    for n in range(4):
        rows = slice(4 * n, 4 * n + 4)
        qkv_f[:, 384 * n : 384 * n + 256] = d[rows, :]
        qkv_f[:, 384 * n + 256 : 384 * n + 384] = e[rows, :128]
        proj_f[:, 128 * n : 128 * n + 128] = e[rows, 128:]


def last(found):
    shapes = [jax.ShapeDtypeStruct((2, 6, WW, 1024), HALF), jax.ShapeDtypeStruct((576, 512), HALF)]
    shapes += [
        jax.ShapeDtypeStruct(shape, FULL)
        for shape in (
            (1, 4),
            (4, 1536),
            (4, 512),
            (1, 16),
            (16, 1024),
            (1, 8),
            (8, 3072),
            (8, 1024),
        )
    ]
    outs = pl.pallas_call(
        last_kernel, out_shape=shapes, in_specs=[VMEM] * 8, out_specs=[VMEM] * 10
    )(*found)
    outs = list(outs)
    outs[1] = outs[1].reshape(2, 12, 24, 512)
    for n in (2, 5, 7):
        outs[n] = outs[n].reshape(-1)
    return tuple(outs)


def local(*args):
    found = whole(prepared(*args), True)
    return last(tuple(found.values()))


def solution(mesh):
    grid = P(None, "lat", "lon", None)
    vector, matrix = P(("lat", "lon")), P(("lat", "lon"), None)
    return jax.shard_map(
        local,
        mesh=mesh,
        in_specs=(grid, grid) + (P(),) * 8,
        out_specs=(grid, grid, vector, matrix, matrix, vector, matrix, vector, matrix, matrix),
        check_vma=False,
    )
```

```python
import functools
from types import SimpleNamespace

import jax
import jax.numpy as jnp
import numpy as np
from jax import lax
from jax.experimental import pallas as pl
from jax.experimental.pallas import tpu as pltpu
from jax.sharding import PartitionSpec as P

MESH = pl.DeviceIdType.MESH
HALF = jnp.bfloat16
FULL = jnp.float32
HD = 64
WH = 6
WW = 12
CELLS = 144
EPSILON = 1e-05
MASKED = -1e30
PIECES = (0, 128, 256)
PACKED = 304
LIMIT = 62 * 1024 * 1024
VMEM = pl.BlockSpec(memory_space=pltpu.VMEM)
SMEM = pl.BlockSpec(memory_space=pltpu.SMEM)
ANYWHERE = pl.BlockSpec(memory_space=pl.ANY)


def dot(left, right):
    return jnp.dot(left, right, preferred_element_type=FULL)


def dot_nt(left, right):
    return lax.dot_general(left, right, (((1,), (1,)), ((), ())), preferred_element_type=FULL)


def dot_tn(left, right):
    return lax.dot_general(left, right, (((0,), (0,)), ((), ())), preferred_element_type=FULL)


def natural_order(rows, cols):
    return lambda level, i, j: (level * rows + i) * cols + j


def level_last_order(rows, cols):
    return lambda level, i, j: (i * cols + j) * 2 + level


def window_order(rows, cols):
    def place(level, i, j):
        window = i // WH * (cols // WW) + j // WW
        return window * CELLS + ((i % WH // 3 * 2 + level) * 3 + i % 3) * WW + j % WW

    return place


def patch_order(rows, cols):
    coarse = window_order(rows // 2, cols // 2)

    def place(level, i, j):
        return (j % 2 * 2 + i % 2) * CELLS + coarse(level, i // 2, j // 2)

    return place


@functools.lru_cache(maxsize=None)
def roll_matrices(rows, cols, source, target, sign):
    orders = {"last": level_last_order, "natural": natural_order, "window": window_order, "patch": patch_order}
    from_place, to_place = orders[source](rows, cols), orders[target](rows, cols)
    count = 2 * rows * cols
    pieces = ([], [], [])
    own = np.zeros((count, count), np.float32)
    for level in range(2):
        for i in range(rows):
            for j in range(cols):
                far_i, far_j = i + 3 * sign, j + 6 * sign
                across = (far_i // rows != 0, far_j // cols != 0)
                here = from_place(level, far_i % rows, far_j % cols)
                there = to_place(level, i, j)
                if across == (False, False):
                    own[there, here] = 1
                else:
                    slot = {(False, True): 0, (True, False): 1, (True, True): 2}[across]
                    pieces[slot].append((there, here))
    sizes = tuple((len(piece) + 15) // 16 * 16 for piece in pieces)
    pack = np.zeros((PACKED, count), np.float32)
    halo = np.zeros((count, PACKED), np.float32)
    for slot, piece in enumerate(pieces):
        for k, (there, here) in enumerate(piece):
            pack[PIECES[slot] + k, here] = 1
            halo[there, PIECES[slot] + k] = 1
    return pack, own, halo, sizes


def norm_parts(values):
    centre = jnp.mean(values, axis=-1, keepdims=True)
    offset = values - centre
    spread = jnp.mean(offset * offset, axis=-1, keepdims=True)
    scale = lax.rsqrt(spread + EPSILON)
    return offset * scale, scale


def norm_back(grad, normal, scale, gain):
    inner = grad * gain
    mean = jnp.mean(inner, axis=-1, keepdims=True)
    along = jnp.mean(inner * normal, axis=-1, keepdims=True)
    return (inner - mean - normal * along) * scale


def two_heads(pair):
    first = lax.broadcasted_iota(jnp.int32, pair.shape, 1) < HD
    zero = jnp.zeros_like(pair)
    return jnp.concatenate([jnp.where(first, pair, zero), jnp.where(first, zero, pair)], axis=0)


def one_pair(stack):
    half = stack.shape[0] // 2
    first = lax.broadcasted_iota(jnp.int32, (half, 2 * HD), 1) < HD
    return jnp.where(first, stack[:half], stack[half:])


def pair_mask(edge):
    shape = (CELLS, 2 * CELLS)
    key = lax.broadcasted_iota(jnp.int32, shape, 0)
    query = lax.broadcasted_iota(jnp.int32, shape, 1)
    query = jnp.where(query >= CELLS, query - CELLS, query)
    apart = (key < CELLS // 2) != (query < CELLS // 2)
    return jnp.where(apart, edge, 0) > 0


def pair_weights(queries, keys, mask):
    scores = dot_nt(keys, queries * 0.125)
    scores = jnp.where(mask, MASKED, scores)
    powers = jnp.exp(scores - jnp.max(scores, axis=0, keepdims=True))
    return powers * (1.0 / jnp.sum(powers, axis=0, keepdims=True))


def pair_forward(rounded, values):
    return one_pair(dot_tn(rounded, values)).astype(HALF)


def pair_back(weights, rounded, queries, keys, values, upstream):
    weight_grad = dot_nt(values, upstream)
    inner = jnp.sum(weights * weight_grad, axis=0, keepdims=True)
    score_grad = (weights * (weight_grad - inner) * 0.125).astype(HALF)
    query_grad = one_pair(dot_tn(score_grad, keys)).astype(HALF)
    key_grad = dot(score_grad, queries).astype(HALF)
    value_grad = dot(rounded, upstream).astype(HALF)
    return query_grad, key_grad, value_grad


def four_stacked(pieces):
    rows, width = pieces[0].shape
    shaped = [piece.reshape(rows // 8, 8, width) for piece in pieces]
    upper = lax.broadcasted_iota(jnp.int32, shaped[0].shape, 1) < 4
    turned = [pltpu.roll(piece, 4, 1) for piece in shaped]
    even = [jnp.where(upper, shaped[n], turned[n + 1]) for n in (0, 2)]
    odd = [jnp.where(upper, turned[n], shaped[n + 1]) for n in (0, 2)]
    return [jnp.concatenate(pair, axis=1).astype(HALF) for pair in (even, odd)]


ORDERS = (("x", "y", "z"), ("y", "z", "x"), ("z", "x", "y"))
LEADS = (((4, 2, 2), (2, 2)), ((2, 4, 2), (4,)), ((4, 4), (4,)))
WIDTHS = (1152, 1024, 1024, 256, 256, 128)
LON, LAT, DIAG = 0, 1, 2
STEPS = ((0, 1), (1, 0), (1, 1))


def device_at(place, core):
    lat = place["y"] * 2 + place["z"] // 2
    lon = place["x"] * 4 + place["z"] % 2 * 2 + core
    return (lat, lon)


def along(place, axis, steps):
    moved = dict(place)
    moved[axis] = lax.rem(place[axis] + steps, 4)
    return moved


def first_cut(kind, ref, index):
    if kind == 0:
        return ref.at[:, :, index]
    if kind == 1:
        return ref.at[index]
    return ref.at[:, index // 2, :, index % 2]


def second_cut(kind, ref, index):
    if kind == 0:
        return ref.at[index]
    if kind == 1:
        return ref.at[index // 2, :, index % 2]
    return ref.at[:, index]


def third_cut(kind, ref, index):
    if kind == 0:
        return ref.at[index // 2, index % 2]
    return ref.at[index]


def spots(lead, i):
    found = []
    for size in reversed(lead):
        found.insert(0, i % size)
        i = i // size
    return tuple(found)


def added(base, arrivals):
    total = base.astype(FULL)
    for arrival in arrivals:
        total = total + arrival.astype(FULL)
    return total


def of(r, name, p):
    return getattr(r, name + str(p))


def owner_pick(rows_each, core):
    shift = rows_each.bit_length() - 1
    feature = lax.broadcasted_iota(jnp.int32, (256, 128), 0)
    place = lax.broadcasted_iota(jnp.int32, (256, 128), 1)
    wanted = ((place >> shift) << (shift + 1)) + (place & (rows_each - 1)) + core * rows_each
    return jnp.where(feature == wanted, 1.0, 0.0).astype(HALF)


def in_two(row):
    high = row.astype(HALF)
    low = (row - high.astype(FULL)).astype(HALF)
    place = lax.broadcasted_iota(jnp.int32, (16, row.shape[1]), 0)
    wide_high = jnp.broadcast_to(high.astype(FULL), place.shape)
    wide_low = jnp.broadcast_to(low.astype(FULL), place.shape)
    return jnp.where(place == 0, wide_high, jnp.where(place == 1, wide_low, 0.0)).astype(HALF)


def whole_kernel(names, summing, *refs):
    r = SimpleNamespace(**dict(zip(names, refs)))
    lat, lon = lax.axis_index("lat"), lax.axis_index("lon")
    lats, lons = lax.axis_size("lat"), lax.axis_size("lon")
    core = lon % 2
    place = {"y": lat // 2, "x": lon // 4, "z": lat % 2 * 2 + lon // 2 % 2}
    sibling = (lat, lon + 1 - 2 * core)
    edge = jnp.where(lat == lats - 1, 1, 0)
    used = [0]

    def remote(source, target, device):
        slot = used[0]
        used[0] += 1
        copy = pltpu.make_async_remote_copy(
            src_ref=source,
            dst_ref=target,
            send_sem=r.send_sem.at[slot],
            recv_sem=r.recv_sem.at[slot],
            device_id=device,
            device_id_type=MESH,
        )
        copy.start()
        return copy

    def neighbour(step, way):
        return (
            lax.rem(lat + lats + way * step[0], lats),
            lax.rem(lon + lons + way * step[1], lons),
        )

    loads = {}

    def load(name):
        slot = LOADED.index(name)
        loads[name] = pltpu.make_async_copy(getattr(r, name + "_any"), getattr(r, name), r.load_sem.at[slot])
        loads[name].start()

    for kind, held in (("back", "in"), ("end", "mid")):
        for matrix in ("_pack", "_own", "_halo"):
            setattr(r, kind + matrix, getattr(r, held + matrix))
    r.patches_grad = r.fine_out
    r.normal, r.cot_flat, r.wide = r.tokens_back, r.coarse_attended, r.unit_coarse
    r.back_packed, r.end_packed, r.out_packed = r.in_packed, r.mid_packed, r.cot_packed
    for name in LOADED[:6]:
        load(name)

    for landed, size in (
        (r.in_landed, 112),
        (r.mid_landed, 112),
        (r.back_landed, 112),
        (r.end_landed, 112),
        (r.cot_landed, 48),
        (r.out_landed, 48),
    ):
        for start in PIECES[:2]:
            landed[start + size : start + 128, :] = jnp.zeros((128 - size, landed.shape[1]), HALF)

    barrier = pltpu.get_barrier_semaphore()
    partners = [neighbour(step, way) for step in STEPS for way in (1, -1)] + [sibling]
    if summing:
        partners += [
            device_at(along(place, axis, k), core) for axis in ("x", "y", "z") for k in (1, 2, 3)
        ]
    for partner in partners:
        pl.semaphore_signal(barrier, inc=1, device_id=partner, device_id_type=MESH)

    def pack_piece(kind, value, slot, size):
        rows = slice(PIECES[slot], PIECES[slot] + size)
        getattr(r, kind + "_packed")[rows, :] = dot(getattr(r, kind + "_pack")[rows, :], value).astype(HALF)

    def send_piece(kind, slot, size, sign):
        rows = pl.ds(PIECES[slot], size)
        return remote(
            getattr(r, kind + "_packed").at[rows],
            getattr(r, kind + "_landed").at[rows],
            neighbour(STEPS[slot], -sign),
        )

    def gathered(kind, rows, value, sizes, needed):
        total = dot(getattr(r, kind + "_own")[rows, :], value)
        if len(needed) == 3:
            return total + dot(getattr(r, kind + "_halo")[rows, :], getattr(r, kind + "_landed")[...])
        for slot in needed:
            piece = slice(PIECES[slot], PIECES[slot] + sizes[slot])
            total = total + dot(getattr(r, kind + "_halo")[rows, piece], getattr(r, kind + "_landed")[piece, :])
        return total

    fine_sizes, coarse_sizes = (112, 112, 48), (48, 48, 48)
    loads["in_pack"].wait()
    for slot in (LAT, DIAG, LON):
        pack_piece("in", r.tokens[...], slot, fine_sizes[slot])
    pl.semaphore_wait(barrier, len(partners))
    arrive = {slot: send_piece("in", slot, fine_sizes[slot], 1) for slot in (LAT, DIAG, LON)}
    for n in range(12):
        r.wide[WW * n : WW * n + WW, :] = r.cotangent[n // 6, n % 6].astype(FULL)
    cotangent = r.wide[...].astype(HALF)
    r.cot_flat[...] = cotangent
    for slot in (LAT, DIAG, LON):
        pack_piece("cot", cotangent, slot, coarse_sizes[slot])
    r.fine_out[...] = jnp.zeros_like(r.fine_out)

    pick4, pick8, pick16 = (
        jnp.concatenate([owner_pick(n, core), owner_pick(n, 1 - core)], axis=1) for n in (4, 8, 16)
    )

    def split(value, pick, name, rows):
        for block in range(value.shape[1] // 256):
            parts = dot(value[:, 256 * block : 256 * block + 256], pick).astype(HALF)
            cols = slice(128 * block, 128 * block + 128)
            getattr(r, name + "_left")[rows, cols] = parts[:, :128]
            getattr(r, name + "_give")[rows, cols] = parts[:, 128:]

    def hand_left(name):
        count = getattr(r, name + "_give").shape[0]
        return remote(getattr(r, name + "_give"), getattr(r, name + "_left").at[pl.ds(count, count)], sibling)

    def hand_right(name, start, size):
        half = getattr(r, name).shape[0] // 2
        held = getattr(r, name)
        return remote(held.at[pl.ds(start, size)], held.at[pl.ds(half + start, size)], sibling)

    handed_fine, handed_coarse, late = [], [], []

    needs = ((), (LON,), (LAT,), (LON, LAT, DIAG))
    waited = set()
    mid_arrive = []
    for name in LOADED[1:6]:
        loads[name].wait()
    for name in LOADED[6:11]:
        load(name)
    for w in range(4):
        for slot in needs[w]:
            if slot not in waited:
                arrive[slot].wait()
                waited.add(slot)
        rows = slice(CELLS * w, CELLS * w + CELLS)
        values = gathered("in", rows, r.tokens[...], fine_sizes, needs[w])
        r.rolled[rows, :] = values.astype(HALF)
        unit, _ = norm_parts(values)
        normed = (unit * r.gain_f[...]).astype(HALF)
        r.normal[rows, :] = normed
        qkv = r.qkv
        for n in range(3):
            cols = slice(512 * n, 512 * n + 512)
            qkv[rows, cols] = dot(normed, r.qkv_f[:, cols]).astype(HALF)
        mask = pair_mask(edge if w >= 2 else 0)
        for p in range(4):
            at = 128 * p
            queries = two_heads(qkv[rows, at : at + 128])
            weights = pair_weights(queries, qkv[rows, 512 + at : 640 + at], mask)
            rounded = weights.astype(HALF)
            r.kept[4 * w + p] = rounded
            r.attended[rows, at : at + 128] = pair_forward(
                rounded, qkv[rows, 1024 + at : 1152 + at]
            )
        attended = r.attended[rows, :]
        r.fine_out[rows, :] = (values + dot(attended, r.proj_f[...])).astype(HALF)
        for slot in {1: (LAT,), 2: (DIAG, LON)}.get(w, ()):
            pack_piece("mid", r.fine_out[...], slot, fine_sizes[slot])
            mid_arrive.append(send_piece("mid", slot, fine_sizes[slot], 1))
        if w == 2:
            cot_arrive = [send_piece("cot", n, coarse_sizes[n], 1) for n in (LAT, DIAG, LON)]
    rows = slice(0, 576)
    split(r.normal[...], pick4, "normal", rows)
    split(r.attended[...], pick4, "attended", rows)
    handed_fine += [hand_left("normal"), hand_left("attended")]
    for name in LOADED[11:14]:
        load(name)

    every, own = slice(None), slice(0, CELLS)
    loads["mid_own"].wait()
    loads["mid_halo"].wait()
    for copy in mid_arrive:
        copy.wait()
    values = jnp.concatenate(
        [
            gathered(
                "mid",
                slice(CELLS * g, CELLS * g + CELLS),
                r.fine_out[...],
                fine_sizes,
                (LON, LAT, DIAG),
            )
            for g in range(4)
        ],
        axis=1,
    )
    for name in LOADED[14:]:
        load(name)
    unit, scale_merge = norm_parts(values)
    r.unit_merge[...] = unit
    merged = (unit * r.gain_m[...]).astype(HALF)
    loads["merge_w"].wait()
    coarse_in = dot(merged, r.merge_w[...]).astype(HALF).astype(FULL)
    split(merged, pick16, "merged", own)
    merged_handed = hand_left("merged")
    unit, scale_coarse = norm_parts(coarse_in)
    r.unit_coarse[...] = unit
    normed = (unit * r.gain_c[...]).astype(HALF)
    loads["qkv_c"].wait()
    for n in range(3):
        cols = slice(1024 * n, 1024 * (n + 1))
        r.qkv_coarse[:, cols] = dot(normed, r.qkv_c[:, cols]).astype(HALF)
    split(normed, pick8, "normed", own)
    handed_coarse.append(hand_left("normed"))
    for copy in cot_arrive:
        copy.wait()
    cot = gathered("cot", every, r.cot_flat[...], coarse_sizes, (LON, LAT, DIAG)).astype(HALF)
    r.cot_right[own, :] = cot
    handed_coarse.append(hand_right("cot_right", 0, CELLS))
    loads["proj_c"].wait()
    r.cot_attended[...] = dot_nt(cot, r.proj_c[...]).astype(HALF)
    qkv = r.qkv_coarse
    mask = pair_mask(edge)
    for p in range(8):
        at = 128 * p
        queries = two_heads(qkv[:, at : at + 128])
        keys, worth = qkv[:, 1024 + at : 1152 + at], qkv[:, 2048 + at : 2176 + at]
        weights = pair_weights(queries, keys, mask)
        rounded = weights.astype(HALF)
        r.coarse_attended[:, at : at + 128] = pair_forward(rounded, worth)
        upstream = two_heads(r.cot_attended[:, at : at + 128])
        grads = pair_back(weights, rounded, queries, keys, worth, upstream)
        for n in range(3):
            r.qkv_right[own, 1024 * n + at : 1024 * n + at + 128] = grads[n]
    handed_coarse.append(hand_right("qkv_right", 0, CELLS))
    attended = r.coarse_attended[...]
    split(attended, pick8, "coarse", own)
    handed_coarse.append(hand_left("coarse"))
    normed_grad = dot_nt(r.qkv_right[own, :], r.qkv_c[...]).astype(HALF).astype(FULL)
    gain_row = jnp.sum(normed_grad * r.unit_coarse[...], axis=0, keepdims=True)
    split(in_two(gain_row), pick8, "gain_coarse", slice(0, 16))
    gains_handed = [hand_left("gain_coarse")]
    coarse_grad = r.cot_right[own, :].astype(FULL) + norm_back(
        normed_grad, r.unit_coarse[...], scale_coarse, r.gain_c[...]
    )
    r.inner_right[own, :] = coarse_grad.astype(HALF)
    inner_handed = hand_right("inner_right", 0, CELLS)
    merged_grad = dot_nt(r.inner_right[own, :], r.merge_w[...]).astype(HALF).astype(FULL)
    gain_row = jnp.sum(merged_grad * r.unit_merge[...], axis=0, keepdims=True)
    split(in_two(gain_row), pick16, "gain_merge", slice(0, 16))
    gains_handed.append(hand_left("gain_merge"))
    back = norm_back(merged_grad, r.unit_merge[...], scale_merge, r.gain_m[...]).astype(HALF)
    for g in range(4):
        r.patches_grad[CELLS * g : CELLS * (g + 1), :] = back[:, 512 * g : 512 * (g + 1)]
    for name in ("back_pack", "back_own", "back_halo"):
        loads[name].wait()
    back_arrive = {}
    for slot in (LAT, DIAG, LON):
        pack_piece("back", r.patches_grad[...], slot, fine_sizes[slot])
        back_arrive[slot] = send_piece("back", slot, fine_sizes[slot], -1)
    r.coarse_out[...] = (coarse_in + dot(attended, r.proj_c[...])).astype(HALF)
    for slot in (LAT, DIAG, LON):
        pack_piece("out", r.coarse_out[...], slot, coarse_sizes[slot])

    sums = {}

    def across(axis):
        mine = place[axis]
        near, far = mine + 1 - 2 * (mine % 2), 3 - mine
        return mine, ((near, far), (far, near))

    def there(axis, index):
        return device_at({**place, axis: index}, core)

    def stage_of(p, stage):
        landed = of(r, ("landed0_", "landed1_")[stage], p)
        lead = LEADS[p % 3][stage]
        size = int(np.prod(lead))
        if stage == 0:
            source = lambda index: first_cut(p % 3, of(r, "share", p), index)
        else:
            source = lambda index: second_cut(p % 3, of(r, "landed0_", p).at[1], index)
        return source, landed, lead, size, ORDERS[p % 3][stage]

    def halves(lead):
        return [pl.ds(h * (lead[0] // 2), lead[0] // 2) for h in range(2)]

    def begin(p, stage):
        source, landed, lead, size, axis = stage_of(p, stage)
        mine, pairs = across(axis)
        sums[p] = {}
        for slot in range(2):
            for h, rows in enumerate(halves(lead)):
                one = pairs[h][0]
                quarter = lax.rem(mine + 2, 4) if slot == 0 else one
                sums[p][h, slot] = remote(
                    source(quarter).at[rows], landed.at[slot, rows], there(axis, one)
                )

    def forward(p, stage):
        source, landed, lead, size, axis = stage_of(p, stage)
        mine, pairs = across(axis)
        for h, rows in enumerate(halves(lead)):
            two = pairs[h][1]
            theirs = source(two)
            sums[p][h, 0].wait()

            def add(i, carry, h=h, theirs=theirs):
                at = spots(lead, i + h * (size // 2))
                landed[(0,) + at] = added(theirs[at], [landed[(0,) + at]]).astype(HALF)
                return carry

            for i in range(size // 2):
                add(i, 0)
            sums[p][h, 2] = remote(landed.at[0, rows], landed.at[2, rows], there(axis, two))

    def collect(p, stage):
        source, landed, lead, size, axis = stage_of(p, stage)
        mine = source(place[axis])
        for h in range(2):
            sums[p][h, 1].wait()
            sums[p][h, 2].wait()

        def add(i, carry):
            at = spots(lead, i)
            total = added(mine[at], [landed[(1,) + at], landed[(2,) + at]])
            landed[(1,) + at] = total.astype(HALF)
            return carry

        for i in range(size):
            add(i, 0)

    def start_first(p):
        axis = ORDERS[p % 3][0]
        sums[p] = []
        for k in (2, 1, 3):
            moved = along(place, axis, k)
            sums[p].append(
                remote(
                    first_cut(p % 3, of(r, "share", p), moved[axis]),
                    of(r, "landed0_", p).at[k - 1],
                    device_at(moved, core),
                )
            )

    def collect_first(p):
        source, landed, lead, size, axis = stage_of(p, 0)
        mine = source(place[axis])
        for copy in sums[p]:
            copy.wait()

        def add(i, carry):
            at = spots(lead, i)
            total = added(mine[at], [landed[(k,) + at] for k in range(3)])
            landed[(1,) + at] = total.astype(HALF)
            return carry

        for i in range(size):
            add(i, 0)

    def start_second(p):
        source, landed, lead, size, axis = stage_of(p, 1)
        sums[p] = []
        for k in (2, 1, 3):
            moved = along(place, axis, k)
            sums[p].append(
                remote(source(moved[axis]), landed.at[k - 1], device_at(moved, core))
            )

    def collect_second(p):
        source, landed, lead, size, axis = stage_of(p, 1)
        for copy in sums[p]:
            copy.wait()
        total = added(source(place[axis])[...], [landed[k] for k in range(3)])
        landed[1] = total.astype(HALF)

    def start_third(p):
        axis = ORDERS[p % 3][2]
        sums[p] = []
        for k in (2, 1, 3):
            moved = along(place, axis, k)
            sums[p].append(
                remote(
                    third_cut(p % 3, of(r, "landed1_", p).at[1], moved[axis]),
                    of(r, "landed2_", p).at[k - 1],
                    device_at(moved, core),
                )
            )

    def finish(p):
        for copy in sums[p]:
            copy.wait()
        mine = third_cut(p % 3, of(r, "landed1_", p).at[1], place[ORDERS[p % 3][2]])
        total = added(mine[...], [of(r, "landed2_", p)[k] for k in range(3)])
        of(r, "sum", p)[...] = total

    for copy in handed_coarse:
        copy.wait()

    def paired(grad, lead):
        width = grad.shape[1] // 2
        rows = grad.shape[0] // 8
        pieces = [grad[:, :width].reshape(rows, 8, width), grad[:, width:].reshape(rows, 8, width)]
        return jnp.concatenate(pieces, axis=1).astype(HALF).reshape(lead + (16, width))

    def qkv_rows(n, carry):
        cols = pl.ds(pl.multiple_of(n * 256, 256), 256)
        left = r.normed_left[:, cols]
        for low, share, at in ((0, 1, 0), (512, 1, 512), (1024, 2, 0)):
            right = jnp.concatenate(
                [
                    r.qkv_right[:, low : low + 512],
                    r.qkv_right[:, low + 1536 : low + 2048],
                ],
                axis=1,
            )
            of(r, "share", share)[pl.ds(n * 2, 2), :, :, :, :, at : at + 512] = paired(
                dot_tn(left, right), (2, 2, 4, 2)
            )
        grad = dot_tn(r.coarse_left[:, cols], r.cot_right[...])
        r.share2[pl.ds(n * 2, 2), :, :, :, :, 512:] = paired(grad, (2, 2, 4, 2))
        return carry

    lax.fori_loop(0, 2, qkv_rows, 0)
    if summing:
        begin(1, 0)
        begin(2, 0)
    for copy in gains_handed + [merged_handed, inner_handed]:
        copy.wait()
    ones = jnp.ones((32, 128), HALF)
    left_lane = lax.broadcasted_iota(jnp.int32, (64, 16, 128), 2) < HD
    by_merge = dot_tn(r.gain_merge_left[...], ones).reshape(64, 16, 128)
    by_coarse = dot_tn(r.gain_coarse_left[...], ones).reshape(64, 8, 128)
    by_coarse = jnp.concatenate([by_coarse, by_coarse], axis=1)
    gains = jnp.where(left_lane, by_merge, by_coarse).astype(HALF)
    r.share0[:, :, :, :, :, 1024:] = gains.reshape(4, 2, 4, 2, 16, 128)

    def merge_rows(n, carry):
        left = r.merged_left[:, pl.ds(pl.multiple_of(n * 256, 256), 256)]
        grad = dot_tn(left, r.inner_right[...])
        r.share0[n, :, :, :, :, :1024] = grad.astype(HALF).reshape(2, 4, 2, 16, 1024)
        return carry

    lax.fori_loop(0, 4, merge_rows, 0)
    if summing:
        begin(0, 0)

    needs = ((LON, LAT, DIAG), (LAT,), (LON,), ())
    waited = set()
    end_arrive = []
    for w in (3, 2, 1, 0):
        for slot in needs[w]:
            if slot not in waited:
                back_arrive[slot].wait()
                waited.add(slot)
        rows = slice(CELLS * w, CELLS * w + CELLS)
        grad = gathered("back", rows, r.patches_grad[...], fine_sizes, needs[w]).astype(HALF)
        r.fine_right[rows, :] = grad
        handed_fine.append(hand_right("fine_right", CELLS * w, CELLS))
        attended_grad = dot_nt(grad, r.proj_f[...]).astype(HALF)
        qkv = r.qkv
        for p in range(4):
            at = 128 * p
            queries = two_heads(qkv[rows, at : at + 128])
            keys, worth = qkv[rows, 512 + at : 640 + at], qkv[rows, 1024 + at : 1152 + at]
            rounded = r.kept[4 * w + p]
            upstream = two_heads(attended_grad[:, at : at + 128])
            grads = pair_back(rounded.astype(FULL), rounded, queries, keys, worth, upstream)
            for n in range(3):
                r.triple_right[rows, 512 * n + at : 512 * n + at + 128] = grads[n]
        handed_fine.append(hand_right("triple_right", CELLS * w, CELLS))
        if w == 3:
            out_arrive = [send_piece("out", n, coarse_sizes[n], -1) for n in (LAT, DIAG, LON)]
        if summing:
            for p in {2: (1, 2), 0: (0,)}.get(w, ()):
                forward(p, 0)
    for copy in handed_fine:
        copy.wait()

    def store(n, p, at, pieces):
        width = pieces[0].shape[1]
        for side, value in enumerate(four_stacked(pieces)):
            of(r, "share", p)[pl.ds(n * 2, 2), :, :, side, :, at : at + width] = value.reshape(
                2, 2, 4, 16, width
            )

    def fine_rows(n, carry):
        cols = pl.ds(pl.multiple_of(n * 128, 128), 128)
        grad = dot_tn(r.normal_left[:, cols], r.triple_right[...])
        store(n, 3, 0, [grad[:, 384 * m : 384 * m + 256] for m in range(4)])
        store(n, 4, 0, [grad[:, 384 * m + 256 : 384 * m + 384] for m in range(4)])
        grad = dot_tn(r.attended_left[:, cols], r.fine_right[...])
        store(n, 4, 128, [grad[:, 128 * m : 128 * m + 128] for m in range(4)])
        return carry

    lax.fori_loop(0, 2, fine_rows, 0)
    if summing:
        for p in (3, 4):
            start_first(p)
        for p in (1, 2):
            collect(p, 0)
            begin(p, 1)
    gain_row = jnp.zeros((1, 512), FULL)
    r.tokens_back[...] = jnp.zeros_like(r.tokens_back)
    for w in (3, 2, 1, 0):
        rows = slice(CELLS * w, CELLS * w + CELLS)
        normed_grad = dot_nt(r.triple_right[rows, :], r.qkv_f[...]).astype(HALF).astype(FULL)
        unit, scale = norm_parts(r.rolled[rows, :].astype(FULL))
        gain_row = gain_row + jnp.sum(normed_grad * unit, axis=0, keepdims=True)
        back = norm_back(normed_grad, unit, scale, r.gain_f[...])
        r.tokens_back[rows, :] = (r.fine_right[rows, :].astype(FULL) + back).astype(HALF)
        for slot in {2: (LAT,), 1: (DIAG, LON)}.get(w, ()):
            if not end_arrive:
                loads["end_pack"].wait()
            pack_piece("end", r.tokens_back[...], slot, fine_sizes[slot])
            end_arrive.append(send_piece("end", slot, fine_sizes[slot], -1))
        if summing and w == 2:
            collect(0, 0)
            begin(0, 1)
            forward(1, 1)
            forward(2, 1)
    split(in_two(gain_row), pick4, "gain_fine", slice(0, 16))
    gain_handed = hand_left("gain_fine")
    if summing:
        for p in (3, 4):
            collect_first(p)
            start_second(p)
        forward(0, 1)
    gain_handed.wait()
    for n in range(2):
        cols = slice(128 * n, 128 * n + 128)
        store(n, 5, 0, [dot_tn(r.gain_fine_left[:, cols], ones)] * 4)
    if summing:
        start_first(5)
    for copy in out_arrive:
        copy.wait()
    r.coarse_tokens[...] = gathered(
        "out", every, r.coarse_out[...], coarse_sizes, (LON, LAT, DIAG)
    ).astype(HALF)
    if summing:
        for p in (1, 2):
            collect(p, 1)
            start_third(p)
        collect_first(5)
        start_second(5)
        for p in (3, 4):
            collect_second(p)
            start_third(p)
        collect(0, 1)
        start_third(0)
    for name in ("end_own", "end_halo"):
        loads[name].wait()
    for copy in end_arrive:
        copy.wait()
    r.tokens_grad[...] = gathered(
        "end", every, r.tokens_back[...], fine_sizes, (LON, LAT, DIAG)
    ).astype(HALF)
    if summing:
        collect_second(5)
        start_third(5)
        for p in (1, 2, 0, 3, 4, 5):
            finish(p)
    else:
        for p in range(6):
            of(r, "sum", p)[...] = of(r, "share", p)[...].reshape(64, 16, WIDTHS[p])


LOADED = tuple(
    dict(
        in_pack=0,
        in_own=0,
        in_halo=0,
        qkv_f=0,
        proj_f=0,
        mid_pack=0,
        proj_c=0,
        mid_own=0,
        mid_halo=0,
        merge_w=0,
        qkv_c=0,
        back_pack=0,
        back_own=0,
        back_halo=0,
        end_pack=0,
        end_own=0,
        end_halo=0,
    )
)


def whole(values, summing):
    inputs, scratch, outputs = [], [], []

    def matrices(kind, rows, cols, source, target, sign):
        pack, own, halo, _ = roll_matrices(rows, cols, source, target, sign)
        return {
            kind + "_pack": jnp.asarray(pack, HALF),
            kind + "_own": jnp.asarray(own, HALF),
            kind + "_halo": jnp.asarray(halo, HALF),
        }

    values = dict(values)
    values.update(matrices("in", 12, 24, "natural", "window", 1))
    values.update(matrices("cot", 6, 12, "natural", "window", 1))
    values.update(matrices("mid", 12, 24, "window", "patch", 1))
    values.update(matrices("back", 12, 24, "patch", "window", -1))
    values.update(matrices("end", 12, 24, "window", "natural", -1))
    values.update(matrices("out", 6, 12, "window", "natural", -1))
    specs, operands = [], []
    for name, value in values.items():
        loaded = name in LOADED
        inputs.append(name + "_any" if loaded else name)
        specs.append(ANYWHERE if loaded else VMEM)
        operands.append(value)
    half = {name: values[name].shape for name in LOADED[:11]}
    for kind, width in (("in", 512), ("cot", 1024), ("mid", 512), ("back", 512), ("end", 512), ("out", 1024)):
        half[kind + "_landed"] = (PACKED, width)
    half.update(in_packed=(PACKED, 512), cot_packed=(PACKED, 1024), mid_packed=(PACKED, 512))
    lefts = dict(
        normal=(576, 256),
        attended=(576, 256),
        merged=(CELLS, 1024),
        normed=(CELLS, 512),
        coarse=(CELLS, 512),
        gain_coarse=(16, 512),
        gain_merge=(16, 1024),
        gain_fine=(16, 256),
    )
    for name, (count, width) in lefts.items():
        half[name + "_left"] = (2 * count, width)
        half[name + "_give"] = (count, width)
    half.update(
        kept=(16, CELLS, 2 * CELLS),
        rolled=(576, 512),
        qkv=(576, 1536),
        attended=(576, 512),
        fine_out=(576, 512),
        tokens_back=(576, 512),
        cot_right=(2 * CELLS, 1024),
        cot_attended=(CELLS, 1024),
        qkv_coarse=(CELLS, 3072),
        coarse_attended=(CELLS, 1024),
        coarse_out=(CELLS, 1024),
        qkv_right=(2 * CELLS, 3072),
        inner_right=(2 * CELLS, 1024),
        fine_right=(1152, 512),
        triple_right=(1152, 1536),
    )
    for p, width in enumerate(WIDTHS):
        half["share" + str(p)] = (4, 2, 4, 2, 16, width)
        if summing:
            first, second = LEADS[p % 3]
            half["landed0_" + str(p)] = (3,) + first + (16, width)
            half["landed1_" + str(p)] = (3,) + second + (16, width)
            half["landed2_" + str(p)] = (3, 16, width)
    memory = {name: pltpu.VMEM(shape, HALF) for name, shape in half.items()}
    memory["unit_merge"] = pltpu.VMEM((CELLS, 2048), FULL)
    memory["unit_coarse"] = pltpu.VMEM((CELLS, 1024), FULL)
    memory["send_sem"] = pltpu.SemaphoreType.DMA((150,))
    memory["recv_sem"] = pltpu.SemaphoreType.DMA((150,))
    memory["load_sem"] = pltpu.SemaphoreType.DMA((len(LOADED),))
    outputs = {
        "coarse_tokens": jax.ShapeDtypeStruct((CELLS, 1024), HALF),
        "tokens_grad": jax.ShapeDtypeStruct((576, 512), HALF),
    }
    for p, width in enumerate(WIDTHS):
        outputs["sum" + str(p)] = (
            jax.ShapeDtypeStruct((16, width), FULL)
            if summing
            else jax.ShapeDtypeStruct((64, 16, width), HALF)
        )
    names = tuple(inputs) + tuple(outputs) + tuple(memory)
    results = pl.pallas_call(
        functools.partial(whole_kernel, names, summing),
        out_shape=list(outputs.values()),
        in_specs=specs,
        out_specs=[VMEM] * len(outputs),
        scratch_shapes=list(memory.values()),
        compiler_params=pltpu.CompilerParams(
            collective_id=1, has_side_effects=True, vmem_limit_bytes=LIMIT
        ),
    )(*operands)
    return dict(zip(outputs, results))


def prepared(
    tokens,
    cotangent,
    gain_fine,
    qkv_fine,
    proj_fine,
    gain_merge,
    merge_weight,
    gain_coarse,
    qkv_coarse,
    proj_coarse,
):
    return dict(
        tokens=tokens.reshape(576, 512),
        cotangent=cotangent,
        gain_f=gain_fine.reshape(1, 512),
        gain_m=gain_merge.reshape(1, 2048),
        gain_c=gain_coarse.reshape(1, 1024),
        qkv_f=qkv_fine,
        proj_f=proj_fine,
        merge_w=merge_weight,
        qkv_c=qkv_coarse,
        proj_c=proj_coarse,
    )


def last_kernel(*refs):
    coarse, tokens, a, b, c, d, e, f = refs[:8]
    coarse_out, tokens_out, fine_gain, qkv_f, proj_f, merge_gain, merge, coarse_gain, qkv_c, proj_c = refs[8:]
    cells = coarse[...].astype(FULL)
    for n in range(12):
        coarse_out[n // 6, n % 6] = cells[WW * n : WW * n + WW].astype(HALF)
    tokens_out[...] = tokens[...]

    def across(column, count):
        row = lax.broadcasted_iota(jnp.int32, (16, 128), 0)
        lane = lax.broadcasted_iota(jnp.int32, (16, 128), 1)
        line = jnp.sum(jnp.where(row == lane, column, 0.0), axis=0, keepdims=True)
        return line[:, :count]

    block = a[:, 1024:]
    merge_gain[...] = across(jnp.broadcast_to(block[:, :1], (16, 128)), 16)
    coarse_gain[...] = across(jnp.broadcast_to(block[:, HD : HD + 1], (16, 128)), 8)
    fine_gain[...] = across(f[...], 4)
    merge[...] = a[:, :1024]
    for n in range(2):
        rows = slice(8 * n, 8 * n + 8)
        qkv_c[:, 1536 * n : 1536 * n + 1024] = b[rows, :]
        qkv_c[:, 1536 * n + 1024 : 1536 * n + 1536] = c[rows, :512]
        proj_c[:, 512 * n : 512 * n + 512] = c[rows, 512:]
    for n in range(4):
        rows = slice(4 * n, 4 * n + 4)
        qkv_f[:, 384 * n : 384 * n + 256] = d[rows, :]
        qkv_f[:, 384 * n + 256 : 384 * n + 384] = e[rows, :128]
        proj_f[:, 128 * n : 128 * n + 128] = e[rows, 128:]


def last(found):
    shapes = [jax.ShapeDtypeStruct((2, 6, WW, 1024), HALF), jax.ShapeDtypeStruct((576, 512), HALF)]
    shapes += [
        jax.ShapeDtypeStruct(shape, FULL)
        for shape in (
            (1, 4),
            (4, 1536),
            (4, 512),
            (1, 16),
            (16, 1024),
            (1, 8),
            (8, 3072),
            (8, 1024),
        )
    ]
    outs = pl.pallas_call(
        last_kernel, out_shape=shapes, in_specs=[VMEM] * 8, out_specs=[VMEM] * 10
    )(*found)
    outs = list(outs)
    outs[1] = outs[1].reshape(2, 12, 24, 512)
    for n in (2, 5, 7):
        outs[n] = outs[n].reshape(-1)
    return tuple(outs)


def local(*args):
    found = whole(prepared(*args), True)
    return last(tuple(found.values()))


def solution(mesh):
    grid = P(None, "lat", "lon", None)
    vector, matrix = P(("lat", "lon")), P(("lat", "lon"), None)
    return jax.shard_map(
        local,
        mesh=mesh,
        in_specs=(grid, grid) + (P(),) * 8,
        out_specs=(grid, grid, vector, matrix, matrix, vector, matrix, vector, matrix, matrix),
        check_vma=False,
    )
```

```python
import functools
from types import SimpleNamespace

import jax
import jax.numpy as jnp
import numpy as np
from jax import lax
from jax.experimental import pallas as pl
from jax.experimental.pallas import tpu as pltpu
from jax.sharding import PartitionSpec as P

MESH = pl.DeviceIdType.MESH
HALF = jnp.bfloat16
FULL = jnp.float32
HD = 64
WH = 6
WW = 12
CELLS = 144
EPSILON = 1e-05
MASKED = -1e30
PIECES = (0, 128, 256)
PACKED = 304
LIMIT = 62 * 1024 * 1024
VMEM = pl.BlockSpec(memory_space=pltpu.VMEM)
SMEM = pl.BlockSpec(memory_space=pltpu.SMEM)
ANYWHERE = pl.BlockSpec(memory_space=pl.ANY)


def dot(left, right):
    return jnp.dot(left, right, preferred_element_type=FULL)


def dot_nt(left, right):
    return lax.dot_general(left, right, (((1,), (1,)), ((), ())), preferred_element_type=FULL)


def dot_tn(left, right):
    return lax.dot_general(left, right, (((0,), (0,)), ((), ())), preferred_element_type=FULL)


def natural_order(rows, cols):
    return lambda level, i, j: (level * rows + i) * cols + j


def level_last_order(rows, cols):
    return lambda level, i, j: (i * cols + j) * 2 + level


def window_order(rows, cols):
    def place(level, i, j):
        window = i // WH * (cols // WW) + j // WW
        return window * CELLS + ((i % WH // 3 * 2 + level) * 3 + i % 3) * WW + j % WW

    return place


def patch_order(rows, cols):
    coarse = window_order(rows // 2, cols // 2)

    def place(level, i, j):
        return (j % 2 * 2 + i % 2) * CELLS + coarse(level, i // 2, j // 2)

    return place


@functools.lru_cache(maxsize=None)
def roll_matrices(rows, cols, source, target, sign):
    orders = {"last": level_last_order, "natural": natural_order, "window": window_order, "patch": patch_order}
    from_place, to_place = orders[source](rows, cols), orders[target](rows, cols)
    count = 2 * rows * cols
    pieces = ([], [], [])
    own = np.zeros((count, count), np.float32)
    for level in range(2):
        for i in range(rows):
            for j in range(cols):
                far_i, far_j = i + 3 * sign, j + 6 * sign
                across = (far_i // rows != 0, far_j // cols != 0)
                here = from_place(level, far_i % rows, far_j % cols)
                there = to_place(level, i, j)
                if across == (False, False):
                    own[there, here] = 1
                else:
                    slot = {(False, True): 0, (True, False): 1, (True, True): 2}[across]
                    pieces[slot].append((there, here))
    sizes = tuple((len(piece) + 15) // 16 * 16 for piece in pieces)
    pack = np.zeros((PACKED, count), np.float32)
    halo = np.zeros((count, PACKED), np.float32)
    for slot, piece in enumerate(pieces):
        for k, (there, here) in enumerate(piece):
            pack[PIECES[slot] + k, here] = 1
            halo[there, PIECES[slot] + k] = 1
    return pack, own, halo, sizes


def norm_parts(values):
    centre = jnp.mean(values, axis=-1, keepdims=True)
    offset = values - centre
    spread = jnp.mean(offset * offset, axis=-1, keepdims=True)
    scale = lax.rsqrt(spread + EPSILON)
    return offset * scale, scale


def norm_back(grad, normal, scale, gain):
    inner = grad * gain
    mean = jnp.mean(inner, axis=-1, keepdims=True)
    along = jnp.mean(inner * normal, axis=-1, keepdims=True)
    return (inner - mean - normal * along) * scale


def two_heads(pair):
    first = lax.broadcasted_iota(jnp.int32, pair.shape, 1) < HD
    zero = jnp.zeros_like(pair)
    return jnp.concatenate([jnp.where(first, pair, zero), jnp.where(first, zero, pair)], axis=0)


def one_pair(stack):
    half = stack.shape[0] // 2
    first = lax.broadcasted_iota(jnp.int32, (half, 2 * HD), 1) < HD
    return jnp.where(first, stack[:half], stack[half:])


def pair_mask(edge):
    shape = (CELLS, 2 * CELLS)
    key = lax.broadcasted_iota(jnp.int32, shape, 0)
    query = lax.broadcasted_iota(jnp.int32, shape, 1)
    query = jnp.where(query >= CELLS, query - CELLS, query)
    apart = (key < CELLS // 2) != (query < CELLS // 2)
    return jnp.where(apart, edge, 0) > 0


def pair_weights(queries, keys, mask):
    scores = dot_nt(keys, queries * 0.125)
    scores = jnp.where(mask, MASKED, scores)
    powers = jnp.exp(scores - jnp.max(scores, axis=0, keepdims=True))
    return powers * (1.0 / jnp.sum(powers, axis=0, keepdims=True))


def pair_forward(rounded, values):
    return one_pair(dot_tn(rounded, values)).astype(HALF)


def pair_back(weights, rounded, queries, keys, values, upstream):
    weight_grad = dot_nt(values, upstream)
    inner = jnp.sum(weights * weight_grad, axis=0, keepdims=True)
    score_grad = (weights * (weight_grad - inner) * 0.125).astype(HALF)
    query_grad = one_pair(dot_tn(score_grad, keys)).astype(HALF)
    key_grad = dot(score_grad, queries).astype(HALF)
    value_grad = dot(rounded, upstream).astype(HALF)
    return query_grad, key_grad, value_grad


def four_stacked(pieces):
    rows, width = pieces[0].shape
    shaped = [piece.reshape(rows // 8, 8, width) for piece in pieces]
    upper = lax.broadcasted_iota(jnp.int32, shaped[0].shape, 1) < 4
    turned = [pltpu.roll(piece, 4, 1) for piece in shaped]
    even = [jnp.where(upper, shaped[n], turned[n + 1]) for n in (0, 2)]
    odd = [jnp.where(upper, turned[n], shaped[n + 1]) for n in (0, 2)]
    return [jnp.concatenate(pair, axis=1).astype(HALF) for pair in (even, odd)]


ORDERS = (("x", "y", "z"), ("y", "z", "x"), ("z", "x", "y"))
LEADS = (((4, 2, 2), (2, 2)), ((2, 4, 2), (4,)), ((4, 4), (4,)))
WIDTHS = (1152, 1024, 1024, 256, 256, 128)
LON, LAT, DIAG = 0, 1, 2
STEPS = ((0, 1), (1, 0), (1, 1))


def device_at(place, core):
    lat = place["y"] * 2 + place["z"] // 2
    lon = place["x"] * 4 + place["z"] % 2 * 2 + core
    return (lat, lon)


def along(place, axis, steps):
    moved = dict(place)
    moved[axis] = lax.rem(place[axis] + steps, 4)
    return moved


def first_cut(kind, ref, index):
    if kind == 0:
        return ref.at[:, :, index]
    if kind == 1:
        return ref.at[index]
    return ref.at[:, index // 2, :, index % 2]


def second_cut(kind, ref, index):
    if kind == 0:
        return ref.at[index]
    if kind == 1:
        return ref.at[index // 2, :, index % 2]
    return ref.at[:, index]


def third_cut(kind, ref, index):
    if kind == 0:
        return ref.at[index // 2, index % 2]
    return ref.at[index]


def spots(lead, i):
    found = []
    for size in reversed(lead):
        found.insert(0, i % size)
        i = i // size
    return tuple(found)


def added(base, arrivals):
    total = base.astype(FULL)
    for arrival in arrivals:
        total = total + arrival.astype(FULL)
    return total


def of(r, name, p):
    return getattr(r, name + str(p))


def owner_pick(rows_each, core):
    shift = rows_each.bit_length() - 1
    feature = lax.broadcasted_iota(jnp.int32, (256, 128), 0)
    place = lax.broadcasted_iota(jnp.int32, (256, 128), 1)
    wanted = ((place >> shift) << (shift + 1)) + (place & (rows_each - 1)) + core * rows_each
    return jnp.where(feature == wanted, 1.0, 0.0).astype(HALF)


def in_two(row):
    high = row.astype(HALF)
    low = (row - high.astype(FULL)).astype(HALF)
    place = lax.broadcasted_iota(jnp.int32, (16, row.shape[1]), 0)
    wide_high = jnp.broadcast_to(high.astype(FULL), place.shape)
    wide_low = jnp.broadcast_to(low.astype(FULL), place.shape)
    return jnp.where(place == 0, wide_high, jnp.where(place == 1, wide_low, 0.0)).astype(HALF)


def whole_kernel(names, summing, *refs):
    r = SimpleNamespace(**dict(zip(names, refs)))
    lat, lon = lax.axis_index("lat"), lax.axis_index("lon")
    lats, lons = lax.axis_size("lat"), lax.axis_size("lon")
    core = lon % 2
    place = {"y": lat // 2, "x": lon // 4, "z": lat % 2 * 2 + lon // 2 % 2}
    sibling = (lat, lon + 1 - 2 * core)
    edge = jnp.where(lat == lats - 1, 1, 0)
    used = [0]

    def remote(source, target, device):
        slot = used[0]
        used[0] += 1
        copy = pltpu.make_async_remote_copy(
            src_ref=source,
            dst_ref=target,
            send_sem=r.send_sem.at[slot],
            recv_sem=r.recv_sem.at[slot],
            device_id=device,
            device_id_type=MESH,
        )
        copy.start()
        return copy

    def neighbour(step, way):
        return (
            lax.rem(lat + lats + way * step[0], lats),
            lax.rem(lon + lons + way * step[1], lons),
        )

    loads = {}

    def load(name):
        slot = LOADED.index(name)
        loads[name] = pltpu.make_async_copy(getattr(r, name + "_any"), getattr(r, name), r.load_sem.at[slot])
        loads[name].start()

    for kind, held in (("back", "in"), ("end", "mid")):
        for matrix in ("_pack", "_own", "_halo"):
            setattr(r, kind + matrix, getattr(r, held + matrix))
    r.patches_grad = r.fine_out
    r.normal, r.cot_flat, r.wide = r.tokens_back, r.coarse_attended, r.unit_coarse
    r.back_packed, r.end_packed, r.out_packed = r.in_packed, r.mid_packed, r.cot_packed
    for name in LOADED[:6]:
        load(name)

    for landed, size in (
        (r.in_landed, 112),
        (r.mid_landed, 112),
        (r.back_landed, 112),
        (r.end_landed, 112),
        (r.cot_landed, 48),
        (r.out_landed, 48),
    ):
        for start in PIECES[:2]:
            landed[start + size : start + 128, :] = jnp.zeros((128 - size, landed.shape[1]), HALF)

    barrier = pltpu.get_barrier_semaphore()
    partners = [neighbour(step, way) for step in STEPS for way in (1, -1)] + [sibling]
    if summing:
        partners += [
            device_at(along(place, axis, k), core) for axis in ("x", "y", "z") for k in (1, 2, 3)
        ]
    for partner in partners:
        pl.semaphore_signal(barrier, inc=1, device_id=partner, device_id_type=MESH)

    def pack_piece(kind, value, slot, size):
        rows = slice(PIECES[slot], PIECES[slot] + size)
        getattr(r, kind + "_packed")[rows, :] = dot(getattr(r, kind + "_pack")[rows, :], value).astype(HALF)

    def send_piece(kind, slot, size, sign):
        rows = pl.ds(PIECES[slot], size)
        return remote(
            getattr(r, kind + "_packed").at[rows],
            getattr(r, kind + "_landed").at[rows],
            neighbour(STEPS[slot], -sign),
        )

    def gathered(kind, rows, value, sizes, needed):
        total = dot(getattr(r, kind + "_own")[rows, :], value)
        if len(needed) == 3:
            return total + dot(getattr(r, kind + "_halo")[rows, :], getattr(r, kind + "_landed")[...])
        for slot in needed:
            piece = slice(PIECES[slot], PIECES[slot] + sizes[slot])
            total = total + dot(getattr(r, kind + "_halo")[rows, piece], getattr(r, kind + "_landed")[piece, :])
        return total

    fine_sizes, coarse_sizes = (112, 112, 48), (48, 48, 48)
    loads["in_pack"].wait()
    for slot in (LAT, DIAG, LON):
        pack_piece("in", r.tokens[...], slot, fine_sizes[slot])
    pl.semaphore_wait(barrier, len(partners))
    arrive = {slot: send_piece("in", slot, fine_sizes[slot], 1) for slot in (LAT, DIAG, LON)}
    for n in range(12):
        r.wide[WW * n : WW * n + WW, :] = r.cotangent[n // 6, n % 6].astype(FULL)
    cotangent = r.wide[...].astype(HALF)
    r.cot_flat[...] = cotangent
    for slot in (LAT, DIAG, LON):
        pack_piece("cot", cotangent, slot, coarse_sizes[slot])
    r.fine_out[...] = jnp.zeros_like(r.fine_out)

    pick4, pick8, pick16 = (
        jnp.concatenate([owner_pick(n, core), owner_pick(n, 1 - core)], axis=1) for n in (4, 8, 16)
    )

    def split(value, pick, name, rows):
        for block in range(value.shape[1] // 256):
            parts = dot(value[:, 256 * block : 256 * block + 256], pick).astype(HALF)
            cols = slice(128 * block, 128 * block + 128)
            getattr(r, name + "_left")[rows, cols] = parts[:, :128]
            getattr(r, name + "_give")[rows, cols] = parts[:, 128:]

    def hand_left(name):
        count = getattr(r, name + "_give").shape[0]
        return remote(getattr(r, name + "_give"), getattr(r, name + "_left").at[pl.ds(count, count)], sibling)

    def hand_right(name, start, size):
        half = getattr(r, name).shape[0] // 2
        held = getattr(r, name)
        return remote(held.at[pl.ds(start, size)], held.at[pl.ds(half + start, size)], sibling)

    handed_fine, handed_coarse, late = [], [], []

    needs = ((), (LON,), (LAT,), (LON, LAT, DIAG))
    waited = set()
    mid_arrive = []
    for name in LOADED[1:6]:
        loads[name].wait()
    for name in LOADED[6:11]:
        load(name)
    for w in range(4):
        for slot in needs[w]:
            if slot not in waited:
                arrive[slot].wait()
                waited.add(slot)
        rows = slice(CELLS * w, CELLS * w + CELLS)
        values = gathered("in", rows, r.tokens[...], fine_sizes, needs[w])
        r.rolled[rows, :] = values.astype(HALF)
        unit, _ = norm_parts(values)
        normed = (unit * r.gain_f[...]).astype(HALF)
        r.normal[rows, :] = normed
        qkv = r.qkv
        for n in range(3):
            cols = slice(512 * n, 512 * n + 512)
            qkv[rows, cols] = dot(normed, r.qkv_f[:, cols]).astype(HALF)
        mask = pair_mask(edge if w >= 2 else 0)
        for p in range(4):
            at = 128 * p
            queries = two_heads(qkv[rows, at : at + 128])
            weights = pair_weights(queries, qkv[rows, 512 + at : 640 + at], mask)
            rounded = weights.astype(HALF)
            r.kept[4 * w + p] = rounded
            r.attended[rows, at : at + 128] = pair_forward(
                rounded, qkv[rows, 1024 + at : 1152 + at]
            )
        attended = r.attended[rows, :]
        r.fine_out[rows, :] = (values + dot(attended, r.proj_f[...])).astype(HALF)
        for slot in {1: (LAT,), 2: (DIAG, LON)}.get(w, ()):
            pack_piece("mid", r.fine_out[...], slot, fine_sizes[slot])
            mid_arrive.append(send_piece("mid", slot, fine_sizes[slot], 1))
        if w == 2:
            cot_arrive = [send_piece("cot", n, coarse_sizes[n], 1) for n in (LAT, DIAG, LON)]
    rows = slice(0, 576)
    split(r.normal[...], pick4, "normal", rows)
    split(r.attended[...], pick4, "attended", rows)
    handed_fine += [hand_left("normal"), hand_left("attended")]
    for name in LOADED[11:14]:
        load(name)

    every, own = slice(None), slice(0, CELLS)
    loads["mid_own"].wait()
    loads["mid_halo"].wait()
    for copy in mid_arrive:
        copy.wait()
    values = jnp.concatenate(
        [
            gathered(
                "mid",
                slice(CELLS * g, CELLS * g + CELLS),
                r.fine_out[...],
                fine_sizes,
                (LON, LAT, DIAG),
            )
            for g in range(4)
        ],
        axis=1,
    )
    for name in LOADED[14:]:
        load(name)
    unit, scale_merge = norm_parts(values)
    r.unit_merge[...] = unit
    merged = (unit * r.gain_m[...]).astype(HALF)
    loads["merge_w"].wait()
    coarse_in = dot(merged, r.merge_w[...]).astype(HALF).astype(FULL)
    split(merged, pick16, "merged", own)
    merged_handed = hand_left("merged")
    unit, scale_coarse = norm_parts(coarse_in)
    r.unit_coarse[...] = unit
    normed = (unit * r.gain_c[...]).astype(HALF)
    loads["qkv_c"].wait()
    for n in range(3):
        cols = slice(1024 * n, 1024 * (n + 1))
        r.qkv_coarse[:, cols] = dot(normed, r.qkv_c[:, cols]).astype(HALF)
    split(normed, pick8, "normed", own)
    handed_coarse.append(hand_left("normed"))
    for copy in cot_arrive:
        copy.wait()
    cot = gathered("cot", every, r.cot_flat[...], coarse_sizes, (LON, LAT, DIAG)).astype(HALF)
    r.cot_right[own, :] = cot
    handed_coarse.append(hand_right("cot_right", 0, CELLS))
    loads["proj_c"].wait()
    r.cot_attended[...] = dot_nt(cot, r.proj_c[...]).astype(HALF)
    qkv = r.qkv_coarse
    mask = pair_mask(edge)
    for p in range(8):
        at = 128 * p
        queries = two_heads(qkv[:, at : at + 128])
        keys, worth = qkv[:, 1024 + at : 1152 + at], qkv[:, 2048 + at : 2176 + at]
        weights = pair_weights(queries, keys, mask)
        rounded = weights.astype(HALF)
        r.coarse_attended[:, at : at + 128] = pair_forward(rounded, worth)
        upstream = two_heads(r.cot_attended[:, at : at + 128])
        grads = pair_back(weights, rounded, queries, keys, worth, upstream)
        for n in range(3):
            r.qkv_right[own, 1024 * n + at : 1024 * n + at + 128] = grads[n]
    handed_coarse.append(hand_right("qkv_right", 0, CELLS))
    attended = r.coarse_attended[...]
    split(attended, pick8, "coarse", own)
    handed_coarse.append(hand_left("coarse"))
    normed_grad = dot_nt(r.qkv_right[own, :], r.qkv_c[...]).astype(HALF).astype(FULL)
    gain_row = jnp.sum(normed_grad * r.unit_coarse[...], axis=0, keepdims=True)
    split(in_two(gain_row), pick8, "gain_coarse", slice(0, 16))
    gains_handed = [hand_left("gain_coarse")]
    coarse_grad = r.cot_right[own, :].astype(FULL) + norm_back(
        normed_grad, r.unit_coarse[...], scale_coarse, r.gain_c[...]
    )
    r.inner_right[own, :] = coarse_grad.astype(HALF)
    inner_handed = hand_right("inner_right", 0, CELLS)
    merged_grad = dot_nt(r.inner_right[own, :], r.merge_w[...]).astype(HALF).astype(FULL)
    gain_row = jnp.sum(merged_grad * r.unit_merge[...], axis=0, keepdims=True)
    split(in_two(gain_row), pick16, "gain_merge", slice(0, 16))
    gains_handed.append(hand_left("gain_merge"))
    back = norm_back(merged_grad, r.unit_merge[...], scale_merge, r.gain_m[...]).astype(HALF)
    for g in range(4):
        r.patches_grad[CELLS * g : CELLS * (g + 1), :] = back[:, 512 * g : 512 * (g + 1)]
    for name in ("back_pack", "back_own", "back_halo"):
        loads[name].wait()
    back_arrive = {}
    for slot in (LAT, DIAG, LON):
        pack_piece("back", r.patches_grad[...], slot, fine_sizes[slot])
        back_arrive[slot] = send_piece("back", slot, fine_sizes[slot], -1)
    r.coarse_out[...] = (coarse_in + dot(attended, r.proj_c[...])).astype(HALF)
    for slot in (LAT, DIAG, LON):
        pack_piece("out", r.coarse_out[...], slot, coarse_sizes[slot])

    sums = {}

    def stage_of(p, stage):
        landed = of(r, ("landed0_", "landed1_")[stage], p)
        lead = LEADS[p % 3][stage]
        size = int(np.prod(lead))
        if stage == 0:
            source = lambda index: first_cut(p % 3, of(r, "share", p), index)
        else:
            source = lambda index: second_cut(p % 3, of(r, "landed0_", p).at[1], index)
        return source, landed, lead, size, ORDERS[p % 3][stage]

    def start_first(p):
        axis = ORDERS[p % 3][0]
        sums[p] = []
        for k in (2, 1, 3):
            moved = along(place, axis, k)
            sums[p].append(
                remote(
                    first_cut(p % 3, of(r, "share", p), moved[axis]),
                    of(r, "landed0_", p).at[k - 1],
                    device_at(moved, core),
                )
            )

    def collect_first(p):
        source, landed, lead, size, axis = stage_of(p, 0)
        mine = source(place[axis])
        for copy in sums[p]:
            copy.wait()

        def add(i, carry):
            at = spots(lead, i)
            total = added(mine[at], [landed[(k,) + at] for k in range(3)])
            landed[(1,) + at] = total.astype(HALF)
            return carry

        for i in range(size):
            add(i, 0)

    def start_second(p):
        source, landed, lead, size, axis = stage_of(p, 1)
        sums[p] = []
        for k in (2, 1, 3):
            moved = along(place, axis, k)
            sums[p].append(
                remote(source(moved[axis]), landed.at[k - 1], device_at(moved, core))
            )

    def collect_second(p):
        source, landed, lead, size, axis = stage_of(p, 1)
        for copy in sums[p]:
            copy.wait()
        total = added(source(place[axis])[...], [landed[k] for k in range(3)])
        landed[1] = total.astype(HALF)

    def start_third(p):
        axis = ORDERS[p % 3][2]
        sums[p] = []
        for k in (2, 1, 3):
            moved = along(place, axis, k)
            sums[p].append(
                remote(
                    third_cut(p % 3, of(r, "landed1_", p).at[1], moved[axis]),
                    of(r, "landed2_", p).at[k - 1],
                    device_at(moved, core),
                )
            )

    def finish(p):
        for copy in sums[p]:
            copy.wait()
        mine = third_cut(p % 3, of(r, "landed1_", p).at[1], place[ORDERS[p % 3][2]])
        total = added(mine[...], [of(r, "landed2_", p)[k] for k in range(3)])
        of(r, "sum", p)[...] = total

    for copy in handed_coarse:
        copy.wait()

    def paired(grad, lead):
        width = grad.shape[1] // 2
        rows = grad.shape[0] // 8
        pieces = [grad[:, :width].reshape(rows, 8, width), grad[:, width:].reshape(rows, 8, width)]
        return jnp.concatenate(pieces, axis=1).astype(HALF).reshape(lead + (16, width))

    def qkv_rows(n, carry):
        cols = pl.ds(pl.multiple_of(n * 256, 256), 256)
        left = r.normed_left[:, cols]
        for low, share, at in ((0, 1, 0), (512, 1, 512), (1024, 2, 0)):
            right = jnp.concatenate(
                [
                    r.qkv_right[:, low : low + 512],
                    r.qkv_right[:, low + 1536 : low + 2048],
                ],
                axis=1,
            )
            of(r, "share", share)[pl.ds(n * 2, 2), :, :, :, :, at : at + 512] = paired(
                dot_tn(left, right), (2, 2, 4, 2)
            )
        grad = dot_tn(r.coarse_left[:, cols], r.cot_right[...])
        r.share2[pl.ds(n * 2, 2), :, :, :, :, 512:] = paired(grad, (2, 2, 4, 2))
        return carry

    lax.fori_loop(0, 2, qkv_rows, 0)
    if summing:
        start_first(1)
        start_first(2)
    for copy in gains_handed + [merged_handed, inner_handed]:
        copy.wait()
    ones = jnp.ones((32, 128), HALF)
    left_lane = lax.broadcasted_iota(jnp.int32, (64, 16, 128), 2) < HD
    by_merge = dot_tn(r.gain_merge_left[...], ones).reshape(64, 16, 128)
    by_coarse = dot_tn(r.gain_coarse_left[...], ones).reshape(64, 8, 128)
    by_coarse = jnp.concatenate([by_coarse, by_coarse], axis=1)
    gains = jnp.where(left_lane, by_merge, by_coarse).astype(HALF)
    r.share0[:, :, :, :, :, 1024:] = gains.reshape(4, 2, 4, 2, 16, 128)

    def merge_rows(n, carry):
        left = r.merged_left[:, pl.ds(pl.multiple_of(n * 256, 256), 256)]
        grad = dot_tn(left, r.inner_right[...])
        r.share0[n, :, :, :, :, :1024] = grad.astype(HALF).reshape(2, 4, 2, 16, 1024)
        return carry

    lax.fori_loop(0, 4, merge_rows, 0)
    if summing:
        start_first(0)

    needs = ((LON, LAT, DIAG), (LAT,), (LON,), ())
    waited = set()
    end_arrive = []
    for w in (3, 2, 1, 0):
        for slot in needs[w]:
            if slot not in waited:
                back_arrive[slot].wait()
                waited.add(slot)
        rows = slice(CELLS * w, CELLS * w + CELLS)
        grad = gathered("back", rows, r.patches_grad[...], fine_sizes, needs[w]).astype(HALF)
        r.fine_right[rows, :] = grad
        handed_fine.append(hand_right("fine_right", CELLS * w, CELLS))
        attended_grad = dot_nt(grad, r.proj_f[...]).astype(HALF)
        qkv = r.qkv
        for p in range(4):
            at = 128 * p
            queries = two_heads(qkv[rows, at : at + 128])
            keys, worth = qkv[rows, 512 + at : 640 + at], qkv[rows, 1024 + at : 1152 + at]
            rounded = r.kept[4 * w + p]
            upstream = two_heads(attended_grad[:, at : at + 128])
            grads = pair_back(rounded.astype(FULL), rounded, queries, keys, worth, upstream)
            for n in range(3):
                r.triple_right[rows, 512 * n + at : 512 * n + at + 128] = grads[n]
        handed_fine.append(hand_right("triple_right", CELLS * w, CELLS))
        if w == 3:
            out_arrive = [send_piece("out", n, coarse_sizes[n], -1) for n in (LAT, DIAG, LON)]
    for copy in handed_fine:
        copy.wait()

    def store(n, p, at, pieces):
        width = pieces[0].shape[1]
        for side, value in enumerate(four_stacked(pieces)):
            of(r, "share", p)[pl.ds(n * 2, 2), :, :, side, :, at : at + width] = value.reshape(
                2, 2, 4, 16, width
            )

    def fine_rows(n, carry):
        cols = pl.ds(pl.multiple_of(n * 128, 128), 128)
        grad = dot_tn(r.normal_left[:, cols], r.triple_right[...])
        store(n, 3, 0, [grad[:, 384 * m : 384 * m + 256] for m in range(4)])
        store(n, 4, 0, [grad[:, 384 * m + 256 : 384 * m + 384] for m in range(4)])
        grad = dot_tn(r.attended_left[:, cols], r.fine_right[...])
        store(n, 4, 128, [grad[:, 128 * m : 128 * m + 128] for m in range(4)])
        return carry

    lax.fori_loop(0, 2, fine_rows, 0)
    if summing:
        for p in (3, 4):
            start_first(p)
    gain_row = jnp.zeros((1, 512), FULL)
    r.tokens_back[...] = jnp.zeros_like(r.tokens_back)
    for w in (3, 2, 1, 0):
        rows = slice(CELLS * w, CELLS * w + CELLS)
        normed_grad = dot_nt(r.triple_right[rows, :], r.qkv_f[...]).astype(HALF).astype(FULL)
        unit, scale = norm_parts(r.rolled[rows, :].astype(FULL))
        gain_row = gain_row + jnp.sum(normed_grad * unit, axis=0, keepdims=True)
        back = norm_back(normed_grad, unit, scale, r.gain_f[...])
        r.tokens_back[rows, :] = (r.fine_right[rows, :].astype(FULL) + back).astype(HALF)
        for slot in {2: (LAT,), 1: (DIAG, LON)}.get(w, ()):
            if not end_arrive:
                loads["end_pack"].wait()
            pack_piece("end", r.tokens_back[...], slot, fine_sizes[slot])
            end_arrive.append(send_piece("end", slot, fine_sizes[slot], -1))
    split(in_two(gain_row), pick4, "gain_fine", slice(0, 16))
    gain_handed = hand_left("gain_fine")
    if summing:
        for p in (1, 2):
            collect_first(p)
            start_second(p)
    gain_handed.wait()
    for n in range(2):
        cols = slice(128 * n, 128 * n + 128)
        store(n, 5, 0, [dot_tn(r.gain_fine_left[:, cols], ones)] * 4)
    if summing:
        start_first(5)
        for p in (0, 3, 4):
            collect_first(p)
            start_second(p)
    for copy in out_arrive:
        copy.wait()
    r.coarse_tokens[...] = gathered(
        "out", every, r.coarse_out[...], coarse_sizes, (LON, LAT, DIAG)
    ).astype(HALF)
    if summing:
        collect_first(5)
        start_second(5)
        for p in (1, 2, 0, 3, 4):
            collect_second(p)
            start_third(p)
    for name in ("end_own", "end_halo"):
        loads[name].wait()
    for copy in end_arrive:
        copy.wait()
    r.tokens_grad[...] = gathered(
        "end", every, r.tokens_back[...], fine_sizes, (LON, LAT, DIAG)
    ).astype(HALF)
    if summing:
        collect_second(5)
        start_third(5)
        for p in (1, 2, 0, 3, 4, 5):
            finish(p)
    else:
        for p in range(6):
            of(r, "sum", p)[...] = of(r, "share", p)[...].reshape(64, 16, WIDTHS[p])


LOADED = tuple(
    dict(
        in_pack=0,
        in_own=0,
        in_halo=0,
        qkv_f=0,
        proj_f=0,
        mid_pack=0,
        proj_c=0,
        mid_own=0,
        mid_halo=0,
        merge_w=0,
        qkv_c=0,
        back_pack=0,
        back_own=0,
        back_halo=0,
        end_pack=0,
        end_own=0,
        end_halo=0,
    )
)


def whole(values, summing):
    inputs, scratch, outputs = [], [], []

    def matrices(kind, rows, cols, source, target, sign):
        pack, own, halo, _ = roll_matrices(rows, cols, source, target, sign)
        return {
            kind + "_pack": jnp.asarray(pack, HALF),
            kind + "_own": jnp.asarray(own, HALF),
            kind + "_halo": jnp.asarray(halo, HALF),
        }

    values = dict(values)
    values.update(matrices("in", 12, 24, "natural", "window", 1))
    values.update(matrices("cot", 6, 12, "natural", "window", 1))
    values.update(matrices("mid", 12, 24, "window", "patch", 1))
    values.update(matrices("back", 12, 24, "patch", "window", -1))
    values.update(matrices("end", 12, 24, "window", "natural", -1))
    values.update(matrices("out", 6, 12, "window", "natural", -1))
    specs, operands = [], []
    for name, value in values.items():
        loaded = name in LOADED
        inputs.append(name + "_any" if loaded else name)
        specs.append(ANYWHERE if loaded else VMEM)
        operands.append(value)
    half = {name: values[name].shape for name in LOADED[:11]}
    for kind, width in (("in", 512), ("cot", 1024), ("mid", 512), ("back", 512), ("end", 512), ("out", 1024)):
        half[kind + "_landed"] = (PACKED, width)
    half.update(in_packed=(PACKED, 512), cot_packed=(PACKED, 1024), mid_packed=(PACKED, 512))
    lefts = dict(
        normal=(576, 256),
        attended=(576, 256),
        merged=(CELLS, 1024),
        normed=(CELLS, 512),
        coarse=(CELLS, 512),
        gain_coarse=(16, 512),
        gain_merge=(16, 1024),
        gain_fine=(16, 256),
    )
    for name, (count, width) in lefts.items():
        half[name + "_left"] = (2 * count, width)
        half[name + "_give"] = (count, width)
    half.update(
        kept=(16, CELLS, 2 * CELLS),
        rolled=(576, 512),
        qkv=(576, 1536),
        attended=(576, 512),
        fine_out=(576, 512),
        tokens_back=(576, 512),
        cot_right=(2 * CELLS, 1024),
        cot_attended=(CELLS, 1024),
        qkv_coarse=(CELLS, 3072),
        coarse_attended=(CELLS, 1024),
        coarse_out=(CELLS, 1024),
        qkv_right=(2 * CELLS, 3072),
        inner_right=(2 * CELLS, 1024),
        fine_right=(1152, 512),
        triple_right=(1152, 1536),
    )
    for p, width in enumerate(WIDTHS):
        half["share" + str(p)] = (4, 2, 4, 2, 16, width)
        if summing:
            first, second = LEADS[p % 3]
            half["landed0_" + str(p)] = (3,) + first + (16, width)
            half["landed1_" + str(p)] = (3,) + second + (16, width)
            half["landed2_" + str(p)] = (3, 16, width)
    memory = {name: pltpu.VMEM(shape, HALF) for name, shape in half.items()}
    memory["unit_merge"] = pltpu.VMEM((CELLS, 2048), FULL)
    memory["unit_coarse"] = pltpu.VMEM((CELLS, 1024), FULL)
    memory["send_sem"] = pltpu.SemaphoreType.DMA((150,))
    memory["recv_sem"] = pltpu.SemaphoreType.DMA((150,))
    memory["load_sem"] = pltpu.SemaphoreType.DMA((len(LOADED),))
    outputs = {
        "coarse_tokens": jax.ShapeDtypeStruct((CELLS, 1024), HALF),
        "tokens_grad": jax.ShapeDtypeStruct((576, 512), HALF),
    }
    for p, width in enumerate(WIDTHS):
        outputs["sum" + str(p)] = (
            jax.ShapeDtypeStruct((16, width), FULL)
            if summing
            else jax.ShapeDtypeStruct((64, 16, width), HALF)
        )
    names = tuple(inputs) + tuple(outputs) + tuple(memory)
    results = pl.pallas_call(
        functools.partial(whole_kernel, names, summing),
        out_shape=list(outputs.values()),
        in_specs=specs,
        out_specs=[VMEM] * len(outputs),
        scratch_shapes=list(memory.values()),
        compiler_params=pltpu.CompilerParams(
            collective_id=1, has_side_effects=True, vmem_limit_bytes=LIMIT
        ),
    )(*operands)
    return dict(zip(outputs, results))


def prepared(
    tokens,
    cotangent,
    gain_fine,
    qkv_fine,
    proj_fine,
    gain_merge,
    merge_weight,
    gain_coarse,
    qkv_coarse,
    proj_coarse,
):
    return dict(
        tokens=tokens.reshape(576, 512),
        cotangent=cotangent,
        gain_f=gain_fine.reshape(1, 512),
        gain_m=gain_merge.reshape(1, 2048),
        gain_c=gain_coarse.reshape(1, 1024),
        qkv_f=qkv_fine,
        proj_f=proj_fine,
        merge_w=merge_weight,
        qkv_c=qkv_coarse,
        proj_c=proj_coarse,
    )


def last_kernel(*refs):
    coarse, tokens, a, b, c, d, e, f = refs[:8]
    coarse_out, tokens_out, fine_gain, qkv_f, proj_f, merge_gain, merge, coarse_gain, qkv_c, proj_c = refs[8:]
    cells = coarse[...].astype(FULL)
    for n in range(12):
        coarse_out[n // 6, n % 6] = cells[WW * n : WW * n + WW].astype(HALF)
    tokens_out[...] = tokens[...]

    def across(column, count):
        row = lax.broadcasted_iota(jnp.int32, (16, 128), 0)
        lane = lax.broadcasted_iota(jnp.int32, (16, 128), 1)
        line = jnp.sum(jnp.where(row == lane, column, 0.0), axis=0, keepdims=True)
        return line[:, :count]

    block = a[:, 1024:]
    merge_gain[...] = across(jnp.broadcast_to(block[:, :1], (16, 128)), 16)
    coarse_gain[...] = across(jnp.broadcast_to(block[:, HD : HD + 1], (16, 128)), 8)
    fine_gain[...] = across(f[...], 4)
    merge[...] = a[:, :1024]
    for n in range(2):
        rows = slice(8 * n, 8 * n + 8)
        qkv_c[:, 1536 * n : 1536 * n + 1024] = b[rows, :]
        qkv_c[:, 1536 * n + 1024 : 1536 * n + 1536] = c[rows, :512]
        proj_c[:, 512 * n : 512 * n + 512] = c[rows, 512:]
    for n in range(4):
        rows = slice(4 * n, 4 * n + 4)
        qkv_f[:, 384 * n : 384 * n + 256] = d[rows, :]
        qkv_f[:, 384 * n + 256 : 384 * n + 384] = e[rows, :128]
        proj_f[:, 128 * n : 128 * n + 128] = e[rows, 128:]


def last(found):
    shapes = [jax.ShapeDtypeStruct((2, 6, WW, 1024), HALF), jax.ShapeDtypeStruct((576, 512), HALF)]
    shapes += [
        jax.ShapeDtypeStruct(shape, FULL)
        for shape in (
            (1, 4),
            (4, 1536),
            (4, 512),
            (1, 16),
            (16, 1024),
            (1, 8),
            (8, 3072),
            (8, 1024),
        )
    ]
    outs = pl.pallas_call(
        last_kernel, out_shape=shapes, in_specs=[VMEM] * 8, out_specs=[VMEM] * 10
    )(*found)
    outs = list(outs)
    outs[1] = outs[1].reshape(2, 12, 24, 512)
    for n in (2, 5, 7):
        outs[n] = outs[n].reshape(-1)
    return tuple(outs)


def local(*args):
    found = whole(prepared(*args), True)
    return last(tuple(found.values()))


def solution(mesh):
    grid = P(None, "lat", "lon", None)
    vector, matrix = P(("lat", "lon")), P(("lat", "lon"), None)
    return jax.shard_map(
        local,
        mesh=mesh,
        in_specs=(grid, grid) + (P(),) * 8,
        out_specs=(grid, grid, vector, matrix, matrix, vector, matrix, vector, matrix, matrix),
        check_vma=False,
    )
```

```python
import functools
from types import SimpleNamespace

import jax
import jax.numpy as jnp
import numpy as np
from jax import lax
from jax.experimental import pallas as pl
from jax.experimental.pallas import tpu as pltpu
from jax.sharding import PartitionSpec as P

MESH = pl.DeviceIdType.MESH
HALF = jnp.bfloat16
FULL = jnp.float32
HD = 64
WH = 6
WW = 12
CELLS = 144
EPSILON = 1e-05
MASKED = -1e30
PIECES = (0, 128, 256)
PACKED = 304
LIMIT = 62 * 1024 * 1024
VMEM = pl.BlockSpec(memory_space=pltpu.VMEM)
SMEM = pl.BlockSpec(memory_space=pltpu.SMEM)
ANYWHERE = pl.BlockSpec(memory_space=pl.ANY)


def dot(left, right):
    return jnp.dot(left, right, preferred_element_type=FULL)


def dot_nt(left, right):
    return lax.dot_general(left, right, (((1,), (1,)), ((), ())), preferred_element_type=FULL)


def dot_tn(left, right):
    return lax.dot_general(left, right, (((0,), (0,)), ((), ())), preferred_element_type=FULL)


def natural_order(rows, cols):
    return lambda level, i, j: (level * rows + i) * cols + j


def level_last_order(rows, cols):
    return lambda level, i, j: (i * cols + j) * 2 + level


def window_order(rows, cols):
    def place(level, i, j):
        window = i // WH * (cols // WW) + j // WW
        return window * CELLS + ((i % WH // 3 * 2 + level) * 3 + i % 3) * WW + j % WW

    return place


def patch_order(rows, cols):
    coarse = window_order(rows // 2, cols // 2)

    def place(level, i, j):
        return (j % 2 * 2 + i % 2) * CELLS + coarse(level, i // 2, j // 2)

    return place


@functools.lru_cache(maxsize=None)
def roll_matrices(rows, cols, source, target, sign):
    orders = {"last": level_last_order, "natural": natural_order, "window": window_order, "patch": patch_order}
    from_place, to_place = orders[source](rows, cols), orders[target](rows, cols)
    count = 2 * rows * cols
    pieces = ([], [], [])
    own = np.zeros((count, count), np.float32)
    for level in range(2):
        for i in range(rows):
            for j in range(cols):
                far_i, far_j = i + 3 * sign, j + 6 * sign
                across = (far_i // rows != 0, far_j // cols != 0)
                here = from_place(level, far_i % rows, far_j % cols)
                there = to_place(level, i, j)
                if across == (False, False):
                    own[there, here] = 1
                else:
                    slot = {(False, True): 0, (True, False): 1, (True, True): 2}[across]
                    pieces[slot].append((there, here))
    sizes = tuple((len(piece) + 15) // 16 * 16 for piece in pieces)
    pack = np.zeros((PACKED, count), np.float32)
    halo = np.zeros((count, PACKED), np.float32)
    for slot, piece in enumerate(pieces):
        for k, (there, here) in enumerate(piece):
            pack[PIECES[slot] + k, here] = 1
            halo[there, PIECES[slot] + k] = 1
    return pack, own, halo, sizes


def norm_parts(values):
    centre = jnp.mean(values, axis=-1, keepdims=True)
    offset = values - centre
    spread = jnp.mean(offset * offset, axis=-1, keepdims=True)
    scale = lax.rsqrt(spread + EPSILON)
    return offset * scale, scale


def norm_back(grad, normal, scale, gain):
    inner = grad * gain
    mean = jnp.mean(inner, axis=-1, keepdims=True)
    along = jnp.mean(inner * normal, axis=-1, keepdims=True)
    return (inner - mean - normal * along) * scale


def two_heads(pair):
    first = lax.broadcasted_iota(jnp.int32, pair.shape, 1) < HD
    zero = jnp.zeros_like(pair)
    return jnp.concatenate([jnp.where(first, pair, zero), jnp.where(first, zero, pair)], axis=0)


def one_pair(stack):
    half = stack.shape[0] // 2
    first = lax.broadcasted_iota(jnp.int32, (half, 2 * HD), 1) < HD
    return jnp.where(first, stack[:half], stack[half:])


def pair_mask(edge):
    shape = (CELLS, 2 * CELLS)
    key = lax.broadcasted_iota(jnp.int32, shape, 0)
    query = lax.broadcasted_iota(jnp.int32, shape, 1)
    query = jnp.where(query >= CELLS, query - CELLS, query)
    apart = (key < CELLS // 2) != (query < CELLS // 2)
    return jnp.where(apart, edge, 0) > 0


def pair_weights(queries, keys, mask):
    scores = [dot_nt(key, query * 0.125) for query, key in zip(queries, keys)]
    scores = [jnp.where(mask, MASKED, score) for score in scores]
    powers = [jnp.exp(score - jnp.max(score, axis=0, keepdims=True)) for score in scores]
    return [power * (1.0 / jnp.sum(power, axis=0, keepdims=True)) for power in powers]


def pair_forward(rounded, values):
    stacks = [dot_tn(weights, value) for weights, value in zip(rounded, values)]
    return [one_pair(stack).astype(HALF) for stack in stacks]


def pair_back(weights, rounded, queries, keys, values, upstream):
    weight_grads = [dot_nt(value, above) for value, above in zip(values, upstream)]
    value_grads = [dot(half, above).astype(HALF) for half, above in zip(rounded, upstream)]
    score_grads = []
    for weight, grad in zip(weights, weight_grads):
        inner = jnp.sum(weight * grad, axis=0, keepdims=True)
        score_grads.append((weight * (grad - inner) * 0.125).astype(HALF))
    key_grads = [dot(grad, query).astype(HALF) for grad, query in zip(score_grads, queries)]
    query_grads = [
        one_pair(dot_tn(grad, key)).astype(HALF) for grad, key in zip(score_grads, keys)
    ]
    return query_grads, key_grads, value_grads


def four_stacked(pieces):
    rows, width = pieces[0].shape
    shaped = [piece.reshape(rows // 8, 8, width) for piece in pieces]
    upper = lax.broadcasted_iota(jnp.int32, shaped[0].shape, 1) < 4
    turned = [pltpu.roll(piece, 4, 1) for piece in shaped]
    even = [jnp.where(upper, shaped[n], turned[n + 1]) for n in (0, 2)]
    odd = [jnp.where(upper, turned[n], shaped[n + 1]) for n in (0, 2)]
    return [jnp.concatenate(pair, axis=1).astype(HALF) for pair in (even, odd)]


ORDERS = (("x", "y", "z"), ("y", "z", "x"), ("z", "x", "y"))
LEADS = (((4, 2, 2), (2, 2)), ((2, 4, 2), (4,)), ((4, 4), (4,)))
WIDTHS = (1152, 1024, 1024, 256, 256, 128)
LON, LAT, DIAG = 0, 1, 2
STEPS = ((0, 1), (1, 0), (1, 1))


def device_at(place, core):
    lat = place["y"] * 2 + place["z"] // 2
    lon = place["x"] * 4 + place["z"] % 2 * 2 + core
    return (lat, lon)


def along(place, axis, steps):
    moved = dict(place)
    moved[axis] = lax.rem(place[axis] + steps, 4)
    return moved


def first_cut(kind, ref, index):
    if kind == 0:
        return ref.at[:, :, index]
    if kind == 1:
        return ref.at[index]
    return ref.at[:, index // 2, :, index % 2]


def second_cut(kind, ref, index):
    if kind == 0:
        return ref.at[index]
    if kind == 1:
        return ref.at[index // 2, :, index % 2]
    return ref.at[:, index]


def third_cut(kind, ref, index):
    if kind == 0:
        return ref.at[index // 2, index % 2]
    return ref.at[index]


def spots(lead, i):
    found = []
    for size in reversed(lead):
        found.insert(0, i % size)
        i = i // size
    return tuple(found)


def added(base, arrivals):
    total = base.astype(FULL)
    for arrival in arrivals:
        total = total + arrival.astype(FULL)
    return total


def of(r, name, p):
    return getattr(r, name + str(p))


def owner_pick(rows_each, core):
    shift = rows_each.bit_length() - 1
    feature = lax.broadcasted_iota(jnp.int32, (256, 128), 0)
    place = lax.broadcasted_iota(jnp.int32, (256, 128), 1)
    wanted = ((place >> shift) << (shift + 1)) + (place & (rows_each - 1)) + core * rows_each
    return jnp.where(feature == wanted, 1.0, 0.0).astype(HALF)


def in_two(row):
    high = row.astype(HALF)
    low = (row - high.astype(FULL)).astype(HALF)
    place = lax.broadcasted_iota(jnp.int32, (16, row.shape[1]), 0)
    wide_high = jnp.broadcast_to(high.astype(FULL), place.shape)
    wide_low = jnp.broadcast_to(low.astype(FULL), place.shape)
    return jnp.where(place == 0, wide_high, jnp.where(place == 1, wide_low, 0.0)).astype(HALF)


def whole_kernel(names, summing, *refs):
    r = SimpleNamespace(**dict(zip(names, refs)))
    lat, lon = lax.axis_index("lat"), lax.axis_index("lon")
    lats, lons = lax.axis_size("lat"), lax.axis_size("lon")
    core = lon % 2
    place = {"y": lat // 2, "x": lon // 4, "z": lat % 2 * 2 + lon // 2 % 2}
    sibling = (lat, lon + 1 - 2 * core)
    edge = jnp.where(lat == lats - 1, 1, 0)
    used = [0]

    def remote(source, target, device):
        slot = used[0]
        used[0] += 1
        copy = pltpu.make_async_remote_copy(
            src_ref=source,
            dst_ref=target,
            send_sem=r.send_sem.at[slot],
            recv_sem=r.recv_sem.at[slot],
            device_id=device,
            device_id_type=MESH,
        )
        copy.start()
        return copy

    def neighbour(step, way):
        return (
            lax.rem(lat + lats + way * step[0], lats),
            lax.rem(lon + lons + way * step[1], lons),
        )

    loads = {}

    def load(name):
        slot = LOADED.index(name)
        loads[name] = pltpu.make_async_copy(getattr(r, name + "_any"), getattr(r, name), r.load_sem.at[slot])
        loads[name].start()

    for kind, held in (("back", "in"), ("end", "mid")):
        for matrix in ("_pack", "_own", "_halo"):
            setattr(r, kind + matrix, getattr(r, held + matrix))
    r.patches_grad = r.fine_out
    r.normal, r.cot_flat, r.wide = r.tokens_back, r.coarse_attended, r.unit_coarse
    r.back_packed, r.end_packed, r.out_packed = r.in_packed, r.mid_packed, r.cot_packed
    for name in LOADED[:6]:
        load(name)

    for landed, size in (
        (r.in_landed, 112),
        (r.mid_landed, 112),
        (r.back_landed, 112),
        (r.end_landed, 112),
        (r.cot_landed, 48),
        (r.out_landed, 48),
    ):
        for start in PIECES[:2]:
            landed[start + size : start + 128, :] = jnp.zeros((128 - size, landed.shape[1]), HALF)

    barrier = pltpu.get_barrier_semaphore()
    partners = [neighbour(step, way) for step in STEPS for way in (1, -1)] + [sibling]
    if summing:
        partners += [
            device_at(along(place, axis, k), core) for axis in ("x", "y", "z") for k in (1, 2, 3)
        ]
    for partner in partners:
        pl.semaphore_signal(barrier, inc=1, device_id=partner, device_id_type=MESH)

    def pack_piece(kind, value, slot, size):
        rows = slice(PIECES[slot], PIECES[slot] + size)
        getattr(r, kind + "_packed")[rows, :] = dot(getattr(r, kind + "_pack")[rows, :], value).astype(HALF)

    def send_piece(kind, slot, size, sign):
        rows = pl.ds(PIECES[slot], size)
        return remote(
            getattr(r, kind + "_packed").at[rows],
            getattr(r, kind + "_landed").at[rows],
            neighbour(STEPS[slot], -sign),
        )

    def gathered(kind, rows, value, sizes, needed):
        total = dot(getattr(r, kind + "_own")[rows, :], value)
        if len(needed) == 3:
            return total + dot(getattr(r, kind + "_halo")[rows, :], getattr(r, kind + "_landed")[...])
        for slot in needed:
            piece = slice(PIECES[slot], PIECES[slot] + sizes[slot])
            total = total + dot(getattr(r, kind + "_halo")[rows, piece], getattr(r, kind + "_landed")[piece, :])
        return total

    fine_sizes, coarse_sizes = (112, 112, 48), (48, 48, 48)
    loads["in_pack"].wait()
    for slot in (LAT, DIAG, LON):
        pack_piece("in", r.tokens[...], slot, fine_sizes[slot])
    pl.semaphore_wait(barrier, len(partners))
    arrive = {slot: send_piece("in", slot, fine_sizes[slot], 1) for slot in (LAT, DIAG, LON)}
    for n in range(12):
        r.wide[WW * n : WW * n + WW, :] = r.cotangent[n // 6, n % 6].astype(FULL)
    cotangent = r.wide[...].astype(HALF)
    r.cot_flat[...] = cotangent
    for slot in (LAT, DIAG, LON):
        pack_piece("cot", cotangent, slot, coarse_sizes[slot])
    r.fine_out[...] = jnp.zeros_like(r.fine_out)

    pick4, pick8, pick16 = (
        jnp.concatenate([owner_pick(n, core), owner_pick(n, 1 - core)], axis=1) for n in (4, 8, 16)
    )

    def split(value, pick, name, rows):
        for block in range(value.shape[1] // 256):
            parts = dot(value[:, 256 * block : 256 * block + 256], pick).astype(HALF)
            cols = slice(128 * block, 128 * block + 128)
            getattr(r, name + "_left")[rows, cols] = parts[:, :128]
            getattr(r, name + "_give")[rows, cols] = parts[:, 128:]

    def hand_left(name):
        count = getattr(r, name + "_give").shape[0]
        return remote(getattr(r, name + "_give"), getattr(r, name + "_left").at[pl.ds(count, count)], sibling)

    def hand_right(name, start, size):
        half = getattr(r, name).shape[0] // 2
        held = getattr(r, name)
        return remote(held.at[pl.ds(start, size)], held.at[pl.ds(half + start, size)], sibling)

    handed_fine, handed_coarse, late = [], [], []

    needs = ((), (LON,), (LAT,), (LON, LAT, DIAG))
    waited = set()
    mid_arrive = []
    for name in LOADED[1:6]:
        loads[name].wait()
    for name in LOADED[6:11]:
        load(name)
    for w in range(4):
        for slot in needs[w]:
            if slot not in waited:
                arrive[slot].wait()
                waited.add(slot)
        rows = slice(CELLS * w, CELLS * w + CELLS)
        values = gathered("in", rows, r.tokens[...], fine_sizes, needs[w])
        r.rolled[rows, :] = values.astype(HALF)
        unit, _ = norm_parts(values)
        normed = (unit * r.gain_f[...]).astype(HALF)
        r.normal[rows, :] = normed
        qkv = r.qkv
        for n in range(3):
            cols = slice(512 * n, 512 * n + 512)
            qkv[rows, cols] = dot(normed, r.qkv_f[:, cols]).astype(HALF)
        mask = pair_mask(edge if w >= 2 else 0)
        lanes = [slice(128 * p, 128 * p + 128) for p in range(4)]

        def parts(base):
            return [qkv[rows, base + 128 * p : base + 128 * p + 128] for p in range(4)]

        weights = pair_weights([two_heads(part) for part in parts(0)], parts(512), mask)
        rounded = [weight.astype(HALF) for weight in weights]
        for p, mixed in enumerate(pair_forward(rounded, parts(1024))):
            r.attended[rows, lanes[p]] = mixed
        for p in range(4):
            r.kept[4 * w + p] = rounded[p]
        attended = r.attended[rows, :]
        r.fine_out[rows, :] = (values + dot(attended, r.proj_f[...])).astype(HALF)
        for slot in {1: (LAT,), 2: (DIAG, LON)}.get(w, ()):
            pack_piece("mid", r.fine_out[...], slot, fine_sizes[slot])
            mid_arrive.append(send_piece("mid", slot, fine_sizes[slot], 1))
        if w == 2:
            cot_arrive = [send_piece("cot", n, coarse_sizes[n], 1) for n in (LAT, DIAG, LON)]
    rows = slice(0, 576)
    split(r.normal[...], pick4, "normal", rows)
    split(r.attended[...], pick4, "attended", rows)
    handed_fine += [hand_left("normal"), hand_left("attended")]
    for name in LOADED[11:14]:
        load(name)

    every, own = slice(None), slice(0, CELLS)
    loads["mid_own"].wait()
    loads["mid_halo"].wait()
    for copy in mid_arrive:
        copy.wait()
    values = jnp.concatenate(
        [
            gathered(
                "mid",
                slice(CELLS * g, CELLS * g + CELLS),
                r.fine_out[...],
                fine_sizes,
                (LON, LAT, DIAG),
            )
            for g in range(4)
        ],
        axis=1,
    )
    for name in LOADED[14:]:
        load(name)
    unit, scale_merge = norm_parts(values)
    r.unit_merge[...] = unit
    merged = (unit * r.gain_m[...]).astype(HALF)
    loads["merge_w"].wait()
    coarse_in = dot(merged, r.merge_w[...]).astype(HALF).astype(FULL)
    split(merged, pick16, "merged", own)
    merged_handed = hand_left("merged")
    unit, scale_coarse = norm_parts(coarse_in)
    r.unit_coarse[...] = unit
    normed = (unit * r.gain_c[...]).astype(HALF)
    loads["qkv_c"].wait()
    for n in range(3):
        cols = slice(1024 * n, 1024 * (n + 1))
        r.qkv_coarse[:, cols] = dot(normed, r.qkv_c[:, cols]).astype(HALF)
    split(normed, pick8, "normed", own)
    handed_coarse.append(hand_left("normed"))
    for copy in cot_arrive:
        copy.wait()
    cot = gathered("cot", every, r.cot_flat[...], coarse_sizes, (LON, LAT, DIAG)).astype(HALF)
    r.cot_right[own, :] = cot
    handed_coarse.append(hand_right("cot_right", 0, CELLS))
    loads["proj_c"].wait()
    r.cot_attended[...] = dot_nt(cot, r.proj_c[...]).astype(HALF)
    qkv = r.qkv_coarse
    mask = pair_mask(edge)
    for group in range(2):
        starts = [512 * group + 128 * p for p in range(4)]

        def parts(base, held=qkv, starts=starts):
            return [held[:, base + at : base + at + 128] for at in starts]

        queries = [two_heads(part) for part in parts(0)]
        keys, worth = parts(1024), parts(2048)
        weights = pair_weights(queries, keys, mask)
        rounded = [weight.astype(HALF) for weight in weights]
        for at, mixed in zip(starts, pair_forward(rounded, worth)):
            r.coarse_attended[:, at : at + 128] = mixed
        upstream = [two_heads(part) for part in parts(0, r.cot_attended)]
        grads = pair_back(weights, rounded, queries, keys, worth, upstream)
        for n in range(3):
            for at, grad in zip(starts, grads[n]):
                r.qkv_right[own, 1024 * n + at : 1024 * n + at + 128] = grad
    handed_coarse.append(hand_right("qkv_right", 0, CELLS))
    attended = r.coarse_attended[...]
    split(attended, pick8, "coarse", own)
    handed_coarse.append(hand_left("coarse"))
    normed_grad = dot_nt(r.qkv_right[own, :], r.qkv_c[...]).astype(HALF).astype(FULL)
    gain_row = jnp.sum(normed_grad * r.unit_coarse[...], axis=0, keepdims=True)
    split(in_two(gain_row), pick8, "gain_coarse", slice(0, 16))
    gains_handed = [hand_left("gain_coarse")]
    coarse_grad = r.cot_right[own, :].astype(FULL) + norm_back(
        normed_grad, r.unit_coarse[...], scale_coarse, r.gain_c[...]
    )
    r.inner_right[own, :] = coarse_grad.astype(HALF)
    inner_handed = hand_right("inner_right", 0, CELLS)
    merged_grad = dot_nt(r.inner_right[own, :], r.merge_w[...]).astype(HALF).astype(FULL)
    gain_row = jnp.sum(merged_grad * r.unit_merge[...], axis=0, keepdims=True)
    split(in_two(gain_row), pick16, "gain_merge", slice(0, 16))
    gains_handed.append(hand_left("gain_merge"))
    back = norm_back(merged_grad, r.unit_merge[...], scale_merge, r.gain_m[...]).astype(HALF)
    for g in range(4):
        r.patches_grad[CELLS * g : CELLS * (g + 1), :] = back[:, 512 * g : 512 * (g + 1)]
    for name in ("back_pack", "back_own", "back_halo"):
        loads[name].wait()
    back_arrive = {}
    for slot in (LAT, DIAG, LON):
        pack_piece("back", r.patches_grad[...], slot, fine_sizes[slot])
        back_arrive[slot] = send_piece("back", slot, fine_sizes[slot], -1)
    r.coarse_out[...] = (coarse_in + dot(attended, r.proj_c[...])).astype(HALF)
    for slot in (LAT, DIAG, LON):
        pack_piece("out", r.coarse_out[...], slot, coarse_sizes[slot])

    sums = {}

    def across(axis):
        mine = place[axis]
        near, far = mine + 1 - 2 * (mine % 2), 3 - mine
        return mine, ((near, far), (far, near))

    def there(axis, index):
        return device_at({**place, axis: index}, core)

    def stage_of(p, stage):
        landed = of(r, ("landed0_", "landed1_")[stage], p)
        lead = LEADS[p % 3][stage]
        size = int(np.prod(lead))
        if stage == 0:
            source = lambda index: first_cut(p % 3, of(r, "share", p), index)
        else:
            source = lambda index: second_cut(p % 3, of(r, "landed0_", p).at[1], index)
        return source, landed, lead, size, ORDERS[p % 3][stage]

    def halves(lead):
        return [pl.ds(h * (lead[0] // 2), lead[0] // 2) for h in range(2)]

    def begin(p, stage):
        source, landed, lead, size, axis = stage_of(p, stage)
        mine, pairs = across(axis)
        sums[p] = {}
        for slot in range(2):
            for h, rows in enumerate(halves(lead)):
                one = pairs[h][0]
                quarter = lax.rem(mine + 2, 4) if slot == 0 else one
                sums[p][h, slot] = remote(
                    source(quarter).at[rows], landed.at[slot, rows], there(axis, one)
                )

    def forward(p, stage):
        source, landed, lead, size, axis = stage_of(p, stage)
        mine, pairs = across(axis)
        for h, rows in enumerate(halves(lead)):
            two = pairs[h][1]
            theirs = source(two)
            sums[p][h, 0].wait()

            def add(i, carry, h=h, theirs=theirs):
                at = spots(lead, i + h * (size // 2))
                landed[(0,) + at] = added(theirs[at], [landed[(0,) + at]]).astype(HALF)
                return carry

            for i in range(size // 2):
                add(i, 0)
            sums[p][h, 2] = remote(landed.at[0, rows], landed.at[2, rows], there(axis, two))

    def collect(p, stage):
        source, landed, lead, size, axis = stage_of(p, stage)
        mine = source(place[axis])
        for h in range(2):
            sums[p][h, 1].wait()
            sums[p][h, 2].wait()

        def add(i, carry):
            at = spots(lead, i)
            total = added(mine[at], [landed[(1,) + at], landed[(2,) + at]])
            landed[(1,) + at] = total.astype(HALF)
            return carry

        for i in range(size):
            add(i, 0)

    def start_first(p):
        axis = ORDERS[p % 3][0]
        sums[p] = []
        for k in (2, 1, 3):
            moved = along(place, axis, k)
            sums[p].append(
                remote(
                    first_cut(p % 3, of(r, "share", p), moved[axis]),
                    of(r, "landed0_", p).at[k - 1],
                    device_at(moved, core),
                )
            )

    def collect_first(p):
        source, landed, lead, size, axis = stage_of(p, 0)
        mine = source(place[axis])
        for copy in sums[p]:
            copy.wait()

        def add(i, carry):
            at = spots(lead, i)
            total = added(mine[at], [landed[(k,) + at] for k in range(3)])
            landed[(1,) + at] = total.astype(HALF)
            return carry

        for i in range(size):
            add(i, 0)

    def start_second(p):
        source, landed, lead, size, axis = stage_of(p, 1)
        sums[p] = []
        for k in (2, 1, 3):
            moved = along(place, axis, k)
            sums[p].append(
                remote(source(moved[axis]), landed.at[k - 1], device_at(moved, core))
            )

    def collect_second(p):
        source, landed, lead, size, axis = stage_of(p, 1)
        for copy in sums[p]:
            copy.wait()
        total = added(source(place[axis])[...], [landed[k] for k in range(3)])
        landed[1] = total.astype(HALF)

    def start_third(p):
        axis = ORDERS[p % 3][2]
        sums[p] = []
        for k in (2, 1, 3):
            moved = along(place, axis, k)
            sums[p].append(
                remote(
                    third_cut(p % 3, of(r, "landed1_", p).at[1], moved[axis]),
                    of(r, "landed2_", p).at[k - 1],
                    device_at(moved, core),
                )
            )

    def finish(p):
        for copy in sums[p]:
            copy.wait()
        mine = third_cut(p % 3, of(r, "landed1_", p).at[1], place[ORDERS[p % 3][2]])
        total = added(mine[...], [of(r, "landed2_", p)[k] for k in range(3)])
        of(r, "sum", p)[...] = total

    for copy in handed_coarse:
        copy.wait()

    def paired(grad, lead):
        width = grad.shape[1] // 2
        rows = grad.shape[0] // 8
        pieces = [grad[:, :width].reshape(rows, 8, width), grad[:, width:].reshape(rows, 8, width)]
        return jnp.concatenate(pieces, axis=1).astype(HALF).reshape(lead + (16, width))

    def qkv_rows(n, carry):
        cols = pl.ds(pl.multiple_of(n * 256, 256), 256)
        left = r.normed_left[:, cols]
        for low, share, at in ((0, 1, 0), (512, 1, 512), (1024, 2, 0)):
            right = jnp.concatenate(
                [
                    r.qkv_right[:, low : low + 512],
                    r.qkv_right[:, low + 1536 : low + 2048],
                ],
                axis=1,
            )
            of(r, "share", share)[pl.ds(n * 2, 2), :, :, :, :, at : at + 512] = paired(
                dot_tn(left, right), (2, 2, 4, 2)
            )
        grad = dot_tn(r.coarse_left[:, cols], r.cot_right[...])
        r.share2[pl.ds(n * 2, 2), :, :, :, :, 512:] = paired(grad, (2, 2, 4, 2))
        return carry

    lax.fori_loop(0, 2, qkv_rows, 0)
    if summing:
        begin(1, 0)
        begin(2, 0)
    for copy in gains_handed + [merged_handed, inner_handed]:
        copy.wait()
    ones = jnp.ones((32, 128), HALF)
    left_lane = lax.broadcasted_iota(jnp.int32, (64, 16, 128), 2) < HD
    by_merge = dot_tn(r.gain_merge_left[...], ones).reshape(64, 16, 128)
    by_coarse = dot_tn(r.gain_coarse_left[...], ones).reshape(64, 8, 128)
    by_coarse = jnp.concatenate([by_coarse, by_coarse], axis=1)
    gains = jnp.where(left_lane, by_merge, by_coarse).astype(HALF)
    r.share0[:, :, :, :, :, 1024:] = gains.reshape(4, 2, 4, 2, 16, 128)

    def merge_rows(n, carry):
        left = r.merged_left[:, pl.ds(pl.multiple_of(n * 256, 256), 256)]
        grad = dot_tn(left, r.inner_right[...])
        r.share0[n, :, :, :, :, :1024] = grad.astype(HALF).reshape(2, 4, 2, 16, 1024)
        return carry

    lax.fori_loop(0, 4, merge_rows, 0)
    if summing:
        begin(0, 0)

    needs = ((LON, LAT, DIAG), (LAT,), (LON,), ())
    waited = set()
    end_arrive = []
    for w in (3, 2, 1, 0):
        for slot in needs[w]:
            if slot not in waited:
                back_arrive[slot].wait()
                waited.add(slot)
        rows = slice(CELLS * w, CELLS * w + CELLS)
        grad = gathered("back", rows, r.patches_grad[...], fine_sizes, needs[w]).astype(HALF)
        r.fine_right[rows, :] = grad
        handed_fine.append(hand_right("fine_right", CELLS * w, CELLS))
        attended_grad = dot_nt(grad, r.proj_f[...]).astype(HALF)
        qkv = r.qkv

        def parts(base):
            return [qkv[rows, base + 128 * p : base + 128 * p + 128] for p in range(4)]

        rounded = [r.kept[4 * w + p] for p in range(4)]
        upstream = [two_heads(attended_grad[:, 128 * p : 128 * p + 128]) for p in range(4)]
        grads = pair_back(
            [half.astype(FULL) for half in rounded],
            rounded,
            [two_heads(part) for part in parts(0)],
            parts(512),
            parts(1024),
            upstream,
        )
        for n in range(3):
            for p in range(4):
                at = 512 * n + 128 * p
                r.triple_right[rows, at : at + 128] = grads[n][p]
        handed_fine.append(hand_right("triple_right", CELLS * w, CELLS))
        if w == 3:
            out_arrive = [send_piece("out", n, coarse_sizes[n], -1) for n in (LAT, DIAG, LON)]
        if summing:
            for p in {2: (1, 2), 0: (0,)}.get(w, ()):
                forward(p, 0)
    for copy in handed_fine:
        copy.wait()

    def store(n, p, at, pieces):
        width = pieces[0].shape[1]
        for side, value in enumerate(four_stacked(pieces)):
            of(r, "share", p)[pl.ds(n * 2, 2), :, :, side, :, at : at + width] = value.reshape(
                2, 2, 4, 16, width
            )

    def fine_rows(n, carry):
        cols = pl.ds(pl.multiple_of(n * 128, 128), 128)
        grad = dot_tn(r.normal_left[:, cols], r.triple_right[...])
        store(n, 3, 0, [grad[:, 384 * m : 384 * m + 256] for m in range(4)])
        store(n, 4, 0, [grad[:, 384 * m + 256 : 384 * m + 384] for m in range(4)])
        grad = dot_tn(r.attended_left[:, cols], r.fine_right[...])
        store(n, 4, 128, [grad[:, 128 * m : 128 * m + 128] for m in range(4)])
        return carry

    lax.fori_loop(0, 2, fine_rows, 0)
    if summing:
        for p in (3, 4):
            start_first(p)
        for p in (1, 2):
            collect(p, 0)
            begin(p, 1)
    gain_row = jnp.zeros((1, 512), FULL)
    r.tokens_back[...] = jnp.zeros_like(r.tokens_back)
    for w in (3, 2, 1, 0):
        rows = slice(CELLS * w, CELLS * w + CELLS)
        normed_grad = dot_nt(r.triple_right[rows, :], r.qkv_f[...]).astype(HALF).astype(FULL)
        unit, scale = norm_parts(r.rolled[rows, :].astype(FULL))
        gain_row = gain_row + jnp.sum(normed_grad * unit, axis=0, keepdims=True)
        back = norm_back(normed_grad, unit, scale, r.gain_f[...])
        r.tokens_back[rows, :] = (r.fine_right[rows, :].astype(FULL) + back).astype(HALF)
        for slot in {2: (LAT,), 1: (DIAG, LON)}.get(w, ()):
            if not end_arrive:
                loads["end_pack"].wait()
            pack_piece("end", r.tokens_back[...], slot, fine_sizes[slot])
            end_arrive.append(send_piece("end", slot, fine_sizes[slot], -1))
        if summing and w == 2:
            collect(0, 0)
            begin(0, 1)
            forward(1, 1)
            forward(2, 1)
    split(in_two(gain_row), pick4, "gain_fine", slice(0, 16))
    gain_handed = hand_left("gain_fine")
    if summing:
        for p in (3, 4):
            collect_first(p)
            start_second(p)
        forward(0, 1)
    gain_handed.wait()
    for n in range(2):
        cols = slice(128 * n, 128 * n + 128)
        store(n, 5, 0, [dot_tn(r.gain_fine_left[:, cols], ones)] * 4)
    if summing:
        start_first(5)
    for copy in out_arrive:
        copy.wait()
    r.coarse_tokens[...] = gathered(
        "out", every, r.coarse_out[...], coarse_sizes, (LON, LAT, DIAG)
    ).astype(HALF)
    if summing:
        for p in (1, 2):
            collect(p, 1)
            start_third(p)
        collect_first(5)
        start_second(5)
        for p in (3, 4):
            collect_second(p)
            start_third(p)
        collect(0, 1)
        start_third(0)
    for name in ("end_own", "end_halo"):
        loads[name].wait()
    for copy in end_arrive:
        copy.wait()
    r.tokens_grad[...] = gathered(
        "end", every, r.tokens_back[...], fine_sizes, (LON, LAT, DIAG)
    ).astype(HALF)
    if summing:
        collect_second(5)
        start_third(5)
        for p in (1, 2, 0, 3, 4, 5):
            finish(p)
    else:
        for p in range(6):
            of(r, "sum", p)[...] = of(r, "share", p)[...].reshape(64, 16, WIDTHS[p])


LOADED = tuple(
    dict(
        in_pack=0,
        in_own=0,
        in_halo=0,
        qkv_f=0,
        proj_f=0,
        mid_pack=0,
        proj_c=0,
        mid_own=0,
        mid_halo=0,
        merge_w=0,
        qkv_c=0,
        back_pack=0,
        back_own=0,
        back_halo=0,
        end_pack=0,
        end_own=0,
        end_halo=0,
    )
)


def whole(values, summing):
    inputs, scratch, outputs = [], [], []

    def matrices(kind, rows, cols, source, target, sign):
        pack, own, halo, _ = roll_matrices(rows, cols, source, target, sign)
        return {
            kind + "_pack": jnp.asarray(pack, HALF),
            kind + "_own": jnp.asarray(own, HALF),
            kind + "_halo": jnp.asarray(halo, HALF),
        }

    values = dict(values)
    values.update(matrices("in", 12, 24, "natural", "window", 1))
    values.update(matrices("cot", 6, 12, "natural", "window", 1))
    values.update(matrices("mid", 12, 24, "window", "patch", 1))
    values.update(matrices("back", 12, 24, "patch", "window", -1))
    values.update(matrices("end", 12, 24, "window", "natural", -1))
    values.update(matrices("out", 6, 12, "window", "natural", -1))
    specs, operands = [], []
    for name, value in values.items():
        loaded = name in LOADED
        inputs.append(name + "_any" if loaded else name)
        specs.append(ANYWHERE if loaded else VMEM)
        operands.append(value)
    half = {name: values[name].shape for name in LOADED[:11]}
    for kind, width in (("in", 512), ("cot", 1024), ("mid", 512), ("back", 512), ("end", 512), ("out", 1024)):
        half[kind + "_landed"] = (PACKED, width)
    half.update(in_packed=(PACKED, 512), cot_packed=(PACKED, 1024), mid_packed=(PACKED, 512))
    lefts = dict(
        normal=(576, 256),
        attended=(576, 256),
        merged=(CELLS, 1024),
        normed=(CELLS, 512),
        coarse=(CELLS, 512),
        gain_coarse=(16, 512),
        gain_merge=(16, 1024),
        gain_fine=(16, 256),
    )
    for name, (count, width) in lefts.items():
        half[name + "_left"] = (2 * count, width)
        half[name + "_give"] = (count, width)
    half.update(
        kept=(16, CELLS, 2 * CELLS),
        rolled=(576, 512),
        qkv=(576, 1536),
        attended=(576, 512),
        fine_out=(576, 512),
        tokens_back=(576, 512),
        cot_right=(2 * CELLS, 1024),
        cot_attended=(CELLS, 1024),
        qkv_coarse=(CELLS, 3072),
        coarse_attended=(CELLS, 1024),
        coarse_out=(CELLS, 1024),
        qkv_right=(2 * CELLS, 3072),
        inner_right=(2 * CELLS, 1024),
        fine_right=(1152, 512),
        triple_right=(1152, 1536),
    )
    for p, width in enumerate(WIDTHS):
        half["share" + str(p)] = (4, 2, 4, 2, 16, width)
        if summing:
            first, second = LEADS[p % 3]
            half["landed0_" + str(p)] = (3,) + first + (16, width)
            half["landed1_" + str(p)] = (3,) + second + (16, width)
            half["landed2_" + str(p)] = (3, 16, width)
    memory = {name: pltpu.VMEM(shape, HALF) for name, shape in half.items()}
    memory["unit_merge"] = pltpu.VMEM((CELLS, 2048), FULL)
    memory["unit_coarse"] = pltpu.VMEM((CELLS, 1024), FULL)
    memory["send_sem"] = pltpu.SemaphoreType.DMA((150,))
    memory["recv_sem"] = pltpu.SemaphoreType.DMA((150,))
    memory["load_sem"] = pltpu.SemaphoreType.DMA((len(LOADED),))
    outputs = {
        "coarse_tokens": jax.ShapeDtypeStruct((CELLS, 1024), HALF),
        "tokens_grad": jax.ShapeDtypeStruct((576, 512), HALF),
    }
    for p, width in enumerate(WIDTHS):
        outputs["sum" + str(p)] = (
            jax.ShapeDtypeStruct((16, width), FULL)
            if summing
            else jax.ShapeDtypeStruct((64, 16, width), HALF)
        )
    names = tuple(inputs) + tuple(outputs) + tuple(memory)
    results = pl.pallas_call(
        functools.partial(whole_kernel, names, summing),
        out_shape=list(outputs.values()),
        in_specs=specs,
        out_specs=[VMEM] * len(outputs),
        scratch_shapes=list(memory.values()),
        compiler_params=pltpu.CompilerParams(
            collective_id=1, has_side_effects=True, vmem_limit_bytes=LIMIT
        ),
    )(*operands)
    return dict(zip(outputs, results))


def prepared(
    tokens,
    cotangent,
    gain_fine,
    qkv_fine,
    proj_fine,
    gain_merge,
    merge_weight,
    gain_coarse,
    qkv_coarse,
    proj_coarse,
):
    return dict(
        tokens=tokens.reshape(576, 512),
        cotangent=cotangent,
        gain_f=gain_fine.reshape(1, 512),
        gain_m=gain_merge.reshape(1, 2048),
        gain_c=gain_coarse.reshape(1, 1024),
        qkv_f=qkv_fine,
        proj_f=proj_fine,
        merge_w=merge_weight,
        qkv_c=qkv_coarse,
        proj_c=proj_coarse,
    )


def last_kernel(*refs):
    coarse, tokens, a, b, c, d, e, f = refs[:8]
    coarse_out, tokens_out, fine_gain, qkv_f, proj_f, merge_gain, merge, coarse_gain, qkv_c, proj_c = refs[8:]
    cells = coarse[...].astype(FULL)
    for n in range(12):
        coarse_out[n // 6, n % 6] = cells[WW * n : WW * n + WW].astype(HALF)
    tokens_out[...] = tokens[...]

    def across(column, count):
        row = lax.broadcasted_iota(jnp.int32, (16, 128), 0)
        lane = lax.broadcasted_iota(jnp.int32, (16, 128), 1)
        line = jnp.sum(jnp.where(row == lane, column, 0.0), axis=0, keepdims=True)
        return line[:, :count]

    block = a[:, 1024:]
    merge_gain[...] = across(jnp.broadcast_to(block[:, :1], (16, 128)), 16)
    coarse_gain[...] = across(jnp.broadcast_to(block[:, HD : HD + 1], (16, 128)), 8)
    fine_gain[...] = across(f[...], 4)
    merge[...] = a[:, :1024]
    for n in range(2):
        rows = slice(8 * n, 8 * n + 8)
        qkv_c[:, 1536 * n : 1536 * n + 1024] = b[rows, :]
        qkv_c[:, 1536 * n + 1024 : 1536 * n + 1536] = c[rows, :512]
        proj_c[:, 512 * n : 512 * n + 512] = c[rows, 512:]
    for n in range(4):
        rows = slice(4 * n, 4 * n + 4)
        qkv_f[:, 384 * n : 384 * n + 256] = d[rows, :]
        qkv_f[:, 384 * n + 256 : 384 * n + 384] = e[rows, :128]
        proj_f[:, 128 * n : 128 * n + 128] = e[rows, 128:]


def last(found):
    shapes = [jax.ShapeDtypeStruct((2, 6, WW, 1024), HALF), jax.ShapeDtypeStruct((576, 512), HALF)]
    shapes += [
        jax.ShapeDtypeStruct(shape, FULL)
        for shape in (
            (1, 4),
            (4, 1536),
            (4, 512),
            (1, 16),
            (16, 1024),
            (1, 8),
            (8, 3072),
            (8, 1024),
        )
    ]
    outs = pl.pallas_call(
        last_kernel, out_shape=shapes, in_specs=[VMEM] * 8, out_specs=[VMEM] * 10
    )(*found)
    outs = list(outs)
    outs[1] = outs[1].reshape(2, 12, 24, 512)
    for n in (2, 5, 7):
        outs[n] = outs[n].reshape(-1)
    return tuple(outs)


def local(*args):
    found = whole(prepared(*args), True)
    return last(tuple(found.values()))


def solution(mesh):
    grid = P(None, "lat", "lon", None)
    vector, matrix = P(("lat", "lon")), P(("lat", "lon"), None)
    return jax.shard_map(
        local,
        mesh=mesh,
        in_specs=(grid, grid) + (P(),) * 8,
        out_specs=(grid, grid, vector, matrix, matrix, vector, matrix, vector, matrix, matrix),
        check_vma=False,
    )
```
